32 devices in a mesh: dp: 4 (over y, x), seq: 8 (over z, core).
Axes of the slice: x: 2, y: 2, z: 4, core: 2. Of those that a mesh axis runs over, the one named last changes fastest.
Arguments:
- queries: bfloat16 [4, 8, 256, 40, 128], P('dp', 'seq'), may hold values from -6 to 6
- key_proj: bfloat16 [4, 8, 256, 40, 128], P('dp', 'seq'), may hold values from -6 to 6
- value_proj: bfloat16 [4, 8, 256, 40, 128], P('dp', 'seq'), may hold values from -6 to 6
- out_grad: bfloat16 [4, 8, 256, 40, 128], P('dp', 'seq'), may hold values from -6 to 6
- query_gain: float32 [40, 128], P('dp'), may hold values from 0.5 to 5
- key_gain: float32 [40, 128], P('dp'), may hold values from 0.5 to 5
Outputs:
- query_grad: bfloat16 [4, 8, 256, 40, 128], P('dp', 'seq')
- key_grad: bfloat16 [4, 8, 256, 40, 128], P('dp', 'seq')
- value_grad: bfloat16 [4, 8, 256, 40, 128], P('dp', 'seq')
- query_gain_grad: float32 [40, 128], P('dp')
- key_gain_grad: float32 [40, 128], P('dp')
The draws below stay inside these ranges and needn't reach their ends.
All inputs are finite; a program needn't handle non-finite values.
Results may differ from the reference program's by a relative error of at most 0.0034.
The reference program's roundings to bfloat16 on the way count: a program that leaves them out, or rounds other values in their place, can miss the bound.
Values may be sent and summed in bfloat16 or wider, within the bound.
No kernel may reach another device: no remote copies, remote signals or barrier semaphores. Data moves between devices by JAX's collectives and lax.ppermute only.
A program may use at most 128 MiB of HBM per device.

```python
import math
import jax
import jax.numpy as jnp
from jax import lax

HEADS = 40
HDIM = 128
PATCHES = 256
FRAMES = 8
EPIS = 4


def gain_base(key):
    return jnp.exp(jax.random.uniform(key, (HEADS, HDIM), jnp.float32, math.log(0.5), math.log(2.0)))


def draw_query_gain(key, part):
    key = jax.random.fold_in(key, 11)
    values = gain_base(key)
    return values


def draw_key_gain(key, part):
    key = jax.random.fold_in(key, 12)
    values = gain_base(key)
    return values


def draw_queries(key, part):
    key = jax.random.fold_in(key, 21)
    values = jnp.clip(jax.random.normal(key, (EPIS, FRAMES, PATCHES, HEADS, HDIM), jnp.float32), -6.0, 6.0)
    return values.astype(jnp.bfloat16)


def draw_key_proj(key, part):
    key = jax.random.fold_in(key, 22)
    values = jnp.clip(jax.random.normal(key, (EPIS, FRAMES, PATCHES, HEADS, HDIM), jnp.float32), -6.0, 6.0)
    return values.astype(jnp.bfloat16)


def level_of(rng, extent, cuts, smallest, top_value):
    def one(position, blocks):
        steps = jax.random.uniform(jax.random.fold_in(jax.random.fold_in(rng, 6), position), (blocks,), jnp.float32, smallest / len(cuts), top_value / len(cuts))
        return jnp.repeat(jnp.exp(steps), extent[position] // blocks).reshape((-1,) + (1,) * (len(extent) - position - 1))

    level = one(*cuts[0])
    for cut in cuts[1:]:
        level = level * one(*cut)
    return level


def bell_draw(key, shape, scale, bound, split=(), held_as=jnp.bfloat16):
    values = jax.random.normal(key, shape, jnp.float32) * scale
    if len(split) > 0:
        values = level_of(key, shape, split, -0.22, 0.18) * values
    return jnp.clip(values, min=-bound, max=bound).astype(held_as)


def setup_inputs(seed: int = 0) -> dict:
    streams_of = jax.random.split(jax.random.key(seed), 7)
    queries = draw_queries(jax.random.fold_in(streams_of[6], 71), 0)
    key_proj = draw_key_proj(jax.random.fold_in(streams_of[6], 71), 0)
    value_proj = bell_draw(streams_of[2], (EPIS, FRAMES, PATCHES, HEADS, HDIM), 1.0, 6.0, ((0, 4), (1, 8)))
    out_grad = bell_draw(streams_of[3], (EPIS, FRAMES, PATCHES, HEADS, HDIM), 1.0, 6.0, ((0, 4), (1, 8)))
    query_gain = draw_query_gain(jax.random.fold_in(streams_of[6], 71), 0)
    key_gain = draw_key_gain(jax.random.fold_in(streams_of[6], 71), 0)
    return dict(queries=queries, key_proj=key_proj, value_proj=value_proj, out_grad=out_grad, query_gain=query_gain, key_gain=key_gain)


EPSILON = 1e-06

def widen(values):
    return lax.optimization_barrier(values).astype(jnp.float32)

def normalize(values):
    wide = values.astype(jnp.float32)
    inverse = lax.rsqrt(lax.optimization_barrier(jnp.mean(wide * wide, axis=-1, keepdims=True)) + EPSILON)
    return (wide * inverse, inverse)

def norm_back(step, hat, inverse, gain):
    step_wide = widen(step)
    gained = gain * step_wide
    result = (inverse * (gained - hat * lax.optimization_barrier(jnp.mean(gained * hat, axis=-1, keepdims=True)))).astype(jnp.bfloat16)
    gain_part = lax.optimization_barrier(jnp.sum(step_wide * hat, axis=tuple(range(step.ndim - 2))))
    return (result, gain_part)

def attention_grads(query_norm, key_norm, value_in, grad_in):
    highest = lax.Precision.HIGHEST
    frames = query_norm.shape[0]
    scaling = 1.0 / math.sqrt(query_norm.shape[-1])
    query_wide = widen(query_norm)
    key_wide = widen(key_norm)
    value_wide = widen(value_in)
    grad_wide = widen(grad_in)
    scores = jnp.einsum('fphd,gphd->phfg', query_wide, key_wide, precision=highest) * scaling
    row_ids = lax.broadcasted_iota(jnp.int32, (frames, frames), 0)
    col_ids = lax.broadcasted_iota(jnp.int32, (frames, frames), 1)
    allowed = col_ids <= row_ids
    scores = jnp.where(allowed, scores, -jnp.inf)
    largest = lax.optimization_barrier(jnp.max(scores, axis=-1, keepdims=True))
    expo = jnp.exp(scores - largest)
    probability = expo / lax.optimization_barrier(jnp.sum(expo, axis=-1, keepdims=True))
    prob_wide = widen(probability.astype(jnp.bfloat16))
    attn_out = jnp.einsum('phfg,gphd->fphd', prob_wide, value_wide, precision=highest)
    row_dots = jnp.transpose(lax.optimization_barrier(jnp.sum(grad_wide * attn_out, axis=-1)), (1, 2, 0))
    prob_grad = jnp.einsum('fphd,gphd->phfg', grad_wide, value_wide, precision=highest)
    score_grad = probability * (prob_grad - row_dots[..., None])
    score_wide = widen(score_grad.astype(jnp.bfloat16))
    query_step = (jnp.einsum('phfg,gphd->fphd', score_wide, key_wide, precision=highest) * scaling).astype(jnp.bfloat16)
    key_step = (jnp.einsum('phfg,fphd->gphd', score_wide, query_wide, precision=highest) * scaling).astype(jnp.bfloat16)
    value_step = jnp.einsum('phfg,fphd->gphd', prob_wide, grad_wide, precision=highest).astype(jnp.bfloat16)
    return (query_step, key_step, value_step)

def reference(queries, key_proj, value_proj, out_grad, query_gain, key_gain):

    def episode(pieces):
        query_in, key_in, value_in, grad_in = pieces
        query_hat, query_inverse = normalize(query_in)
        key_hat, key_inverse = normalize(key_in)
        query_norm = (query_hat * query_gain).astype(jnp.bfloat16)
        key_norm = (key_hat * key_gain).astype(jnp.bfloat16)
        query_step, key_step, value_step = attention_grads(query_norm, key_norm, value_in, grad_in)
        query_out, query_part = norm_back(query_step, query_hat, query_inverse, query_gain)
        key_out, key_part = norm_back(key_step, key_hat, key_inverse, key_gain)
        return (query_out, key_out, value_step, query_part, key_part)
    query_out, key_out, value_out, query_parts, key_parts = lax.map(episode, (queries, key_proj, value_proj, out_grad))
    return (query_out, key_out, value_out, lax.optimization_barrier(jnp.sum(query_parts, axis=0)), lax.optimization_barrier(jnp.sum(key_parts, axis=0)))
```

```python
import functools
import math

import jax
import jax.numpy as jnp
from jax import lax
from jax.experimental import pallas as pl
from jax.experimental.pallas import tpu as pltpu
from jax.sharding import PartitionSpec as P

EPSILON = 1e-06
BLOCK = 256
GROUP = 16
SLOTS = 4
WIDE = GROUP * SLOTS
CUTS = (5, 5, 5, 5)

EDGE_S = ((0, 2), (1, 3), (6, 4), (7, 5))
EDGE_X = ((0, 3), (1, 2), (6, 5), (7, 4))
INTRA = ((2, 3), (3, 2), (4, 5), (5, 4))
MID_S = ((2, 4), (3, 5), (4, 2), (5, 3))
MID_X = ((2, 5), (3, 4), (4, 3), (5, 2))
DOWN = ((4, 2), (5, 3))
BACK_S = tuple((b, a) for a, b in EDGE_S)
BACK_X = tuple((b, a) for a, b in EDGE_X)

F32 = jnp.float32
BF16 = jnp.bfloat16
ANY = pl.BlockSpec(memory_space=pl.ANY)
VMEM = pl.BlockSpec(memory_space=pltpu.VMEM)


def place():
    index = lax.axis_index("seq")
    chip, core = index // 2, index % 2
    return chip, core


def pack_kernel(start, rows, q, k, v, g, a_s, a_x, b_s, b_x, sems):
    chip, core = place()

    def move(first, second):
        for left, right in ((first, (a_s, a_x)), (second, (b_s, b_x))):
            for t in range(2):
                for x in range(2):
                    half = core if x == 0 else 1 - core
                    yield left[t].at[half, pl.ds(start, rows)], right[x].at[t]

    def run(first, second):
        copies = [
            pltpu.make_async_copy(src, dst, sems.at[i])
            for i, (src, dst) in enumerate(move(first, second))
        ]
        for copy in copies:
            copy.start()
        for copy in copies:
            copy.wait()

    @pl.when(chip < 2)
    def _():
        run((k, v), (q, g))

    @pl.when(chip >= 2)
    def _():
        run((q, g), (k, v))


def pack(start, rows, arrays):
    return pl.pallas_call(
        functools.partial(pack_kernel, start, rows),
        out_shape=[jax.ShapeDtypeStruct((2, rows, 128), BF16)] * 4,
        in_specs=[ANY] * 4,
        out_specs=[ANY] * 4,
        scratch_shapes=[pltpu.SemaphoreType.DMA((8,))],
        cost_estimate=pl.CostEstimate(flops=0, bytes_accessed=rows * 128 * 2 * 16, transcendentals=0),
        name="pack_rows",
    )(*arrays)


def place_kernel(start, rows, own, other, back_s, back_x, *refs):
    outs, sems = refs[-4:-1], refs[-1]
    chip, core = place()

    def run(near, far):
        copies = []
        for t in range(3):
            for x, src in enumerate((near, far)):
                half = core if x == 0 else 1 - core
                copies.append(
                    pltpu.make_async_copy(
                        src.at[t], outs[t].at[half, pl.ds(start, rows)], sems.at[t * 2 + x]
                    )
                )
        for copy in copies:
            copy.start()
        for copy in copies:
            copy.wait()

    hub = (chip == 1) | (chip == 2)

    @pl.when(hub)
    def _():
        run(own, other)

    @pl.when(jnp.logical_not(hub))
    def _():
        run(back_s, back_x)


def unpack(start, rows, half, pieces, outs):
    first = outs is None
    outs = () if first else outs
    return pl.pallas_call(
        functools.partial(place_kernel, start, rows),
        out_shape=[jax.ShapeDtypeStruct((2, half, 128), BF16)] * 3,
        in_specs=[ANY] * (4 + len(outs)),
        out_specs=[ANY] * 3,
        scratch_shapes=[pltpu.SemaphoreType.DMA((6,))],
        input_output_aliases={} if first else {4: 0, 5: 1, 6: 2},
        cost_estimate=pl.CostEstimate(flops=0, bytes_accessed=rows * 128 * 2 * 12, transcendentals=0),
        name="place_rows",
    )(*pieces, *outs)


def rms(values):
    wide = values.astype(F32)
    inverse = lax.rsqrt(jnp.mean(wide * wide, axis=-1, keepdims=True) + EPSILON)
    return wide * inverse, inverse


def norm_back(step, hat, inverse, gain):
    wide = step.astype(F32)
    gained = gain * wide
    result = inverse * (gained - hat * jnp.mean(gained * hat, axis=-1, keepdims=True))
    return result.astype(BF16), wide * hat


def mul_t(a, b):
    return lax.dot_general(a, b, (((1,), (1,)), ((), ())), preferred_element_type=F32)


def t_mul(a, b):
    return lax.dot_general(a, b, (((0,), (0,)), ((), ())), preferred_element_type=F32)


def mul(a, b):
    return jnp.dot(a, b, preferred_element_type=F32)


def iota(shape, axis):
    return lax.broadcasted_iota(jnp.int32, shape, axis)


def attend(qn, kn, grad, value, allowed):
    scaling = 1.0 / math.sqrt(qn.shape[-1])
    scores = jnp.where(allowed, mul_t(qn, kn) * scaling, -jnp.inf)
    expo = jnp.exp(scores - jnp.max(scores, axis=-1, keepdims=True))
    prob = expo / jnp.sum(expo, axis=-1, keepdims=True)
    prob_low = prob.astype(BF16)
    prob_grad = mul_t(grad, value)
    dots = jnp.sum(prob_low.astype(F32) * prob_grad, axis=-1, keepdims=True)
    score_low = (prob * (prob_grad - dots)).astype(BF16)
    return prob_low, score_low


def frame_of(slot, core, upper):
    cross = slot % 2
    side = slot // 2
    side = side if upper else 1 - side
    return 2 * side + cross + core - 2 * cross * core


def causal(core, upper):
    shape = (WIDE, 2 * WIDE if upper else WIDE)
    rows, cols = iota(shape, 0), iota(shape, 1)
    key = cols // GROUP
    frame = frame_of(key % SLOTS, core, upper)
    if upper:
        frame = jnp.where(key < SLOTS, -1, frame)
    late = frame <= frame_of(rows // GROUP, core, upper)
    return (rows % GROUP == cols % GROUP) & late


def cat(parts):
    return jnp.concatenate(parts, axis=0)


def gains_of(ref, base, j):
    gain = ref[pl.ds(pl.multiple_of(base + j * GROUP, GROUP), GROUP), :]
    return cat([gain] * SLOTS)


def fold(acc, base, j, part):
    rows = pl.ds(pl.multiple_of(base + j * GROUP, GROUP), GROUP)
    total = part[:GROUP]
    for t in range(1, SLOTS):
        total = total + part[t * GROUP : (t + 1) * GROUP]
    acc[rows, :] += total


def settle(outs, rows, parts):
    for t, part in enumerate(parts):
        for s, out in enumerate(outs):
            out[t, rows, :] = part[s * GROUP : (s + 1) * GROUP]


def sum_heads(acc, heads):
    total = acc[0:heads, :]
    for i in range(1, acc.shape[0] // heads):
        total = total + acc[i * heads : (i + 1) * heads, :]
    return total


def upper_kernel(first, steps, heads, *refs):
    data, (gain_q, gain_k), outs = refs[:12], refs[12:14], refs[14:18]
    packed, sum_q, sum_k, acc_q, acc_k = refs[18:]
    chip, core = place()
    acc_q[...] = jnp.zeros_like(acc_q)
    acc_k[...] = jnp.zeros_like(acc_k)
    cycle = acc_q.shape[0] // BLOCK

    def block(*blocks):
        a, b, m = blocks[0:4], blocks[4:8], blocks[8:12]
        out, pack_ref = blocks[12:16], blocks[16]
        base = ((first + pl.program_id(0)) % cycle) * BLOCK
        allowed = causal(core, True)
        scaling = 1.0 / math.sqrt(128)
        lanes = iota((WIDE, 128), 1) // 8
        spread_r, spread_c = iota((2 * WIDE, 128), 0), iota((2 * WIDE, 128), 1)
        spread = jnp.where(spread_r // GROUP == spread_c % 8, 1.0, 0.0).astype(BF16)

        def group(j, total):
            rows = pl.ds(pl.multiple_of(j * GROUP, GROUP), GROUP)
            gq, gk = gains_of(gain_q, base, j), gains_of(gain_k, base, j)
            q_hat, q_inv = rms(cat([r[0, rows, :] for r in a]))
            grad = cat([r[1, rows, :] for r in a])
            kl_hat, _ = rms(cat([r[0, rows, :] for r in m]))
            ku_hat, ku_inv = rms(cat([r[0, rows, :] for r in b]))
            value = cat([r[1, rows, :] for r in (*m, *b)])
            qn = (q_hat * gq).astype(BF16)
            kn = cat([(kl_hat * gk).astype(BF16), (ku_hat * gk).astype(BF16)])
            prob, score = attend(qn, kn, grad, value, allowed)
            q_step = (mul(score, kn) * scaling).astype(BF16)
            k_step = (t_mul(score[:, WIDE:], qn) * scaling).astype(BF16)
            v_step = t_mul(prob[:, WIDE:], grad).astype(BF16)
            dq, part_q = norm_back(q_step, q_hat, q_inv, gq)
            dk, part_k = norm_back(k_step, ku_hat, ku_inv, gk)
            settle(out, rows, (dq, dk, v_step))
            fold(acc_q, base, j, part_q)
            fold(acc_k, base, j, part_k)
            cross = jnp.concatenate([prob[:, :WIDE], score[:, :WIDE]], axis=1)
            return jnp.where(lanes == j, mul(cross, spread), total)

        total = lax.fori_loop(0, BLOCK // GROUP, group, jnp.zeros((WIDE, 128), F32))
        pack_ref[0] = total.astype(BF16)

    @pl.when(chip == 2)
    def _():
        pltpu.emit_pipeline(
            block,
            grid=(steps,),
            in_specs=[pl.BlockSpec((2, BLOCK, 128), lambda i: (0, i, 0))] * 12,
            out_specs=[pl.BlockSpec((3, BLOCK, 128), lambda i: (0, i, 0))] * 4
            + [pl.BlockSpec((1, WIDE, 128), lambda i: (i, 0, 0))],
        )(*data, *outs, packed)

    sum_q[...] = sum_heads(acc_q, heads)
    sum_k[...] = sum_heads(acc_k, heads)


def lower_kernel(first, steps, heads, *refs):
    data, packed, (gain_q, gain_k) = refs[:12], refs[12], refs[13:15]
    outs = refs[19:23]
    sum_q, sum_k, acc_q, acc_k = refs[23:]
    chip, core = place()
    acc_q[...] = jnp.zeros_like(acc_q)
    acc_k[...] = jnp.zeros_like(acc_k)
    cycle = acc_q.shape[0] // BLOCK

    def block(*blocks):
        a, b, m = blocks[0:4], blocks[4:8], blocks[8:12]
        pack_ref, out = blocks[12], blocks[13:17]
        base = ((first + pl.program_id(0)) % cycle) * BLOCK
        allowed = causal(core, False)
        both = iota((WIDE, 2 * WIDE), 0) % GROUP == iota((WIDE, 2 * WIDE), 1) % GROUP
        scaling = 1.0 / math.sqrt(128)
        lanes = iota((WIDE, 128), 1) // 8
        spread_r, spread_c = iota((128, 2 * WIDE), 0), iota((128, 2 * WIDE), 1)
        spread = jnp.where(spread_c // GROUP == spread_r % 8, 1.0, 0.0).astype(BF16)
        crossed = pack_ref[0].astype(F32)

        def group(j, carry):
            rows = pl.ds(pl.multiple_of(j * GROUP, GROUP), GROUP)
            gq, gk = gains_of(gain_q, base, j), gains_of(gain_k, base, j)
            k_hat, k_inv = rms(cat([r[0, rows, :] for r in a]))
            value = cat([r[1, rows, :] for r in a])
            q_hat, q_inv = rms(cat([r[0, rows, :] for r in b]))
            grad = cat([r[1, rows, :] for r in b])
            qu_hat, _ = rms(cat([r[0, rows, :] for r in m]))
            grad_u = cat([r[1, rows, :] for r in m])
            kn = (k_hat * gk).astype(BF16)
            qn = (q_hat * gq).astype(BF16)
            qn_u = (qu_hat * gq).astype(BF16)
            prob, score = attend(qn, kn, grad, value, allowed)
            mine = jnp.where(lanes == j, crossed, 0.0).astype(BF16)
            cross = jnp.where(both, mul(mine, spread), 0.0).astype(BF16)
            q_step = (mul(score, kn) * scaling).astype(BF16)
            k_step = t_mul(cat([score, cross[:, WIDE:]]), cat([qn, qn_u]))
            k_step = (k_step * scaling).astype(BF16)
            v_step = t_mul(cat([prob, cross[:, :WIDE]]), cat([grad, grad_u])).astype(BF16)
            dq, part_q = norm_back(q_step, q_hat, q_inv, gq)
            dk, part_k = norm_back(k_step, k_hat, k_inv, gk)
            settle(out, rows, (dq, dk, v_step))
            fold(acc_q, base, j, part_q)
            fold(acc_k, base, j, part_k)
            return carry

        lax.fori_loop(0, BLOCK // GROUP, group, 0)

    @pl.when(chip == 1)
    def _():
        pltpu.emit_pipeline(
            block,
            grid=(steps,),
            in_specs=[pl.BlockSpec((2, BLOCK, 128), lambda i: (0, i, 0))] * 12
            + [pl.BlockSpec((1, WIDE, 128), lambda i: (i, 0, 0))],
            out_specs=[pl.BlockSpec((3, BLOCK, 128), lambda i: (0, i, 0))] * 4,
        )(*data, packed, *outs)

    sum_q[...] = sum_heads(acc_q, heads)
    sum_k[...] = sum_heads(acc_k, heads)


def hub_cost(rows):
    return pl.CostEstimate(
        flops=rows * 60000, bytes_accessed=rows * 128 * 2 * 36, transcendentals=rows * 600
    )


def upper(first, steps, heads, data, gains):
    rows = steps * BLOCK
    cycle = gains[0].shape[0]
    return pl.pallas_call(
        functools.partial(upper_kernel, first, steps, heads),
        out_shape=[jax.ShapeDtypeStruct((3, rows, 128), BF16)] * 4
        + [jax.ShapeDtypeStruct((steps, WIDE, 128), BF16)]
        + [jax.ShapeDtypeStruct((heads, 128), F32)] * 2,
        in_specs=[ANY] * 12 + [VMEM] * 2,
        out_specs=[ANY] * 5 + [VMEM] * 2,
        scratch_shapes=[pltpu.VMEM((cycle, 128), F32)] * 2,
        compiler_params=pltpu.CompilerParams(vmem_limit_bytes=40 * 1024 * 1024),
        cost_estimate=hub_cost(rows),
        name="upper_frames",
    )(*data, *gains)


def lower(first, steps, heads, data, packed, gains, outs):
    rows = steps * BLOCK
    cycle = gains[0].shape[0]
    return pl.pallas_call(
        functools.partial(lower_kernel, first, steps, heads),
        out_shape=[jax.ShapeDtypeStruct((3, rows, 128), BF16)] * 4
        + [jax.ShapeDtypeStruct((heads, 128), F32)] * 2,
        in_specs=[ANY] * 13 + [VMEM] * 2 + [ANY] * 4,
        out_specs=[ANY] * 4 + [VMEM] * 2,
        scratch_shapes=[pltpu.VMEM((cycle, 128), F32)] * 2,
        input_output_aliases={15 + i: i for i in range(4)},
        compiler_params=pltpu.CompilerParams(vmem_limit_bytes=40 * 1024 * 1024),
        cost_estimate=hub_cost(rows),
        name="lower_frames",
    )(*data, packed, *gains, *outs)


def send(array, pairs):
    return lax.ppermute(array, "seq", pairs)


def hub_body(queries, key_proj, value_proj, out_grad, query_gain, key_gain):
    shape = queries.shape
    heads, width = shape[-2:]
    half = shape[2] // 2 * heads
    arrays = [x.reshape(2, half, width) for x in (queries, key_proj, value_proj, out_grad)]
    cycle = math.lcm(BLOCK, heads)
    both = lax.all_gather(jnp.stack([query_gain, key_gain]), "dp", axis=1, tiled=True)
    gains = [jnp.tile(both[t], (cycle // heads, 1)) for t in range(2)]

    outs = None
    sums = []
    starts = [sum(CUTS[:i]) for i in range(len(CUTS))]
    landed = []
    for first, steps in zip(starts, CUTS):
        rows = steps * BLOCK
        a_s, a_x, b_s, b_x = pack(first * BLOCK, rows, arrays)
        ea_s, ea_x = send(a_s, EDGE_S), send(a_x, EDGE_X)
        m_s, m_x = send(a_s, MID_S), send(a_x, MID_X)
        eb_s, eb_x = send(b_s, EDGE_S), send(b_x, EDGE_X)
        a_i, b_i = send(a_x, INTRA), send(b_x, INTRA)
        n_s, n_x = send(ea_s, MID_S), send(ea_x, MID_S)
        landed.append([a_s, a_i, ea_s, ea_x, b_s, b_i, eb_s, eb_x, m_s, m_x, n_s, n_x])
    for first, steps, data in zip(starts, CUTS, landed):
        rows = steps * BLOCK
        *grads, packed, sum_q, sum_k = upper(first, steps, heads, data, gains)
        sums.append((sum_q, sum_k))
        packed = send(packed, DOWN)
        *grads, sum_q, sum_k = lower(first, steps, heads, data, packed, gains, grads)
        sums.append((sum_q, sum_k))
        own, other, edge_s, edge_x = grads
        pieces = (own, send(other, INTRA), send(edge_s, BACK_S), send(edge_x, BACK_X))
        outs = unpack(first * BLOCK, rows, half, pieces, outs)

    totals = [functools.reduce(jnp.add, [s[t] for s in sums]) for t in range(2)]
    totals = lax.psum(jnp.stack(totals), ("dp", "seq"))
    mine = query_gain.shape[0]
    totals = lax.dynamic_slice_in_dim(totals, lax.axis_index("dp") * mine, mine, 1)
    return (*[x.reshape(shape) for x in outs], totals[0], totals[1])


def wide_attention(query_norm, key_norm, value_in, grad_in):
    frames = query_norm.shape[1]
    scaling = 1.0 / math.sqrt(query_norm.shape[-1])
    scores = (
        jnp.einsum("efphd,egphd->ephfg", query_norm, key_norm, preferred_element_type=F32) * scaling
    )
    allowed = iota((frames, frames), 1) <= iota((frames, frames), 0)
    scores = jnp.where(allowed, scores, -jnp.inf)
    expo = jnp.exp(scores - jnp.max(scores, axis=-1, keepdims=True))
    probability = expo / jnp.sum(expo, axis=-1, keepdims=True)
    prob_low = probability.astype(BF16)
    attn_out = jnp.einsum("ephfg,egphd->efphd", prob_low, value_in, preferred_element_type=F32)
    row_dots = jnp.transpose(jnp.sum(grad_in.astype(F32) * attn_out, axis=-1), (0, 2, 3, 1))
    prob_grad = jnp.einsum("efphd,egphd->ephfg", grad_in, value_in, preferred_element_type=F32)
    score_low = (probability * (prob_grad - row_dots[..., None])).astype(BF16)
    query_step = jnp.einsum("ephfg,egphd->efphd", score_low, key_norm, preferred_element_type=F32)
    key_step = jnp.einsum("ephfg,efphd->egphd", score_low, query_norm, preferred_element_type=F32)
    value_step = jnp.einsum("ephfg,efphd->egphd", prob_low, grad_in, preferred_element_type=F32)
    return (
        (query_step * scaling).astype(BF16),
        (key_step * scaling).astype(BF16),
        value_step.astype(BF16),
    )


def wide_body(queries, key_proj, value_proj, out_grad, query_gain, key_gain):
    gain_q = lax.all_gather(query_gain, "dp", axis=0, tiled=True)
    gain_k = lax.all_gather(key_gain, "dp", axis=0, tiled=True)
    q_hat, q_inv = rms(queries)
    k_hat, k_inv = rms(key_proj)
    pieces = [
        lax.all_to_all(x, "seq", split_axis=2, concat_axis=1, tiled=True)
        for x in ((q_hat * gain_q).astype(BF16), (k_hat * gain_k).astype(BF16), value_proj, out_grad)
    ]
    steps = [
        lax.all_to_all(x, "seq", split_axis=1, concat_axis=2, tiled=True)
        for x in wide_attention(*pieces)
    ]
    query_grad, part_q = norm_back(steps[0], q_hat, q_inv, gain_q)
    key_grad, part_k = norm_back(steps[1], k_hat, k_inv, gain_k)
    axes = tuple(range(part_q.ndim - 2))
    totals = lax.psum((jnp.sum(part_q, axis=axes), jnp.sum(part_k, axis=axes)), "seq")
    totals = [lax.psum_scatter(t, "dp", scatter_dimension=0, tiled=True) for t in totals]
    return (query_grad, key_grad, steps[2], *totals)


def body(*args):
    frames = lax.axis_size("seq")
    patches, heads, width = args[0].shape[2:]
    rows = patches // 2 * heads
    if frames == 8 and args[0].shape[:2] == (1, 1) and width == 128 and rows == sum(CUTS) * BLOCK:
        return hub_body(*args)
    return wide_body(*args)


def solution(mesh):
    whole = P("dp", "seq", None, None, None)
    gain = P("dp", None)
    return jax.shard_map(
        body,
        mesh=mesh,
        in_specs=(whole,) * 4 + (gain,) * 2,
        out_specs=(whole,) * 3 + (gain,) * 2,
        check_vma=False,
    )
```

```python
import functools
import math

import jax
import jax.numpy as jnp
from jax import lax
from jax.experimental import pallas as pl
from jax.experimental.pallas import tpu as pltpu
from jax.sharding import PartitionSpec as P

EPSILON = 1e-06
BLOCK = 256
GROUP = 16
SLOTS = 4
WIDE = GROUP * SLOTS
TOGETHER = 64
CUTS = (5, 5, 5, 5)

EDGE = ((0, 2), (1, 3), (6, 4), (7, 5))
MIDDLE = ((2, 4), (3, 5), (4, 2), (5, 3))
DOWN = ((4, 2), (5, 3))
BACK_S = ((2, 0), (3, 1), (4, 6), (5, 7))
BACK_X = ((2, 1), (3, 0), (4, 7), (5, 6))
SWAP = tuple((i, i ^ 1) for i in range(8))

F32 = jnp.float32
BF16 = jnp.bfloat16
ANY = pl.BlockSpec(memory_space=pltpu.HBM)
VMEM = pl.BlockSpec(memory_space=pltpu.VMEM)


def place():
    index = lax.axis_index("seq")
    chip, core = index // 2, index % 2
    return chip, core


def pack_kernel(first, steps, offset, q, k, v, g, x, a, b):
    chip, core = place()

    def run(pair_a, pair_b, index_a, index_b):
        def step(*refs):
            out_a, out_b = refs[-2:]
            for t in range(2):
                out_a[t] = refs[t][0]
                out_a[2 + t] = refs[4 + t][0]
                out_b[t] = refs[2 + t][0]
                out_b[2 + t] = refs[6 + t][0]

        def swapped(index):
            return pl.BlockSpec((1, BLOCK, 128), lambda i: (index, first - offset + i, 0))

        pltpu.emit_pipeline(
            step,
            grid=(steps,),
            in_specs=[pl.BlockSpec((1, BLOCK, 128), lambda i: (core, first + i, 0))] * 4
            + [swapped(index) for index in (*index_a, *index_b)],
            out_specs=[pl.BlockSpec((4, BLOCK, 128), lambda i: (0, i, 0))] * 2,
        )(*pair_a, *pair_b, *([x] * 4), a, b)

    @pl.when(chip < 2)
    def _():
        run((k, v), (q, g), (1, 2), (0, 3))

    @pl.when(chip >= 2)
    def _():
        run((q, g), (k, v), (0, 3), (1, 2))


def pack(first, steps, offset, arrays, swapped):
    rows = steps * BLOCK
    return pl.pallas_call(
        functools.partial(pack_kernel, first, steps, offset),
        out_shape=[jax.ShapeDtypeStruct((4, rows, 128), BF16)] * 2,
        in_specs=[ANY] * 5,
        out_specs=[ANY] * 2,
        compiler_params=pltpu.CompilerParams(vmem_limit_bytes=32 * 1024 * 1024),
        cost_estimate=pl.CostEstimate(flops=0, bytes_accessed=rows * 128 * 2 * 16, transcendentals=0),
        name="pack_rows",
    )(*arrays, swapped)


def place_kernel(slot, own, other, back_s, back_x, *refs):
    outs = refs[-3:]
    chip, core = place()
    hub = (chip == 1) | (chip == 2)

    def run(chunk, near, far):
        first, steps = sum(CUTS[:chunk]), CUTS[chunk]

        def step(half):
            def copy(src, *dsts):
                for t, dst in enumerate(dsts):
                    dst[0] = src[t]

            return copy

        for half, src in ((core, near), (1 - core, far)):
            pltpu.emit_pipeline(
                step(half),
                grid=(steps,),
                in_specs=[pl.BlockSpec((3, BLOCK, 128), lambda i: (0, i, 0))],
                out_specs=[pl.BlockSpec((1, BLOCK, 128), lambda i, half=half: (half, first + i, 0))] * 3,
            )(src, *outs)

    if slot < len(CUTS):

        @pl.when(chip == 2)
        def _():
            run(slot, own, other)

        @pl.when(chip == 3)
        def _():
            run(slot, back_s, back_x)

    if slot > 0:

        @pl.when(chip == 1)
        def _():
            run(slot - 1, own, other)

        @pl.when(chip == 0)
        def _():
            run(slot - 1, back_s, back_x)


def unpack(slot, half, pieces, outs):
    first = outs is None
    outs = () if first else outs
    return pl.pallas_call(
        functools.partial(place_kernel, slot),
        out_shape=[jax.ShapeDtypeStruct((2, half, 128), BF16)] * 3,
        in_specs=[ANY] * (4 + len(outs)),
        out_specs=[ANY] * 3,
        input_output_aliases={} if first else {4: 0, 5: 1, 6: 2},
        compiler_params=pltpu.CompilerParams(vmem_limit_bytes=32 * 1024 * 1024),
        cost_estimate=pl.CostEstimate(
            flops=0, bytes_accessed=max(CUTS) * BLOCK * 128 * 2 * 12, transcendentals=0
        ),
        name="place_rows",
    )(*pieces, *outs)


def rms(values):
    wide = values.astype(F32)
    inverse = lax.rsqrt(jnp.mean(wide * wide, axis=-1, keepdims=True) + EPSILON)
    return wide * inverse, inverse


def norm_back(step, hat, inverse, gain):
    wide = step.astype(F32)
    gained = gain * wide
    result = inverse * (gained - hat * jnp.mean(gained * hat, axis=-1, keepdims=True))
    return result.astype(BF16), wide * hat


def mul_t(a, b):
    return lax.dot_general(a, b, (((1,), (1,)), ((), ())), preferred_element_type=F32)


def t_mul(a, b):
    return lax.dot_general(a, b, (((0,), (0,)), ((), ())), preferred_element_type=F32)


def mul(a, b):
    return jnp.dot(a, b, preferred_element_type=F32)


def iota(shape, axis):
    return lax.broadcasted_iota(jnp.int32, shape, axis)


def frame_of(slot, core, upper):
    cross = slot % 2
    side = slot // 2
    side = side if upper else 1 - side
    return 2 * side + cross + core - 2 * cross * core


def causal(core, upper):
    shape = (WIDE, 2 * WIDE if upper else WIDE)
    rows, cols = iota(shape, 0), iota(shape, 1)
    key = cols // GROUP
    frame = frame_of(key % SLOTS, core, upper)
    if upper:
        frame = jnp.where(key < SLOTS, -1, frame)
    late = frame <= frame_of(rows // GROUP, core, upper)
    return (rows % GROUP == cols % GROUP) & late


def cat(parts):
    return jnp.concatenate(parts, axis=0)


def tiled(gain):
    return cat([gain] * SLOTS)


def group(wide, j):
    slots = wide.shape[0] // TOGETHER
    return cat([wide[s * TOGETHER + j * GROUP :][:GROUP] for s in range(slots)])


def ungroup(parts):
    return cat([part[s * GROUP :][:GROUP] for s in range(SLOTS) for part in parts])


def fold(acc, rows, part):
    total = part[:TOGETHER]
    for s in range(1, SLOTS):
        total = total + part[s * TOGETHER :][:TOGETHER]
    acc[rows, :] += total


def settle(outs, rows, parts):
    for t, part in enumerate(parts):
        for s, out in enumerate(outs):
            out[t, rows, :] = part[s * TOGETHER :][:TOGETHER]


def sum_heads(acc, heads):
    total = acc[0:heads, :]
    for i in range(1, acc.shape[0] // heads):
        total = total + acc[i * heads : (i + 1) * heads, :]
    return total


def read(refs, t, rows):
    return cat([ref[2 * x + t, rows, :] for ref in refs for x in range(2)])


def attend(qn, kn, grad, value, allowed):
    scaling = 1.0 / math.sqrt(qn.shape[-1])
    count = TOGETHER // GROUP
    scores = cat([mul_t(group(qn, j), group(kn, j)) for j in range(count)])
    prob_grad = cat([mul_t(group(grad, j), group(value, j)) for j in range(count)])
    mask = cat([allowed] * count)
    scores = jnp.where(mask > 0, scores * scaling, -jnp.inf)
    expo = jnp.exp(scores - jnp.max(scores, axis=-1, keepdims=True))
    prob = expo * (1.0 / jnp.sum(expo, axis=-1, keepdims=True))
    prob_low = prob.astype(BF16)
    dots = jnp.sum(prob_low.astype(F32) * prob_grad, axis=-1, keepdims=True)
    score_low = (prob * (prob_grad - dots)).astype(BF16)
    split = lambda x: [x[j * WIDE :][:WIDE] for j in range(count)]
    return split(prob_low), split(score_low)


def upper_kernel(first, steps, heads, own_a, edge_a, own_b, edge_b, other, far, gain_q, gain_k, *refs):
    outs, packed, (sum_q, sum_k, acc_q, acc_k, mask) = refs[:4], refs[4], refs[5:]
    chip, core = place()
    count = TOGETHER // GROUP
    acc_q[...] = jnp.zeros_like(acc_q)
    acc_k[...] = jnp.zeros_like(acc_k)
    cycle = acc_q.shape[0] // BLOCK

    def block(own_a, edge_a, own_b, edge_b, other, far, out_s, out_x, out_es, out_ex, pack_ref):
        base = ((first + pl.program_id(0)) % cycle) * BLOCK
        scaling = 1.0 / math.sqrt(128)
        lanes = iota((WIDE, 128), 1) // 8
        spread_r, spread_c = iota((2 * WIDE, 128), 0), iota((2 * WIDE, 128), 1)
        spread = jnp.where(spread_r // GROUP == spread_c % 8, 1.0, 0.0).astype(BF16)

        def some(i, total):
            rows = pl.ds(pl.multiple_of(i * TOGETHER, TOGETHER), TOGETHER)
            place = pl.ds(pl.multiple_of(base + i * TOGETHER, TOGETHER), TOGETHER)
            gq, gk = tiled(gain_q[place, :]), tiled(gain_k[place, :])
            q_hat, q_inv = rms(read((own_a, edge_a), 0, rows))
            grad = read((own_a, edge_a), 1, rows)
            kl_hat, _ = rms(read((other, far), 0, rows))
            ku_hat, ku_inv = rms(read((own_b, edge_b), 0, rows))
            value = cat([read((other, far), 1, rows), read((own_b, edge_b), 1, rows)])
            qn = (q_hat * gq).astype(BF16)
            kn = cat([(kl_hat * gk).astype(BF16), (ku_hat * gk).astype(BF16)])
            prob, score = attend(qn, kn, grad, value, mask[...])
            q_step = ungroup([mul(score[j], group(kn, j)) for j in range(count)])
            k_step = ungroup([t_mul(score[j][:, WIDE:], group(qn, j)) for j in range(count)])
            v_step = ungroup([t_mul(prob[j][:, WIDE:], group(grad, j)) for j in range(count)])
            q_step, k_step = (q_step * scaling).astype(BF16), (k_step * scaling).astype(BF16)
            dq, part_q = norm_back(q_step, q_hat, q_inv, gq)
            dk, part_k = norm_back(k_step, ku_hat, ku_inv, gk)
            settle((out_s, out_x, out_es, out_ex), rows, (dq, dk, v_step.astype(BF16)))
            fold(acc_q, place, part_q)
            fold(acc_k, place, part_k)
            for j in range(count):
                cross = jnp.concatenate([prob[j][:, :WIDE], score[j][:, :WIDE]], axis=1)
                total = jnp.where(lanes == i * count + j, mul(cross, spread), total)
            return total

        total = lax.fori_loop(0, BLOCK // TOGETHER, some, jnp.zeros((WIDE, 128), F32))
        pack_ref[0] = total.astype(BF16)

    @pl.when(chip == 2)
    def _():
        mask[...] = causal(core, True).astype(F32)
        pltpu.emit_pipeline(
            block,
            grid=(steps,),
            in_specs=[pl.BlockSpec((4, BLOCK, 128), lambda i: (0, i, 0))] * 6,
            out_specs=[pl.BlockSpec((3, BLOCK, 128), lambda i: (0, i, 0))] * 4
            + [pl.BlockSpec((1, WIDE, 128), lambda i: (i, 0, 0))],
        )(own_a, edge_a, own_b, edge_b, other, far, *outs, packed)

    sum_q[...] = sum_heads(acc_q, heads)
    sum_k[...] = sum_heads(acc_k, heads)


def lower_kernel(first, steps, heads, own_a, edge_a, own_b, edge_b, other, far, packed, gain_q, gain_k, *refs):
    outs, (sum_q, sum_k, acc_q, acc_k, mask) = refs[4:8], refs[8:]
    chip, core = place()
    count = TOGETHER // GROUP
    acc_q[...] = jnp.zeros_like(acc_q)
    acc_k[...] = jnp.zeros_like(acc_k)
    cycle = acc_q.shape[0] // BLOCK

    def block(own_a, edge_a, own_b, edge_b, other, far, pack_ref, out_s, out_x, out_es, out_ex):
        base = ((first + pl.program_id(0)) % cycle) * BLOCK
        both = iota((WIDE, 2 * WIDE), 0) % GROUP == iota((WIDE, 2 * WIDE), 1) % GROUP
        scaling = 1.0 / math.sqrt(128)
        lanes = iota((WIDE, 128), 1) // 8
        spread_r, spread_c = iota((128, 2 * WIDE), 0), iota((128, 2 * WIDE), 1)
        spread = jnp.where(spread_c // GROUP == spread_r % 8, 1.0, 0.0).astype(BF16)
        crossed = pack_ref[0].astype(F32)

        def some(i, carry):
            rows = pl.ds(pl.multiple_of(i * TOGETHER, TOGETHER), TOGETHER)
            place = pl.ds(pl.multiple_of(base + i * TOGETHER, TOGETHER), TOGETHER)
            gq, gk = tiled(gain_q[place, :]), tiled(gain_k[place, :])
            k_hat, k_inv = rms(read((own_a, edge_a), 0, rows))
            value = read((own_a, edge_a), 1, rows)
            q_hat, q_inv = rms(read((own_b, edge_b), 0, rows))
            grad = read((own_b, edge_b), 1, rows)
            qu_hat, _ = rms(read((other, far), 0, rows))
            grad_u = read((other, far), 1, rows)
            kn = (k_hat * gk).astype(BF16)
            qn = (q_hat * gq).astype(BF16)
            qn_u = (qu_hat * gq).astype(BF16)
            prob, score = attend(qn, kn, grad, value, mask[...])
            cross = []
            for j in range(count):
                mine = jnp.where(lanes == i * count + j, crossed, 0.0).astype(BF16)
                cross.append(jnp.where(both, mul(mine, spread), 0.0).astype(BF16))
            q_step = ungroup([mul(score[j], group(kn, j)) for j in range(count)])
            k_step = ungroup(
                [
                    t_mul(cat([score[j], cross[j][:, WIDE:]]), cat([group(qn, j), group(qn_u, j)]))
                    for j in range(count)
                ]
            )
            v_step = ungroup(
                [
                    t_mul(cat([prob[j], cross[j][:, :WIDE]]), cat([group(grad, j), group(grad_u, j)]))
                    for j in range(count)
                ]
            )
            q_step, k_step = (q_step * scaling).astype(BF16), (k_step * scaling).astype(BF16)
            dq, part_q = norm_back(q_step, q_hat, q_inv, gq)
            dk, part_k = norm_back(k_step, k_hat, k_inv, gk)
            settle((out_s, out_x, out_es, out_ex), rows, (dq, dk, v_step.astype(BF16)))
            fold(acc_q, place, part_q)
            fold(acc_k, place, part_k)
            return carry

        lax.fori_loop(0, BLOCK // TOGETHER, some, 0)

    @pl.when(chip == 1)
    def _():
        mask[...] = causal(core, False).astype(F32)
        pltpu.emit_pipeline(
            block,
            grid=(steps,),
            in_specs=[pl.BlockSpec((4, BLOCK, 128), lambda i: (0, i, 0))] * 6
            + [pl.BlockSpec((1, WIDE, 128), lambda i: (i, 0, 0))],
            out_specs=[pl.BlockSpec((3, BLOCK, 128), lambda i: (0, i, 0))] * 4,
        )(own_a, edge_a, own_b, edge_b, other, far, packed, *outs)

    sum_q[...] = sum_heads(acc_q, heads)
    sum_k[...] = sum_heads(acc_k, heads)


def hub_cost(rows):
    return pl.CostEstimate(
        flops=rows * 60000, bytes_accessed=rows * 128 * 2 * 36, transcendentals=rows * 600
    )


def out_rows(slot):
    return max(CUTS[max(slot - 1, 0) : slot + 1]) * BLOCK


def upper(slot, heads, data, gains):
    steps = CUTS[slot]
    cycle = gains[0].shape[0]
    return pl.pallas_call(
        functools.partial(upper_kernel, sum(CUTS[:slot]), steps, heads),
        out_shape=[jax.ShapeDtypeStruct((3, out_rows(slot), 128), BF16)] * 4
        + [jax.ShapeDtypeStruct((steps, WIDE, 128), BF16)]
        + [jax.ShapeDtypeStruct((heads, 128), F32)] * 2,
        in_specs=[ANY] * 6 + [VMEM] * 2,
        out_specs=[ANY] * 5 + [VMEM] * 2,
        scratch_shapes=[pltpu.VMEM((cycle, 128), F32)] * 2 + [pltpu.VMEM((WIDE, 2 * WIDE), F32)],
        compiler_params=pltpu.CompilerParams(vmem_limit_bytes=40 * 1024 * 1024),
        cost_estimate=hub_cost(steps * BLOCK),
        name="upper_frames",
    )(*data, *gains)


def lower(slot, heads, data, packed, gains, outs):
    chunk = slot - 1
    steps = CUTS[chunk]
    cycle = gains[0].shape[0]
    return pl.pallas_call(
        functools.partial(lower_kernel, sum(CUTS[:chunk]), steps, heads),
        out_shape=[jax.ShapeDtypeStruct((3, out_rows(slot), 128), BF16)] * 4
        + [jax.ShapeDtypeStruct((heads, 128), F32)] * 2,
        in_specs=[ANY] * 7 + [VMEM] * 2 + [ANY] * 4,
        out_specs=[ANY] * 4 + [VMEM] * 2,
        scratch_shapes=[pltpu.VMEM((cycle, 128), F32)] * 2 + [pltpu.VMEM((WIDE, WIDE), F32)],
        input_output_aliases={9 + i: i for i in range(4)},
        compiler_params=pltpu.CompilerParams(vmem_limit_bytes=40 * 1024 * 1024),
        cost_estimate=hub_cost(steps * BLOCK),
        name="lower_frames",
    )(*data, packed, *gains, *outs)


def blank(slot):
    def kernel(*refs):
        pass

    return pl.pallas_call(
        kernel,
        out_shape=[jax.ShapeDtypeStruct((3, out_rows(slot), 128), BF16)] * 4,
        out_specs=[ANY] * 4,
        name="blank_rows",
    )()


def send(array, pairs):
    return lax.ppermute(array, "seq", pairs)


def hub_body(queries, key_proj, value_proj, out_grad, query_gain, key_gain):
    shape = queries.shape
    heads, width = shape[-2:]
    half = shape[2] // 2 * heads
    arrays = [x.reshape(2, half, width) for x in (queries, key_proj, value_proj, out_grad)]
    cycle = math.lcm(BLOCK, heads)
    other = 1 - lax.axis_index("seq") % 2
    chunks = len(CUTS)

    swapped = []
    for low, high in ((0, CUTS[0]), (CUTS[0], sum(CUTS))):
        rows = [
            lax.dynamic_slice(x, (other, low * BLOCK, 0), (1, (high - low) * BLOCK, width))
            for x in arrays
        ]
        swapped.append((send(jnp.concatenate(rows, axis=0), SWAP), low))

    landed = []
    for chunk in range(chunks):
        own_a, own_b = pack(
            sum(CUTS[:chunk]), CUTS[chunk], swapped[min(chunk, 1)][1], arrays, swapped[min(chunk, 1)][0]
        )
        edge_a = send(own_a, EDGE)
        other_a = send(own_a, MIDDLE)
        edge_b = send(own_b, EDGE)
        far_a = send(edge_a, MIDDLE)
        landed.append((own_a, edge_a, own_b, edge_b, other_a, far_a))

    both = lax.all_gather(jnp.stack([query_gain, key_gain]), "dp", axis=1, tiled=True)
    gains = [jnp.tile(both[t], (cycle // heads, 1)) for t in range(2)]

    outs = None
    sums = []
    packed = None
    for slot in range(chunks + 1):
        last = packed
        if slot < chunks:
            *grads, packed, sum_q, sum_k = upper(slot, heads, landed[slot], gains)
            packed = send(packed, DOWN)
            sums.append((sum_q, sum_k))
        else:
            grads = blank(slot)
        if slot > 0:
            *grads, sum_q, sum_k = lower(slot, heads, landed[slot - 1], last, gains, grads)
            sums.append((sum_q, sum_k))
        own, cross, edge_s, edge_x = grads
        pieces = (own, send(cross, SWAP), send(edge_s, BACK_S), send(edge_x, BACK_X))
        outs = unpack(slot, half, pieces, outs)

    totals = [functools.reduce(jnp.add, [s[t] for s in sums]) for t in range(2)]
    totals = lax.psum(jnp.stack(totals), ("dp", "seq"))
    mine = query_gain.shape[0]
    totals = lax.dynamic_slice_in_dim(totals, lax.axis_index("dp") * mine, mine, 1)
    return (*[x.reshape(shape) for x in outs], totals[0], totals[1])


def wide_attention(query_norm, key_norm, value_in, grad_in):
    frames = query_norm.shape[1]
    scaling = 1.0 / math.sqrt(query_norm.shape[-1])
    scores = (
        jnp.einsum("efphd,egphd->ephfg", query_norm, key_norm, preferred_element_type=F32) * scaling
    )
    allowed = iota((frames, frames), 1) <= iota((frames, frames), 0)
    scores = jnp.where(allowed, scores, -jnp.inf)
    expo = jnp.exp(scores - jnp.max(scores, axis=-1, keepdims=True))
    probability = expo / jnp.sum(expo, axis=-1, keepdims=True)
    prob_low = probability.astype(BF16)
    attn_out = jnp.einsum("ephfg,egphd->efphd", prob_low, value_in, preferred_element_type=F32)
    row_dots = jnp.transpose(jnp.sum(grad_in.astype(F32) * attn_out, axis=-1), (0, 2, 3, 1))
    prob_grad = jnp.einsum("efphd,egphd->ephfg", grad_in, value_in, preferred_element_type=F32)
    score_low = (probability * (prob_grad - row_dots[..., None])).astype(BF16)
    query_step = jnp.einsum("ephfg,egphd->efphd", score_low, key_norm, preferred_element_type=F32)
    key_step = jnp.einsum("ephfg,efphd->egphd", score_low, query_norm, preferred_element_type=F32)
    value_step = jnp.einsum("ephfg,efphd->egphd", prob_low, grad_in, preferred_element_type=F32)
    return (
        (query_step * scaling).astype(BF16),
        (key_step * scaling).astype(BF16),
        value_step.astype(BF16),
    )


def wide_body(queries, key_proj, value_proj, out_grad, query_gain, key_gain):
    gain_q = lax.all_gather(query_gain, "dp", axis=0, tiled=True)
    gain_k = lax.all_gather(key_gain, "dp", axis=0, tiled=True)
    q_hat, q_inv = rms(queries)
    k_hat, k_inv = rms(key_proj)
    pieces = [
        lax.all_to_all(x, "seq", split_axis=2, concat_axis=1, tiled=True)
        for x in ((q_hat * gain_q).astype(BF16), (k_hat * gain_k).astype(BF16), value_proj, out_grad)
    ]
    steps = [
        lax.all_to_all(x, "seq", split_axis=1, concat_axis=2, tiled=True)
        for x in wide_attention(*pieces)
    ]
    query_grad, part_q = norm_back(steps[0], q_hat, q_inv, gain_q)
    key_grad, part_k = norm_back(steps[1], k_hat, k_inv, gain_k)
    axes = tuple(range(part_q.ndim - 2))
    totals = lax.psum((jnp.sum(part_q, axis=axes), jnp.sum(part_k, axis=axes)), "seq")
    totals = [lax.psum_scatter(t, "dp", scatter_dimension=0, tiled=True) for t in totals]
    return (query_grad, key_grad, steps[2], *totals)


def body(*args):
    frames = lax.axis_size("seq")
    patches, heads, width = args[0].shape[2:]
    rows = patches // 2 * heads
    if frames == 8 and args[0].shape[:2] == (1, 1) and width == 128 and rows == sum(CUTS) * BLOCK:
        return hub_body(*args)
    return wide_body(*args)


def solution(mesh):
    whole = P("dp", "seq", None, None, None)
    gain = P("dp", None)
    return jax.shard_map(
        body,
        mesh=mesh,
        in_specs=(whole,) * 4 + (gain,) * 2,
        out_specs=(whole,) * 3 + (gain,) * 2,
        check_vma=False,
    )
```

```python
import functools
import math

import jax
import jax.numpy as jnp
from jax import lax
from jax.experimental import pallas as pl
from jax.experimental.pallas import tpu as pltpu
from jax.sharding import PartitionSpec as P

EPSILON = 1e-06
BLOCK = 256
GROUP = 16
SLOTS = 4
WIDE = GROUP * SLOTS
TOGETHER = 64
CUTS = (3, 5, 6, 4, 2)

EDGE = ((0, 2), (1, 3), (6, 4), (7, 5))
MIDDLE = ((2, 4), (3, 5), (4, 2), (5, 3))
DOWN = ((4, 2), (5, 3))
BACK_S = ((2, 0), (3, 1), (4, 6), (5, 7))
BACK_X = ((2, 1), (3, 0), (4, 7), (5, 6))
SWAP = tuple((i, i ^ 1) for i in range(8))

F32 = jnp.float32
BF16 = jnp.bfloat16
ANY = pl.BlockSpec(memory_space=pl.ANY)
VMEM = pl.BlockSpec(memory_space=pltpu.VMEM)


def place():
    index = lax.axis_index("seq")
    chip, core = index // 2, index % 2
    return chip, core


def call(kernel, inputs, in_specs, after=(), **kwargs):
    count, extra = len(inputs), len(after)

    def trimmed(*refs):
        kernel(*refs[:count], *refs[count + extra :])

    return pl.pallas_call(
        trimmed,
        in_specs=list(in_specs) + [ANY] * extra,
        compiler_params=pltpu.CompilerParams(vmem_limit_bytes=56 * 1024 * 1024),
        **kwargs,
    )(*inputs, *after)


def halves_kernel(first, steps, *refs):
    ins, out = refs[:4], refs[4]
    _, core = place()

    def step(*blocks):
        for t in range(4):
            blocks[4][t] = blocks[t][0]

    pltpu.emit_pipeline(
        step,
        grid=(steps,),
        in_specs=[pl.BlockSpec((1, BLOCK, 128), lambda i: (1 - core, first + i, 0))] * 4,
        out_specs=[pl.BlockSpec((4, BLOCK, 128), lambda i: (0, i, 0))],
    )(*ins, out)


def halves(first, steps, arrays, after):
    rows = steps * BLOCK
    return call(
        functools.partial(halves_kernel, first, steps),
        arrays,
        [ANY] * 4,
        after,
        out_shape=jax.ShapeDtypeStruct((4, rows, 128), BF16),
        out_specs=ANY,
        cost_estimate=pl.CostEstimate(flops=0, bytes_accessed=rows * 128 * 2 * 8, transcendentals=0),
        name="other_half",
    )


def pack_kernel(first, steps, offset, q, k, v, g, x, a, b):
    chip, core = place()

    def run(pair_a, pair_b, index_a, index_b):
        def step(*refs):
            out_a, out_b = refs[-2:]
            for t in range(2):
                out_a[t] = refs[t][0]
                out_a[2 + t] = refs[4 + t][0]
                out_b[t] = refs[2 + t][0]
                out_b[2 + t] = refs[6 + t][0]

        def swapped(index):
            return pl.BlockSpec((1, BLOCK, 128), lambda i: (index, first - offset + i, 0))

        pltpu.emit_pipeline(
            step,
            grid=(steps,),
            in_specs=[pl.BlockSpec((1, BLOCK, 128), lambda i: (core, first + i, 0))] * 4
            + [swapped(index) for index in (*index_a, *index_b)],
            out_specs=[pl.BlockSpec((4, BLOCK, 128), lambda i: (0, i, 0))] * 2,
        )(*pair_a, *pair_b, *([x] * 4), a, b)

    @pl.when(chip < 2)
    def _():
        run((k, v), (q, g), (1, 2), (0, 3))

    @pl.when(chip >= 2)
    def _():
        run((q, g), (k, v), (0, 3), (1, 2))


def pack(first, steps, offset, arrays, swapped, after):
    rows = steps * BLOCK
    return call(
        functools.partial(pack_kernel, first, steps, offset),
        (*arrays, swapped),
        [ANY] * 5,
        after,
        out_shape=[jax.ShapeDtypeStruct((4, rows, 128), BF16)] * 2,
        out_specs=[ANY] * 2,
        cost_estimate=pl.CostEstimate(flops=0, bytes_accessed=rows * 128 * 2 * 16, transcendentals=0),
        name="pack_rows",
    )


def place_kernel(slot, own, other, back_s, back_x, *refs):
    outs = refs[-3:]
    chip, core = place()
    hub = (chip == 1) | (chip == 2)

    def run(chunk, near, far):
        first, steps = sum(CUTS[:chunk]), CUTS[chunk]

        def step(half):
            def copy(src, *dsts):
                for t, dst in enumerate(dsts):
                    dst[0] = src[t]

            return copy

        for half, src in ((core, near), (1 - core, far)):
            pltpu.emit_pipeline(
                step(half),
                grid=(steps,),
                in_specs=[pl.BlockSpec((3, BLOCK, 128), lambda i: (0, i, 0))],
                out_specs=[pl.BlockSpec((1, BLOCK, 128), lambda i, half=half: (half, first + i, 0))] * 3,
            )(src, *outs)

    if slot < len(CUTS):

        @pl.when(chip == 2)
        def _():
            run(slot, own, other)

        @pl.when(chip == 3)
        def _():
            run(slot, back_s, back_x)

    if slot > 0:

        @pl.when(chip == 1)
        def _():
            run(slot - 1, own, other)

        @pl.when(chip == 0)
        def _():
            run(slot - 1, back_s, back_x)


def unpack(slot, half, pieces, outs):
    first = outs is None
    outs = () if first else outs
    return call(
        functools.partial(place_kernel, slot),
        (*pieces, *outs),
        [ANY] * (4 + len(outs)),
        out_shape=[jax.ShapeDtypeStruct((2, half, 128), BF16)] * 3,
        out_specs=[ANY] * 3,
        input_output_aliases={} if first else {4: 0, 5: 1, 6: 2},
        cost_estimate=pl.CostEstimate(
            flops=0, bytes_accessed=out_rows(slot) * 128 * 2 * 12, transcendentals=0
        ),
        name="place_rows",
    )


def rms(values):
    wide = values.astype(F32)
    inverse = lax.rsqrt(jnp.mean(wide * wide, axis=-1, keepdims=True) + EPSILON)
    return wide * inverse, inverse


def norm_back(step, hat, inverse, gain):
    wide = step.astype(F32)
    gained = gain * wide
    result = inverse * (gained - hat * jnp.mean(gained * hat, axis=-1, keepdims=True))
    return result.astype(BF16), wide * hat


def mul_t(a, b):
    return lax.dot_general(a, b, (((1,), (1,)), ((), ())), preferred_element_type=F32)


def t_mul(a, b):
    return lax.dot_general(a, b, (((0,), (0,)), ((), ())), preferred_element_type=F32)


def mul(a, b):
    return jnp.dot(a, b, preferred_element_type=F32)


def iota(shape, axis):
    return lax.broadcasted_iota(jnp.int32, shape, axis)


def frame_of(slot, core, upper):
    cross = slot % 2
    side = slot // 2
    side = side if upper else 1 - side
    return 2 * side + cross + core - 2 * cross * core


def causal(core, upper):
    shape = (WIDE, 2 * WIDE if upper else WIDE)
    rows, cols = iota(shape, 0), iota(shape, 1)
    key = cols // GROUP
    frame = frame_of(key % SLOTS, core, upper)
    if upper:
        frame = jnp.where(key < SLOTS, -1, frame)
    late = frame <= frame_of(rows // GROUP, core, upper)
    return (rows % GROUP == cols % GROUP) & late


def cat(parts):
    return jnp.concatenate(parts, axis=0)


def tiled(gain):
    return cat([gain] * SLOTS)


def group(wide, j):
    slots = wide.shape[0] // TOGETHER
    return cat([wide[s * TOGETHER + j * GROUP :][:GROUP] for s in range(slots)])


def ungroup(parts):
    return cat([part[s * GROUP :][:GROUP] for s in range(SLOTS) for part in parts])


def fold(acc, rows, part):
    total = part[:TOGETHER]
    for s in range(1, SLOTS):
        total = total + part[s * TOGETHER :][:TOGETHER]
    acc[rows, :] += total


def settle(outs, rows, parts):
    for t, part in enumerate(parts):
        for s, out in enumerate(outs):
            out[t, rows, :] = part[s * TOGETHER :][:TOGETHER]


def sum_heads(acc, heads):
    total = acc[0:heads, :]
    for i in range(1, acc.shape[0] // heads):
        total = total + acc[i * heads : (i + 1) * heads, :]
    return total


def read(refs, t, rows):
    return cat([ref[2 * x + t, rows, :] for ref in refs for x in range(2)])


def attend(qn, kn, grad, value, allowed):
    scaling = 1.0 / math.sqrt(qn.shape[-1])
    count = TOGETHER // GROUP
    scores = cat([mul_t(group(qn, j), group(kn, j)) for j in range(count)])
    prob_grad = cat([mul_t(group(grad, j), group(value, j)) for j in range(count)])
    mask = cat([allowed] * count)
    scores = jnp.where(mask > 0, scores * scaling, -jnp.inf)
    expo = jnp.exp(scores - jnp.max(scores, axis=-1, keepdims=True))
    prob = expo * (1.0 / jnp.sum(expo, axis=-1, keepdims=True))
    prob_low = prob.astype(BF16)
    dots = jnp.sum(prob_low.astype(F32) * prob_grad, axis=-1, keepdims=True)
    score_low = (prob * (prob_grad - dots)).astype(BF16)
    split = lambda x: [x[j * WIDE :][:WIDE] for j in range(count)]
    return split(prob_low), split(score_low)


def upper_kernel(first, steps, heads, own_a, edge_a, own_b, edge_b, other, far, gain_q, gain_k, *refs):
    outs, packed, (sum_q, sum_k, acc_q, acc_k, mask) = refs[:4], refs[4], refs[5:]
    chip, core = place()
    count = TOGETHER // GROUP
    acc_q[...] = jnp.zeros_like(acc_q)
    acc_k[...] = jnp.zeros_like(acc_k)
    cycle = acc_q.shape[0] // BLOCK

    def block(own_a, edge_a, own_b, edge_b, other, far, out_s, out_x, out_es, out_ex, pack_ref):
        base = ((first + pl.program_id(0)) % cycle) * BLOCK
        scaling = 1.0 / math.sqrt(128)
        lanes = iota((WIDE, 128), 1) // 8
        spread_r, spread_c = iota((2 * WIDE, 128), 0), iota((2 * WIDE, 128), 1)
        spread = jnp.where(spread_r // GROUP == spread_c % 8, 1.0, 0.0).astype(BF16)

        def some(i, total):
            rows = pl.ds(pl.multiple_of(i * TOGETHER, TOGETHER), TOGETHER)
            place = pl.ds(pl.multiple_of(base + i * TOGETHER, TOGETHER), TOGETHER)
            gq, gk = tiled(gain_q[place, :]), tiled(gain_k[place, :])
            q_hat, q_inv = rms(read((own_a, edge_a), 0, rows))
            grad = read((own_a, edge_a), 1, rows)
            kl_hat, _ = rms(read((other, far), 0, rows))
            ku_hat, ku_inv = rms(read((own_b, edge_b), 0, rows))
            value = cat([read((other, far), 1, rows), read((own_b, edge_b), 1, rows)])
            qn = (q_hat * gq).astype(BF16)
            kn = cat([(kl_hat * gk).astype(BF16), (ku_hat * gk).astype(BF16)])
            prob, score = attend(qn, kn, grad, value, mask[...])
            q_step = ungroup([mul(score[j], group(kn, j)) for j in range(count)])
            k_step = ungroup([t_mul(score[j][:, WIDE:], group(qn, j)) for j in range(count)])
            v_step = ungroup([t_mul(prob[j][:, WIDE:], group(grad, j)) for j in range(count)])
            q_step, k_step = (q_step * scaling).astype(BF16), (k_step * scaling).astype(BF16)
            dq, part_q = norm_back(q_step, q_hat, q_inv, gq)
            dk, part_k = norm_back(k_step, ku_hat, ku_inv, gk)
            settle((out_s, out_x, out_es, out_ex), rows, (dq, dk, v_step.astype(BF16)))
            fold(acc_q, place, part_q)
            fold(acc_k, place, part_k)
            for j in range(count):
                cross = jnp.concatenate([prob[j][:, :WIDE], score[j][:, :WIDE]], axis=1)
                total = jnp.where(lanes == i * count + j, mul(cross, spread), total)
            return total

        total = lax.fori_loop(0, BLOCK // TOGETHER, some, jnp.zeros((WIDE, 128), F32))
        pack_ref[0] = total.astype(BF16)

    @pl.when(chip == 2)
    def _():
        mask[...] = causal(core, True).astype(F32)
        pltpu.emit_pipeline(
            block,
            grid=(steps,),
            in_specs=[pl.BlockSpec((4, BLOCK, 128), lambda i: (0, i, 0))] * 6,
            out_specs=[pl.BlockSpec((3, BLOCK, 128), lambda i: (0, i, 0))] * 4
            + [pl.BlockSpec((1, WIDE, 128), lambda i: (i, 0, 0))],
        )(own_a, edge_a, own_b, edge_b, other, far, *outs, packed)

    sum_q[...] = sum_heads(acc_q, heads)
    sum_k[...] = sum_heads(acc_k, heads)


def lower_kernel(first, steps, heads, own_a, edge_a, own_b, edge_b, other, far, packed, gain_q, gain_k, *refs):
    outs, (sum_q, sum_k, acc_q, acc_k, mask) = refs[4:8], refs[8:]
    chip, core = place()
    count = TOGETHER // GROUP
    acc_q[...] = jnp.zeros_like(acc_q)
    acc_k[...] = jnp.zeros_like(acc_k)
    cycle = acc_q.shape[0] // BLOCK

    def block(own_a, edge_a, own_b, edge_b, other, far, pack_ref, out_s, out_x, out_es, out_ex):
        base = ((first + pl.program_id(0)) % cycle) * BLOCK
        both = iota((WIDE, 2 * WIDE), 0) % GROUP == iota((WIDE, 2 * WIDE), 1) % GROUP
        scaling = 1.0 / math.sqrt(128)
        lanes = iota((WIDE, 128), 1) // 8
        spread_r, spread_c = iota((128, 2 * WIDE), 0), iota((128, 2 * WIDE), 1)
        spread = jnp.where(spread_c // GROUP == spread_r % 8, 1.0, 0.0).astype(BF16)
        crossed = pack_ref[0].astype(F32)

        def some(i, carry):
            rows = pl.ds(pl.multiple_of(i * TOGETHER, TOGETHER), TOGETHER)
            place = pl.ds(pl.multiple_of(base + i * TOGETHER, TOGETHER), TOGETHER)
            gq, gk = tiled(gain_q[place, :]), tiled(gain_k[place, :])
            k_hat, k_inv = rms(read((own_a, edge_a), 0, rows))
            value = read((own_a, edge_a), 1, rows)
            q_hat, q_inv = rms(read((own_b, edge_b), 0, rows))
            grad = read((own_b, edge_b), 1, rows)
            qu_hat, _ = rms(read((other, far), 0, rows))
            grad_u = read((other, far), 1, rows)
            kn = (k_hat * gk).astype(BF16)
            qn = (q_hat * gq).astype(BF16)
            qn_u = (qu_hat * gq).astype(BF16)
            prob, score = attend(qn, kn, grad, value, mask[...])
            cross = []
            for j in range(count):
                mine = jnp.where(lanes == i * count + j, crossed, 0.0).astype(BF16)
                cross.append(jnp.where(both, mul(mine, spread), 0.0).astype(BF16))
            q_step = ungroup([mul(score[j], group(kn, j)) for j in range(count)])
            k_step = ungroup(
                [
                    t_mul(cat([score[j], cross[j][:, WIDE:]]), cat([group(qn, j), group(qn_u, j)]))
                    for j in range(count)
                ]
            )
            v_step = ungroup(
                [
                    t_mul(cat([prob[j], cross[j][:, :WIDE]]), cat([group(grad, j), group(grad_u, j)]))
                    for j in range(count)
                ]
            )
            q_step, k_step = (q_step * scaling).astype(BF16), (k_step * scaling).astype(BF16)
            dq, part_q = norm_back(q_step, q_hat, q_inv, gq)
            dk, part_k = norm_back(k_step, k_hat, k_inv, gk)
            settle((out_s, out_x, out_es, out_ex), rows, (dq, dk, v_step.astype(BF16)))
            fold(acc_q, place, part_q)
            fold(acc_k, place, part_k)
            return carry

        lax.fori_loop(0, BLOCK // TOGETHER, some, 0)

    @pl.when(chip == 1)
    def _():
        mask[...] = causal(core, False).astype(F32)
        pltpu.emit_pipeline(
            block,
            grid=(steps,),
            in_specs=[pl.BlockSpec((4, BLOCK, 128), lambda i: (0, i, 0))] * 6
            + [pl.BlockSpec((1, WIDE, 128), lambda i: (i, 0, 0))],
            out_specs=[pl.BlockSpec((3, BLOCK, 128), lambda i: (0, i, 0))] * 4,
        )(own_a, edge_a, own_b, edge_b, other, far, packed, *outs)

    sum_q[...] = sum_heads(acc_q, heads)
    sum_k[...] = sum_heads(acc_k, heads)


def hub_cost(rows):
    return pl.CostEstimate(
        flops=rows * 60000, bytes_accessed=rows * 128 * 2 * 36, transcendentals=rows * 600
    )


def out_rows(slot):
    return max(CUTS[max(slot - 1, 0) : slot + 1]) * BLOCK


def upper(slot, heads, data, gains, after):
    steps = CUTS[slot]
    cycle = gains[0].shape[0]
    return call(
        functools.partial(upper_kernel, sum(CUTS[:slot]), steps, heads),
        (*data, *gains),
        [ANY] * 6 + [VMEM] * 2,
        after,
        out_shape=[jax.ShapeDtypeStruct((3, out_rows(slot), 128), BF16)] * 4
        + [jax.ShapeDtypeStruct((steps, WIDE, 128), BF16)]
        + [jax.ShapeDtypeStruct((heads, 128), F32)] * 2,
        out_specs=[ANY] * 5 + [VMEM] * 2,
        scratch_shapes=[pltpu.VMEM((cycle, 128), F32)] * 2 + [pltpu.VMEM((WIDE, 2 * WIDE), F32)],
        cost_estimate=hub_cost(steps * BLOCK),
        name="upper_frames",
    )


def lower(slot, heads, data, packed, gains, outs, after):
    chunk = slot - 1
    steps = CUTS[chunk]
    cycle = gains[0].shape[0]
    return call(
        functools.partial(lower_kernel, sum(CUTS[:chunk]), steps, heads),
        (*data, packed, *gains, *outs),
        [ANY] * 7 + [VMEM] * 2 + [ANY] * 4,
        after,
        out_shape=[jax.ShapeDtypeStruct((3, out_rows(slot), 128), BF16)] * 4
        + [jax.ShapeDtypeStruct((heads, 128), F32)] * 2,
        out_specs=[ANY] * 4 + [VMEM] * 2,
        scratch_shapes=[pltpu.VMEM((cycle, 128), F32)] * 2 + [pltpu.VMEM((WIDE, WIDE), F32)],
        input_output_aliases={9 + i: i for i in range(4)},
        cost_estimate=hub_cost(steps * BLOCK),
        name="lower_frames",
    )


def blank(slot, after):
    def kernel(*refs):
        pass

    return call(
        kernel,
        (),
        [],
        after,
        out_shape=[jax.ShapeDtypeStruct((3, out_rows(slot), 128), BF16)] * 4,
        out_specs=[ANY] * 4,
        name="blank_rows",
    )


def send(array, pairs):
    return lax.ppermute(array, "seq", pairs)


def sum_gains(part):
    count = lax.axis_size("dp")
    mine = part.shape[1] // count
    index = lax.axis_index("dp")

    def heads_of(who):
        return lax.dynamic_slice_in_dim(part, who % count * mine, mine, 1)

    total = heads_of(index)
    for shift in range(1, count):
        pairs = [(i, (i + shift) % count) for i in range(count)]
        total = total + lax.ppermute(heads_of(index + shift), "dp", pairs)
    total = total + send(total, SWAP)
    total = total + send(total, MIDDLE)
    edge = send(total, BACK_S)
    chip, _ = place()
    return jnp.where((chip == 1) | (chip == 2), total, edge)


def hub_body(queries, key_proj, value_proj, out_grad, query_gain, key_gain):
    shape = queries.shape
    heads, width = shape[-2:]
    half = shape[2] // 2 * heads
    arrays = [x.reshape(2, half, width) for x in (queries, key_proj, value_proj, out_grad)]
    cycle = math.lcm(BLOCK, heads)
    chunks = len(CUTS)

    near = halves(0, CUTS[0], arrays, ())
    rest = halves(CUTS[0], sum(CUTS[1:]), arrays, (near,))
    near, rest = send(near, SWAP), send(rest, SWAP)

    both = lax.all_gather(jnp.stack([query_gain, key_gain]), "dp", axis=1, tiled=True)
    gains = [jnp.tile(both[t], (cycle // heads, 1)) for t in range(2)]

    landed, grads, packed, outs = {}, {}, {}, {-1: None}
    sums = []

    def bring(chunk):
        after = []
        if chunk >= 2:
            after.append(landed[chunk - 2][1])
        if chunk >= 3:
            after.append(grads[chunk - 3][0])
        swapped, offset = (near, 0) if chunk == 0 else (rest, CUTS[0])
        own_a, own_b = pack(sum(CUTS[:chunk]), CUTS[chunk], offset, arrays, swapped, after)
        edge_a = send(own_a, EDGE)
        other_a = send(own_a, MIDDLE)
        edge_b = send(own_b, EDGE)
        far_a = send(edge_a, MIDDLE)
        landed[chunk] = (own_a, edge_a, own_b, edge_b, other_a, far_a)

    def work(slot):
        after = list(outs[slot - 2][:1]) if slot >= 2 else []
        if slot < chunks:
            *parts, cross, sum_q, sum_k = upper(slot, heads, landed[slot], gains, after)
            packed[slot] = send(cross, DOWN)
            sums.append((sum_q, sum_k))
        else:
            parts = blank(slot, after)
        if slot > 0:
            *parts, sum_q, sum_k = lower(
                slot, heads, landed[slot - 1], packed[slot - 1], gains, parts, after
            )
            sums.append((sum_q, sum_k))
        grads[slot] = parts
        own, cross, edge_s, edge_x = parts
        pieces = (own, send(cross, SWAP), send(edge_s, BACK_S), send(edge_x, BACK_X))
        outs[slot] = unpack(slot, half, pieces, outs[slot - 1])

    for chunk in range(min(3, chunks)):
        bring(chunk)
    for slot in range(chunks + 1):
        work(slot)
        if slot + 3 < chunks:
            bring(slot + 3)

    totals = jnp.stack([functools.reduce(jnp.add, [s[t] for s in sums]) for t in range(2)])
    totals = sum_gains(totals)
    return (*[x.reshape(shape) for x in outs[chunks]], totals[0], totals[1])


def wide_attention(query_norm, key_norm, value_in, grad_in):
    frames = query_norm.shape[1]
    scaling = 1.0 / math.sqrt(query_norm.shape[-1])
    scores = (
        jnp.einsum("efphd,egphd->ephfg", query_norm, key_norm, preferred_element_type=F32) * scaling
    )
    allowed = iota((frames, frames), 1) <= iota((frames, frames), 0)
    scores = jnp.where(allowed, scores, -jnp.inf)
    expo = jnp.exp(scores - jnp.max(scores, axis=-1, keepdims=True))
    probability = expo / jnp.sum(expo, axis=-1, keepdims=True)
    prob_low = probability.astype(BF16)
    attn_out = jnp.einsum("ephfg,egphd->efphd", prob_low, value_in, preferred_element_type=F32)
    row_dots = jnp.transpose(jnp.sum(grad_in.astype(F32) * attn_out, axis=-1), (0, 2, 3, 1))
    prob_grad = jnp.einsum("efphd,egphd->ephfg", grad_in, value_in, preferred_element_type=F32)
    score_low = (probability * (prob_grad - row_dots[..., None])).astype(BF16)
    query_step = jnp.einsum("ephfg,egphd->efphd", score_low, key_norm, preferred_element_type=F32)
    key_step = jnp.einsum("ephfg,efphd->egphd", score_low, query_norm, preferred_element_type=F32)
    value_step = jnp.einsum("ephfg,efphd->egphd", prob_low, grad_in, preferred_element_type=F32)
    return (
        (query_step * scaling).astype(BF16),
        (key_step * scaling).astype(BF16),
        value_step.astype(BF16),
    )


def wide_body(queries, key_proj, value_proj, out_grad, query_gain, key_gain):
    gain_q = lax.all_gather(query_gain, "dp", axis=0, tiled=True)
    gain_k = lax.all_gather(key_gain, "dp", axis=0, tiled=True)
    q_hat, q_inv = rms(queries)
    k_hat, k_inv = rms(key_proj)
    pieces = [
        lax.all_to_all(x, "seq", split_axis=2, concat_axis=1, tiled=True)
        for x in ((q_hat * gain_q).astype(BF16), (k_hat * gain_k).astype(BF16), value_proj, out_grad)
    ]
    steps = [
        lax.all_to_all(x, "seq", split_axis=1, concat_axis=2, tiled=True)
        for x in wide_attention(*pieces)
    ]
    query_grad, part_q = norm_back(steps[0], q_hat, q_inv, gain_q)
    key_grad, part_k = norm_back(steps[1], k_hat, k_inv, gain_k)
    axes = tuple(range(part_q.ndim - 2))
    totals = lax.psum((jnp.sum(part_q, axis=axes), jnp.sum(part_k, axis=axes)), "seq")
    totals = [lax.psum_scatter(t, "dp", scatter_dimension=0, tiled=True) for t in totals]
    return (query_grad, key_grad, steps[2], *totals)


def body(*args):
    frames = lax.axis_size("seq")
    patches, heads, width = args[0].shape[2:]
    rows = patches // 2 * heads
    if frames == 8 and args[0].shape[:2] == (1, 1) and width == 128 and rows == sum(CUTS) * BLOCK:
        return hub_body(*args)
    return wide_body(*args)


def solution(mesh):
    whole = P("dp", "seq", None, None, None)
    gain = P("dp", None)
    return jax.shard_map(
        body,
        mesh=mesh,
        in_specs=(whole,) * 4 + (gain,) * 2,
        out_specs=(whole,) * 3 + (gain,) * 2,
        check_vma=False,
    )
```

```python
import functools
import math

import jax
import jax.numpy as jnp
from jax import lax
from jax.experimental import pallas as pl
from jax.experimental.pallas import tpu as pltpu
from jax.sharding import PartitionSpec as P

EPSILON = 1e-06
BLOCK = 256
GROUP = 16
SLOTS = 4
WIDE = GROUP * SLOTS
TOGETHER = 64
CUTS = (2, 4, 5, 5, 3, 1)

EDGE = ((0, 2), (1, 3), (6, 4), (7, 5))
MIDDLE = ((2, 4), (3, 5), (4, 2), (5, 3))
DOWN = ((4, 2), (5, 3))
BACK_S = ((2, 0), (3, 1), (4, 6), (5, 7))
BACK_X = ((2, 1), (3, 0), (4, 7), (5, 6))
SWAP = tuple((i, i ^ 1) for i in range(8))

F32 = jnp.float32
BF16 = jnp.bfloat16
ANY = pl.BlockSpec(memory_space=pl.ANY)
VMEM = pl.BlockSpec(memory_space=pltpu.VMEM)


def place():
    index = lax.axis_index("seq")
    chip, core = index // 2, index % 2
    return chip, core


def call(kernel, inputs, in_specs, after=(), **kwargs):
    count, extra = len(inputs), len(after)

    def trimmed(*refs):
        kernel(*refs[:count], *refs[count + extra :])

    return pl.pallas_call(
        trimmed,
        in_specs=list(in_specs) + [ANY] * extra,
        compiler_params=pltpu.CompilerParams(vmem_limit_bytes=56 * 1024 * 1024),
        **kwargs,
    )(*inputs, *after)


def first_of(chunk):
    return sum(CUTS[:chunk]) * BLOCK


def rows_of(chunk):
    return CUTS[chunk] * BLOCK


def out_rows(slot):
    return max(CUTS[max(slot - 1, 0) : slot + 1]) * BLOCK


def copy_cost(rows, tensors):
    return pl.CostEstimate(flops=0, bytes_accessed=rows * 128 * 2 * 2 * tensors, transcendentals=0)


def tile_of(rows):
    return next(rows // k for k in range(2, rows) if rows % (16 * k) == 0 and rows // k <= 1024)


def stream(rows, sources, sinks, move):
    tile = tile_of(rows)

    def spec(ref):
        return pl.BlockSpec((ref.shape[0], tile, 128), lambda i: (0, i, 0))

    pltpu.emit_pipeline(
        move,
        grid=(rows // tile,),
        in_specs=[spec(ref) for ref in sources],
        out_specs=[spec(ref) for ref in sinks],
    )(*sources, *sinks)


def window(ref, index, start, rows, count=1):
    return ref.at[pl.ds(index, count), pl.ds(start, rows)]


def halves_kernel(start, rows, q, k, v, g, out):
    _, core = place()

    def move(*blocks):
        for t in range(4):
            blocks[4][t] = blocks[t][0]

    stream(rows, [window(ref, 1 - core, start, rows) for ref in (q, k, v, g)], [out], move)


def halves(start, rows, arrays, after):
    return call(
        functools.partial(halves_kernel, start, rows),
        arrays,
        [ANY] * 4,
        after,
        out_shape=jax.ShapeDtypeStruct((4, rows, 128), BF16),
        out_specs=ANY,
        cost_estimate=copy_cost(rows, 4),
        name="other_half",
    )


def pack_kernel(start, rows, offset, q, k, v, g, x, edge, middle):
    chip, core = place()

    def run(order):
        def move(*blocks):
            sent, crossing = blocks[8:]
            for pair in range(2):
                for t in range(2):
                    for frame in range(2):
                        value = blocks[4 * frame + 2 * pair + t][0]
                        sent[4 * pair + 2 * frame + t] = value
                        if pair == 0:
                            crossing[2 * frame + t] = value

        own = [window((q, k, v, g)[t], core, start, rows) for t in order]
        other = [window(x, t, start - offset, rows) for t in order]
        stream(rows, own + other, [edge, middle], move)

    @pl.when(chip < 2)
    def _():
        run((1, 2, 0, 3))

    @pl.when(chip >= 2)
    def _():
        run((0, 3, 1, 2))


def pack(chunk, offset, arrays, swapped, after):
    rows = rows_of(chunk)
    return call(
        functools.partial(pack_kernel, first_of(chunk), rows, offset),
        (*arrays, swapped),
        [ANY] * 5,
        after,
        out_shape=[jax.ShapeDtypeStruct((n, rows, 128), BF16) for n in (8, 4)],
        out_specs=[ANY] * 2,
        cost_estimate=copy_cost(rows, 10),
        name="pack_rows",
    )


def forward_kernel(rows, extra, edge, *refs):
    packed, out = refs[:-1], refs[-1]
    chip, _ = place()

    def move(src, dst):
        dst[...] = src[...]

    def move_packed(src, dst):
        dst[...] = src[...]

    @pl.when((chip == 1) | (chip == 2))
    def _():
        tile = tile_of(rows)
        pltpu.emit_pipeline(
            lambda src, dst: move(src.at[0], dst),
            grid=(4, rows // tile),
            in_specs=[pl.BlockSpec((1, tile, 128), lambda q, i: (q, i, 0))],
            out_specs=[pl.BlockSpec((tile, 128), lambda q, i: (q * (rows // tile) + i, 0))],
        )(edge, out.at[pl.ds(0, 4 * rows)])
        for ref in packed:
            pltpu.emit_pipeline(
                move_packed,
                grid=(1,),
                in_specs=[pl.BlockSpec((extra, 128), lambda i: (0, 0))],
                out_specs=[pl.BlockSpec((extra, 128), lambda i: (0, 0))],
            )(ref, out.at[pl.ds(4 * rows, extra)])


def forward(chunk, edge, packed, after):
    rows = rows_of(chunk)
    extra = 0 if packed is None else packed.shape[0]
    inputs = (edge,) if packed is None else (edge, packed)
    return call(
        functools.partial(forward_kernel, rows, extra),
        inputs,
        [ANY] * len(inputs),
        after,
        out_shape=jax.ShapeDtypeStruct((4 * rows + extra, 128), BF16),
        out_specs=ANY,
        cost_estimate=copy_cost(rows, 4),
        name="forward_rows",
    )


def copy_three(src, *dsts):
    for t, dst in enumerate(dsts):
        dst[0] = src[t]


def copy_all(src, dst):
    dst[...] = src[...]


def by_chip(slot, run):
    chip, _ = place()
    for which in range(4):
        chunk = slot if which >= 2 else slot - 1
        if 0 <= chunk < len(CUTS):
            pl.when(chip == which)(functools.partial(run, chunk, which in (1, 2)))


def place_kernel(slot, own, other, back, *refs):
    outs, late = refs[-4:-1], refs[-1]
    _, core = place()

    def run(chunk, hub):
        start, rows = first_of(chunk), rows_of(chunk)
        near = own.at[:, pl.ds(0, rows)] if hub else window(back, 0, 0, rows, 3)
        far = other.at[:, pl.ds(0, rows)] if hub else window(back, 3, 0, rows, 3)
        stream(rows, [near], [window(out, core, start, rows) for out in outs], copy_three)
        stream(rows, [far], [window(late, 0, start, rows, 3)], copy_all)

    by_chip(slot, run)


def place_last_kernel(slot, own, other, back_s, back_x, *refs):
    outs = refs[-3:]
    _, core = place()

    def run(chunk, hub):
        start, rows = first_of(chunk), rows_of(chunk)
        for half, src in ((core, own if hub else back_s), (1 - core, other if hub else back_x)):
            sinks = [window(out, half, start, rows) for out in outs]
            stream(rows, [src.at[:, pl.ds(0, rows)]], sinks, copy_three)

    by_chip(slot, run)


def place_late_kernel(slot, late, *refs):
    outs = refs[-3:]
    chip, core = place()

    def run(rows):
        sinks = [window(out, 1 - core, 0, rows) for out in outs]
        stream(rows, [window(late, 0, 0, rows, 3)], sinks, copy_three)

    @pl.when(chip < 2)
    def _():
        run(first_of(slot))

    @pl.when(chip >= 2)
    def _():
        run(first_of(slot + 1))


def settle_rows(kernel, half, pieces, kept, count, rows, after=()):
    kept = kept or ()
    return call(
        kernel,
        (*pieces, *kept),
        [ANY] * (len(pieces) + len(kept)),
        after,
        out_shape=[jax.ShapeDtypeStruct((n, half, 128), BF16) for n in (2, 2, 2, 3)[:count]],
        out_specs=[ANY] * count,
        input_output_aliases={len(pieces) + i: i for i in range(len(kept))},
        cost_estimate=copy_cost(rows, 6),
        name="place_rows",
    )


def rms(values):
    wide = values.astype(F32)
    inverse = lax.rsqrt(jnp.mean(wide * wide, axis=-1, keepdims=True) + EPSILON)
    return wide * inverse, inverse


def norm_back(step, hat, inverse, gain):
    wide = step.astype(F32)
    gained = gain * wide
    result = inverse * (gained - hat * jnp.mean(gained * hat, axis=-1, keepdims=True))
    return result.astype(BF16), wide * hat


def mul_t(a, b):
    return lax.dot_general(a, b, (((1,), (1,)), ((), ())), preferred_element_type=F32)


def t_mul(a, b):
    return lax.dot_general(a, b, (((0,), (0,)), ((), ())), preferred_element_type=F32)


def mul(a, b):
    return jnp.dot(a, b, preferred_element_type=F32)


def iota(shape, axis):
    return lax.broadcasted_iota(jnp.int32, shape, axis)


def frame_of(slot, core, upper):
    cross = slot % 2
    side = slot // 2
    side = side if upper else 1 - side
    return 2 * side + cross + core - 2 * cross * core


def causal(core, upper):
    shape = (WIDE, 2 * WIDE if upper else WIDE)
    rows, cols = iota(shape, 0), iota(shape, 1)
    key = cols // GROUP
    frame = frame_of(key % SLOTS, core, upper)
    if upper:
        frame = jnp.where(key < SLOTS, -1, frame)
    late = frame <= frame_of(rows // GROUP, core, upper)
    return (rows % GROUP == cols % GROUP) & late


def cat(parts):
    return jnp.concatenate(parts, axis=0)


def tiled(gain):
    return cat([gain] * SLOTS)


def group(wide, j):
    slots = wide.shape[0] // TOGETHER
    return cat([wide[s * TOGETHER + j * GROUP :][:GROUP] for s in range(slots)])


def ungroup(parts):
    return cat([part[s * GROUP :][:GROUP] for s in range(SLOTS) for part in parts])


def fold(acc, rows, part):
    total = part[:TOGETHER]
    for s in range(1, SLOTS):
        total = total + part[s * TOGETHER :][:TOGETHER]
    acc[rows, :] += total


def settle(outs, rows, parts):
    for t, part in enumerate(parts):
        for s, out in enumerate(outs):
            out[t, rows, :] = part[s * TOGETHER :][:TOGETHER]


def sum_heads(acc, heads):
    total = acc[0:heads, :]
    for i in range(1, acc.shape[0] // heads):
        total = total + acc[i * heads : (i + 1) * heads, :]
    return total


def read(refs, t, rows):
    return cat([ref[2 * x + t, rows, :] for ref in refs for x in range(2)])


def read_met(near, far, t, rows):
    return cat([near[2 * x + t, rows, :] for x in range(2)] + [far[2 * x + t][rows, :] for x in range(2)])


def hub_specs(steps):
    four = lambda n: pl.BlockSpec((4, BLOCK, 128), lambda i: (n, i, 0))
    flat = lambda q: pl.BlockSpec((BLOCK, 128), lambda i: (q * steps + i, 0))
    return [four(0), four(1), four(0), four(1), four(0)] + [flat(q) for q in range(4)]


def hub_refs(steps, own, edge, other, far):
    return [own, own, edge, edge, other] + [far.at[pl.ds(0, 4 * steps * BLOCK)]] * 4


def grad_specs():
    return [pl.BlockSpec((3, BLOCK, 128), lambda i: (0, i, 0))] * 4


def grad_refs(outs):
    if len(outs) == 4:
        return list(outs)
    return [outs[0], outs[1], outs[2].at[pl.ds(0, 3)], outs[2].at[pl.ds(3, 3)]]


def gain_spec(first, cycle):
    return pl.BlockSpec((BLOCK, 128), lambda i: ((first + i) % cycle, 0))


def attend(qn, kn, grad, value, allowed):
    scaling = 1.0 / math.sqrt(qn.shape[-1])
    count = TOGETHER // GROUP
    scores = cat([mul_t(group(qn, j), group(kn, j)) for j in range(count)])
    prob_grad = cat([mul_t(group(grad, j), group(value, j)) for j in range(count)])
    mask = cat([allowed] * count)
    scores = jnp.where(mask > 0, scores * scaling, -jnp.inf)
    expo = jnp.exp(scores - jnp.max(scores, axis=-1, keepdims=True))
    prob = expo * (1.0 / jnp.sum(expo, axis=-1, keepdims=True))
    prob_low = prob.astype(BF16)
    dots = jnp.sum(prob_low.astype(F32) * prob_grad, axis=-1, keepdims=True)
    score_low = (prob * (prob_grad - dots)).astype(BF16)
    split = lambda x: [x[j * WIDE :][:WIDE] for j in range(count)]
    return split(prob_low), split(score_low)


def upper_kernel(chunk, heads, own, edge, other, far, gain_q, gain_k, *refs):
    outs, (packed, sum_q, sum_k, acc_q, acc_k, mask) = refs[:-6], refs[-6:]
    chip, core = place()
    first, steps = sum(CUTS[:chunk]), CUTS[chunk]
    count = TOGETHER // GROUP
    cycle = acc_q.shape[0] // BLOCK

    def block(own_a, own_b, edge_a, edge_b, other, f0, f1, f2, f3, gain_q, gain_k, *results):
        out, pack_ref = results[:4], results[4]
        far = (f0, f1, f2, f3)
        base = ((first + pl.program_id(0)) % cycle) * BLOCK
        scaling = 1.0 / math.sqrt(128)
        lanes = iota((WIDE, 128), 1) // 8
        spread_r, spread_c = iota((2 * WIDE, 128), 0), iota((2 * WIDE, 128), 1)
        spread = jnp.where(spread_r // GROUP == spread_c % 8, 1.0, 0.0).astype(BF16)

        def some(i, total):
            rows = pl.ds(pl.multiple_of(i * TOGETHER, TOGETHER), TOGETHER)
            place = pl.ds(pl.multiple_of(base + i * TOGETHER, TOGETHER), TOGETHER)
            gq, gk = tiled(gain_q[rows, :]), tiled(gain_k[rows, :])
            q_hat, q_inv = rms(read((own_a, edge_a), 0, rows))
            grad = read((own_a, edge_a), 1, rows)
            kl_hat, _ = rms(read_met(other, far, 0, rows))
            ku_hat, ku_inv = rms(read((own_b, edge_b), 0, rows))
            value = cat([read_met(other, far, 1, rows), read((own_b, edge_b), 1, rows)])
            qn = (q_hat * gq).astype(BF16)
            kn = cat([(kl_hat * gk).astype(BF16), (ku_hat * gk).astype(BF16)])
            prob, score = attend(qn, kn, grad, value, mask[...])
            q_step = ungroup([mul(score[j], group(kn, j)) for j in range(count)])
            k_step = ungroup([t_mul(score[j][:, WIDE:], group(qn, j)) for j in range(count)])
            v_step = ungroup([t_mul(prob[j][:, WIDE:], group(grad, j)) for j in range(count)])
            q_step, k_step = (q_step * scaling).astype(BF16), (k_step * scaling).astype(BF16)
            dq, part_q = norm_back(q_step, q_hat, q_inv, gq)
            dk, part_k = norm_back(k_step, ku_hat, ku_inv, gk)
            settle(out, rows, (dq, dk, v_step.astype(BF16)))
            fold(acc_q, place, part_q)
            fold(acc_k, place, part_k)
            for j in range(count):
                cross = jnp.concatenate([prob[j][:, :WIDE], score[j][:, :WIDE]], axis=1)
                total = jnp.where(lanes == i * count + j, mul(cross, spread), total)
            return total

        total = lax.fori_loop(0, BLOCK // TOGETHER, some, jnp.zeros((WIDE, 128), F32))
        pack_ref[...] = total.astype(BF16)

    @pl.when(chip == 2)
    def _():
        acc_q[...] = jnp.zeros_like(acc_q)
        acc_k[...] = jnp.zeros_like(acc_k)
        mask[...] = causal(core, True).astype(F32)
        pltpu.emit_pipeline(
            block,
            grid=(steps,),
            in_specs=hub_specs(steps) + [gain_spec(first, cycle)] * 2,
            out_specs=grad_specs() + [pl.BlockSpec((WIDE, 128), lambda i: (i, 0))],
        )(*hub_refs(steps, own, edge, other, far), gain_q, gain_k, *grad_refs(outs), packed)
        sum_q[...] = sum_heads(acc_q, heads)
        sum_k[...] = sum_heads(acc_k, heads)

    @pl.when(chip != 2)
    def _():
        sum_q[...] = jnp.zeros_like(sum_q)
        sum_k[...] = jnp.zeros_like(sum_k)


def lower_kernel(chunk, skip, heads, own, edge, other, far, packed, gain_q, gain_k, *refs):
    outs, (sum_q, sum_k, acc_q, acc_k, mask) = refs[:-5], refs[-5:]
    outs = outs[len(outs) // 2 :]
    chip, core = place()
    first, steps = sum(CUTS[:chunk]), CUTS[chunk]
    count = TOGETHER // GROUP
    cycle = acc_q.shape[0] // BLOCK

    def block(own_a, own_b, edge_a, edge_b, other, f0, f1, f2, f3, gain_q, gain_k, pack_ref, *out):
        far = (f0, f1, f2, f3)
        base = ((first + pl.program_id(0)) % cycle) * BLOCK
        both = iota((WIDE, 2 * WIDE), 0) % GROUP == iota((WIDE, 2 * WIDE), 1) % GROUP
        scaling = 1.0 / math.sqrt(128)
        lanes = iota((WIDE, 128), 1) // 8
        spread_r, spread_c = iota((128, 2 * WIDE), 0), iota((128, 2 * WIDE), 1)
        spread = jnp.where(spread_c // GROUP == spread_r % 8, 1.0, 0.0).astype(BF16)
        crossed = pack_ref[...].astype(F32)

        def some(i, carry):
            rows = pl.ds(pl.multiple_of(i * TOGETHER, TOGETHER), TOGETHER)
            place = pl.ds(pl.multiple_of(base + i * TOGETHER, TOGETHER), TOGETHER)
            gq, gk = tiled(gain_q[rows, :]), tiled(gain_k[rows, :])
            k_hat, k_inv = rms(read((own_a, edge_a), 0, rows))
            value = read((own_a, edge_a), 1, rows)
            q_hat, q_inv = rms(read((own_b, edge_b), 0, rows))
            grad = read((own_b, edge_b), 1, rows)
            qu_hat, _ = rms(read_met(other, far, 0, rows))
            grad_u = read_met(other, far, 1, rows)
            kn = (k_hat * gk).astype(BF16)
            qn = (q_hat * gq).astype(BF16)
            qn_u = (qu_hat * gq).astype(BF16)
            prob, score = attend(qn, kn, grad, value, mask[...])
            cross = []
            for j in range(count):
                mine = jnp.where(lanes == i * count + j, crossed, 0.0).astype(BF16)
                cross.append(jnp.where(both, mul(mine, spread), 0.0).astype(BF16))
            q_step = ungroup([mul(score[j], group(kn, j)) for j in range(count)])
            k_step = ungroup(
                [
                    t_mul(cat([score[j], cross[j][:, WIDE:]]), cat([group(qn, j), group(qn_u, j)]))
                    for j in range(count)
                ]
            )
            v_step = ungroup(
                [
                    t_mul(cat([prob[j], cross[j][:, :WIDE]]), cat([group(grad, j), group(grad_u, j)]))
                    for j in range(count)
                ]
            )
            q_step, k_step = (q_step * scaling).astype(BF16), (k_step * scaling).astype(BF16)
            dq, part_q = norm_back(q_step, q_hat, q_inv, gq)
            dk, part_k = norm_back(k_step, k_hat, k_inv, gk)
            settle(out, rows, (dq, dk, v_step.astype(BF16)))
            fold(acc_q, place, part_q)
            fold(acc_k, place, part_k)
            return carry

        lax.fori_loop(0, BLOCK // TOGETHER, some, 0)

    @pl.when(chip == 1)
    def _():
        acc_q[...] = jnp.zeros_like(acc_q)
        acc_k[...] = jnp.zeros_like(acc_k)
        mask[...] = causal(core, False).astype(F32)
        pltpu.emit_pipeline(
            block,
            grid=(steps,),
            in_specs=hub_specs(steps)
            + [gain_spec(first, cycle)] * 2
            + [pl.BlockSpec((WIDE, 128), lambda i: (i, 0))],
            out_specs=grad_specs(),
        )(
            *hub_refs(steps, own, edge, other, far),
            gain_q,
            gain_k,
            packed.at[pl.ds(skip, steps * WIDE)],
            *grad_refs(outs),
        )
        sum_q[...] = sum_heads(acc_q, heads)
        sum_k[...] = sum_heads(acc_k, heads)

    @pl.when(chip != 1)
    def _():
        sum_q[...] = jnp.zeros_like(sum_q)
        sum_k[...] = jnp.zeros_like(sum_k)


def hub_cost(rows):
    return pl.CostEstimate(
        flops=rows * 60000, bytes_accessed=rows * 128 * 2 * 36, transcendentals=rows * 600
    )


def grad_shapes(slot):
    sizes = (3, 3, 6) if slot < len(CUTS) - 1 else (3, 3, 3, 3)
    return [jax.ShapeDtypeStruct((n, out_rows(slot), 128), BF16) for n in sizes]


def upper(slot, heads, data, gains, after):
    steps = CUTS[slot]
    cycle = gains[0].shape[0]
    shapes = grad_shapes(slot)
    return call(
        functools.partial(upper_kernel, slot, heads),
        (*data, *gains),
        [ANY] * 6,
        after,
        out_shape=shapes
        + [jax.ShapeDtypeStruct((steps * WIDE, 128), BF16)]
        + [jax.ShapeDtypeStruct((heads, 128), F32)] * 2,
        out_specs=[ANY] * (len(shapes) + 1) + [VMEM] * 2,
        scratch_shapes=[pltpu.VMEM((cycle, 128), F32)] * 2 + [pltpu.VMEM((WIDE, 2 * WIDE), F32)],
        cost_estimate=hub_cost(steps * BLOCK),
        name="upper_frames",
    )


def lower(slot, heads, data, packed, skip, gains, outs, after):
    chunk = slot - 1
    cycle = gains[0].shape[0]
    shapes = grad_shapes(slot)
    return call(
        functools.partial(lower_kernel, chunk, skip, heads),
        (*data, packed, *gains, *outs),
        [ANY] * (7 + len(outs)),
        after,
        out_shape=shapes + [jax.ShapeDtypeStruct((heads, 128), F32)] * 2,
        out_specs=[ANY] * len(shapes) + [VMEM] * 2,
        scratch_shapes=[pltpu.VMEM((cycle, 128), F32)] * 2 + [pltpu.VMEM((WIDE, WIDE), F32)],
        input_output_aliases={7 + i: i for i in range(len(outs))},
        cost_estimate=hub_cost(rows_of(chunk)),
        name="lower_frames",
    )


def blank(slot, after):
    def kernel(*refs):
        pass

    shapes = grad_shapes(slot)
    return call(
        kernel, (), [], after, out_shape=shapes, out_specs=[ANY] * len(shapes), name="blank_rows"
    )


def send(array, pairs):
    return lax.ppermute(array, "seq", pairs)


def sum_gains(part):
    count = lax.axis_size("dp")
    mine = part.shape[1] // count
    pieces = part.reshape(2, count, mine, part.shape[2])
    total = jnp.sum(lax.all_to_all(pieces, "dp", split_axis=1, concat_axis=1, tiled=True), axis=1)
    total = total + send(total, SWAP)
    total = total + send(total, MIDDLE)
    edge = send(total, BACK_S)
    chip, _ = place()
    return jnp.where((chip == 1) | (chip == 2), total, edge)


def hub_body(queries, key_proj, value_proj, out_grad, query_gain, key_gain):
    shape = queries.shape
    heads, width = shape[-2:]
    half = shape[2] // 2 * heads
    arrays = [x.reshape(2, half, width) for x in (queries, key_proj, value_proj, out_grad)]
    cycle = math.lcm(BLOCK, heads)
    chunks = len(CUTS)

    near = send(halves(0, rows_of(0), arrays, ()), SWAP)
    traded = [(near, 0)]

    edges, others, fars, grads, packed = {}, {}, {}, {}, {}
    passed, sums, kept = {}, [], {-1: None}

    def bring(chunk):
        after = []
        if chunk >= 2:
            after += [passed[chunk - 2], edges[chunk - 2][1]]
        if chunk >= 3:
            after.append(grads[chunk - 3][0])
        swapped, offset = traded[min(chunk, 1)]
        to_hub, to_middle = pack(chunk, offset, arrays, swapped, after)
        edges[chunk] = (to_hub, send(to_hub, EDGE))
        others[chunk] = send(to_middle, MIDDLE)
        return to_hub

    def pass_on(chunk):
        after = [grads[chunk - 1][0]] if chunk else []
        passed[chunk] = forward(chunk, edges[chunk][1], packed.get(chunk - 1), after)
        fars[chunk] = send(passed[chunk], MIDDLE)

    def work(slot):
        after = list(kept[slot - 2][:1]) if slot >= 2 else []
        if slot < chunks:
            data = (*edges[slot], others[slot], fars[slot])
            *parts, packed[slot], sum_q, sum_k = upper(slot, heads, data, gains, after)
            sums.append((sum_q, sum_k))
        else:
            parts = blank(slot, after)
        if slot > 0:
            chunk = slot - 1
            data = (*edges[chunk], others[chunk], fars[chunk])
            if slot < chunks:
                cross, skip = fars[slot], 4 * rows_of(slot)
            else:
                cross, skip = send(packed[chunk], DOWN), 0
            *parts, sum_q, sum_k = lower(slot, heads, data, cross, skip, gains, parts, after)
            sums.append((sum_q, sum_k))
        grads[slot] = parts

    def give(slot):
        own, other, *edge = grads[slot]
        rows = out_rows(slot)
        if slot < chunks - 1:
            pieces = (own, other, send(edge[0], BACK_S))
            kernel = functools.partial(place_kernel, slot)
            kept[slot] = settle_rows(kernel, half, pieces, kept[slot - 1], 4, rows)
            return
        if slot == chunks - 1:
            *outs, late = kept[slot - 1]
            kernel = functools.partial(place_late_kernel, slot - 1)
            kept[slot - 1] = settle_rows(kernel, half, (send(late, SWAP),), outs, 3, half // 2)
        pieces = (own, send(other, SWAP), send(edge[0], BACK_S), send(edge[1], BACK_X))
        kernel = functools.partial(place_last_kernel, slot)
        kept[slot] = settle_rows(kernel, half, pieces, kept[slot - 1], 3, rows)

    first = bring(0)
    rest = halves(rows_of(0), half - rows_of(0), arrays, (first,))
    traded.append((send(rest, SWAP), rows_of(0)))
    bring(1)
    both = lax.all_gather(jnp.stack([query_gain, key_gain]), "dp", axis=1, tiled=True)
    gains = [jnp.tile(both[t], (cycle // heads, 1)) for t in range(2)]
    for slot in range(chunks + 1):
        if slot < chunks:
            pass_on(slot)
        if slot + 2 < chunks:
            bring(slot + 2)
        work(slot)
        give(slot)

    totals = jnp.stack([functools.reduce(jnp.add, [s[t] for s in sums]) for t in range(2)])
    totals = sum_gains(totals)
    return (*[x.reshape(shape) for x in kept[chunks]], totals[0], totals[1])


def wide_attention(query_norm, key_norm, value_in, grad_in):
    frames = query_norm.shape[1]
    scaling = 1.0 / math.sqrt(query_norm.shape[-1])
    scores = (
        jnp.einsum("efphd,egphd->ephfg", query_norm, key_norm, preferred_element_type=F32) * scaling
    )
    allowed = iota((frames, frames), 1) <= iota((frames, frames), 0)
    scores = jnp.where(allowed, scores, -jnp.inf)
    expo = jnp.exp(scores - jnp.max(scores, axis=-1, keepdims=True))
    probability = expo / jnp.sum(expo, axis=-1, keepdims=True)
    prob_low = probability.astype(BF16)
    attn_out = jnp.einsum("ephfg,egphd->efphd", prob_low, value_in, preferred_element_type=F32)
    row_dots = jnp.transpose(jnp.sum(grad_in.astype(F32) * attn_out, axis=-1), (0, 2, 3, 1))
    prob_grad = jnp.einsum("efphd,egphd->ephfg", grad_in, value_in, preferred_element_type=F32)
    score_low = (probability * (prob_grad - row_dots[..., None])).astype(BF16)
    query_step = jnp.einsum("ephfg,egphd->efphd", score_low, key_norm, preferred_element_type=F32)
    key_step = jnp.einsum("ephfg,efphd->egphd", score_low, query_norm, preferred_element_type=F32)
    value_step = jnp.einsum("ephfg,efphd->egphd", prob_low, grad_in, preferred_element_type=F32)
    return (
        (query_step * scaling).astype(BF16),
        (key_step * scaling).astype(BF16),
        value_step.astype(BF16),
    )


def wide_body(queries, key_proj, value_proj, out_grad, query_gain, key_gain):
    gain_q = lax.all_gather(query_gain, "dp", axis=0, tiled=True)
    gain_k = lax.all_gather(key_gain, "dp", axis=0, tiled=True)
    q_hat, q_inv = rms(queries)
    k_hat, k_inv = rms(key_proj)
    pieces = [
        lax.all_to_all(x, "seq", split_axis=2, concat_axis=1, tiled=True)
        for x in ((q_hat * gain_q).astype(BF16), (k_hat * gain_k).astype(BF16), value_proj, out_grad)
    ]
    steps = [
        lax.all_to_all(x, "seq", split_axis=1, concat_axis=2, tiled=True)
        for x in wide_attention(*pieces)
    ]
    query_grad, part_q = norm_back(steps[0], q_hat, q_inv, gain_q)
    key_grad, part_k = norm_back(steps[1], k_hat, k_inv, gain_k)
    axes = tuple(range(part_q.ndim - 2))
    totals = lax.psum((jnp.sum(part_q, axis=axes), jnp.sum(part_k, axis=axes)), "seq")
    totals = [lax.psum_scatter(t, "dp", scatter_dimension=0, tiled=True) for t in totals]
    return (query_grad, key_grad, steps[2], *totals)


def body(*args):
    frames = lax.axis_size("seq")
    patches, heads, width = args[0].shape[2:]
    rows = patches // 2 * heads
    if frames == 8 and args[0].shape[:2] == (1, 1) and width == 128 and rows == sum(CUTS) * BLOCK:
        return hub_body(*args)
    return wide_body(*args)


def solution(mesh):
    whole = P("dp", "seq", None, None, None)
    gain = P("dp", None)
    return jax.shard_map(
        body,
        mesh=mesh,
        in_specs=(whole,) * 4 + (gain,) * 2,
        out_specs=(whole,) * 3 + (gain,) * 2,
        check_vma=False,
    )
```

```python
import functools
import math

import jax
import jax.numpy as jnp
from jax import lax
from jax.experimental import pallas as pl
from jax.experimental.pallas import tpu as pltpu
from jax.sharding import PartitionSpec as P

EPSILON = 1e-06
BLOCK = 512
GROUP = 16
PAIR = 2 * GROUP
HOPS = 4
TOGETHER = 64
CUTS = (2, 3, 3, 1, 1)

UP = tuple((i, i + 2) for i in range(6))
DOWN = tuple((i + 2, i) for i in range(6))
SWAP = tuple((i, i ^ 1) for i in range(8))
NEAR = tuple((i, i ^ 2) for i in range(8))
FAR = tuple((i, i ^ 4) for i in range(8))

F32 = jnp.float32
BF16 = jnp.bfloat16
ANY = pl.BlockSpec(memory_space=pl.ANY)
VMEM = pl.BlockSpec(memory_space=pltpu.VMEM)


def place():
    index = lax.axis_index("seq")
    chip, core = index // 2, index % 2
    return chip, core


def call(kernel, inputs, in_specs, after=(), **kwargs):
    count, extra = len(inputs), len(after)

    def trimmed(*refs):
        kernel(*refs[:count], *refs[count + extra :])

    return pl.pallas_call(
        trimmed,
        in_specs=list(in_specs) + [ANY] * extra,
        compiler_params=pltpu.CompilerParams(vmem_limit_bytes=56 * 1024 * 1024),
        **kwargs,
    )(*inputs, *after)


def first_of(chunk):
    return sum(CUTS[:chunk]) * BLOCK


def rows_of(chunk):
    return CUTS[chunk] * BLOCK


def copy_cost(rows, tensors):
    return pl.CostEstimate(flops=0, bytes_accessed=rows * 128 * 2 * 2 * tensors, transcendentals=0)


def tile_of(rows):
    return next(rows // k for k in range(2, rows) if rows % (16 * k) == 0 and rows // k <= 1024)


def stream(rows, sources, sinks, move):
    tile = tile_of(rows)

    def spec(ref):
        return pl.BlockSpec((ref.shape[0], tile, 128), lambda i: (0, i, 0))

    pltpu.emit_pipeline(
        move,
        grid=(rows // tile,),
        in_specs=[spec(ref) for ref in sources],
        out_specs=[spec(ref) for ref in sinks],
    )(*sources, *sinks)


def window(ref, index, start, rows, count=1):
    return ref.at[pl.ds(index, count), pl.ds(start, rows)]


def halves_kernel(start, rows, q, k, v, g, out):
    _, core = place()

    def move(*blocks):
        for t in range(4):
            blocks[4][t] = blocks[t][0]

    stream(rows, [window(ref, 1 - core, start, rows) for ref in (q, k, v, g)], [out], move)


def halves(start, rows, arrays, after):
    return call(
        functools.partial(halves_kernel, start, rows),
        arrays,
        [ANY] * 4,
        after,
        out_shape=jax.ShapeDtypeStruct((4, rows, 128), BF16),
        out_specs=ANY,
        cost_estimate=copy_cost(rows, 4),
        name="other_half",
    )


def pack_kernel(start, rows, offset, q, k, v, g, x, up, down):
    _, core = place()

    def move(*blocks):
        for t in range(2):
            for frame in range(2):
                blocks[8][2 * frame + t] = blocks[4 * frame + 1 + t][0]
                blocks[9][2 * frame + t] = blocks[4 * frame + 3 * t][0]

    own = [window(ref, core, start, rows) for ref in (q, k, v, g)]
    other = [window(x, t, start - offset, rows) for t in range(4)]
    stream(rows, own + other, [up, down], move)


def pack(chunk, offset, arrays, swapped, after):
    rows = rows_of(chunk)
    return call(
        functools.partial(pack_kernel, first_of(chunk), rows, offset),
        (*arrays, swapped),
        [ANY] * 5,
        after,
        out_shape=[jax.ShapeDtypeStruct((4, rows, 128), BF16)] * 2,
        out_specs=[ANY] * 2,
        cost_estimate=copy_cost(rows, 8),
        name="pack_rows",
    )


def place_kernel(start, rows, swapped, *refs):
    outs = refs[3:]
    _, core = place()

    def move(src, *dsts):
        for t, dst in enumerate(dsts):
            dst[0] = src[t]

    stream(rows, [swapped], [window(out, 1 - core, start, rows) for out in outs], move)


def settle_rows(chunk, swapped, outs):
    rows = rows_of(chunk)
    return call(
        functools.partial(place_kernel, first_of(chunk), rows),
        (swapped, *outs),
        [ANY] * 4,
        out_shape=[jax.ShapeDtypeStruct(out.shape, BF16) for out in outs],
        out_specs=[ANY] * 3,
        input_output_aliases={1 + i: i for i in range(3)},
        cost_estimate=copy_cost(rows, 3),
        name="place_rows",
    )


def rms(values):
    wide = values.astype(F32)
    inverse = lax.rsqrt(jnp.mean(wide * wide, axis=-1, keepdims=True) + EPSILON)
    return wide * inverse, inverse


def norm_back(step, hat, inverse, gain):
    wide = step.astype(F32)
    gained = gain * wide
    result = inverse * (gained - hat * jnp.mean(gained * hat, axis=-1, keepdims=True))
    return result.astype(BF16), wide * hat


def mul_t(a, b):
    return lax.dot_general(a, b, (((1,), (1,)), ((), ())), preferred_element_type=F32)


def t_mul(a, b):
    return lax.dot_general(a, b, (((0,), (0,)), ((), ())), preferred_element_type=F32)


def mul(a, b):
    return jnp.dot(a, b, preferred_element_type=F32)


def iota(shape, axis):
    return lax.broadcasted_iota(jnp.int32, shape, axis)


def allowed_pairs(chip, core):
    shape = (PAIR, HOPS * PAIR)
    rows, cols = iota(shape, 0), iota(shape, 1)
    hop = cols // PAIR

    def parity(index):
        cross = index // GROUP % 2
        return cross + core - 2 * cross * core

    late = ((hop == 0) & (parity(cols) <= parity(rows))) | ((hop > 0) & (hop <= chip))
    return (rows % GROUP == cols % GROUP) & late


def cat(parts):
    return jnp.concatenate(parts, axis=0)


def group(wide, j):
    frames = wide.shape[0] // TOGETHER
    return cat([wide[s * TOGETHER + j * GROUP :][:GROUP] for s in range(frames)])


def ungroup(parts):
    return cat([part[s * GROUP :][:GROUP] for s in range(2) for part in parts])


def read(refs, t, rows):
    return cat([ref[2 * x + t, rows, :] for ref in refs for x in range(2)])


def split_rows(x, size):
    return [x[j * size :][:size] for j in range(x.shape[0] // size)]


def attend(qn, kn, grad, value, mask):
    scaling = 1.0 / math.sqrt(qn.shape[-1])
    count = TOGETHER // GROUP
    scores = cat([mul_t(group(qn, j), group(kn, j)) for j in range(count)])
    prob_grad = cat([mul_t(group(grad, j), group(value, j)) for j in range(count)])
    scores = jnp.where(cat([mask] * count) > 0, scores * scaling, -jnp.inf)
    expo = jnp.exp(scores - jnp.max(scores, axis=-1, keepdims=True))
    prob = expo * (1.0 / jnp.sum(expo, axis=-1, keepdims=True))
    prob_low = prob.astype(BF16)
    dots = jnp.sum(prob_low.astype(F32) * prob_grad, axis=-1, keepdims=True)
    score_low = (prob * (prob_grad - dots)).astype(BF16)
    return prob_low, score_low


def fold(acc, rows, part):
    acc[rows, :] += part[:TOGETHER] + part[TOGETHER:]


def settle(own, other, rows, part):
    own[0, rows, :] = part[:TOGETHER]
    other[0, rows, :] = part[TOGETHER:]


def sum_heads(acc, heads):
    total = acc[0:heads, :]
    for i in range(1, acc.shape[0] // heads):
        total = total + acc[i * heads : (i + 1) * heads, :]
    return total


def row_spec(count):
    return pl.BlockSpec((count, BLOCK, 128), lambda i: (0, i, 0))


def gain_spec(first, cycle):
    return pl.BlockSpec((BLOCK, 128), lambda i: ((first + i) % cycle, 0))


PACKED = pl.BlockSpec((PAIR, 128), lambda i: (i, 0))


def query_kernel(chunk, heads, down, up, u1, u2, u3, gain_q, gain_k, _, out, swap, t0, t1, t2, t3, total, acc, mask):
    chip, core = place()
    first, steps = sum(CUTS[:chunk]), CUTS[chunk]
    count = TOGETHER // GROUP
    cycle = acc.shape[0] // BLOCK
    acc[...] = jnp.zeros_like(acc)
    mask[...] = allowed_pairs(chip, core).astype(F32)

    def block(down, up, u1, u2, u3, gain_q, gain_k, out, swap, *packs):
        base = ((first + pl.program_id(0)) % cycle) * BLOCK
        scaling = 1.0 / math.sqrt(128)
        lanes = iota((PAIR, HOPS * 128), 1) % 128 // 4
        source, sink = iota((2 * HOPS * PAIR, HOPS * 128), 0), iota((2 * HOPS * PAIR, HOPS * 128), 1)
        same = source % (HOPS * PAIR) // PAIR == sink // 128
        value = source // (HOPS * PAIR) * 2 + source // GROUP % 2
        spread = jnp.where(same & (value == sink % 4), 1.0, 0.0).astype(BF16)

        def some(i, total):
            rows = pl.ds(pl.multiple_of(i * TOGETHER, TOGETHER), TOGETHER)
            where = pl.ds(pl.multiple_of(base + i * TOGETHER, TOGETHER), TOGETHER)
            gq, gk = cat([gain_q[rows, :]] * 2), cat([gain_k[rows, :]] * 2 * HOPS)
            q_hat, q_inv = rms(read((down,), 0, rows))
            grad = read((down,), 1, rows)
            k_hat, _ = rms(read((up, u1, u2, u3), 0, rows))
            value = read((up, u1, u2, u3), 1, rows)
            qn, kn = (q_hat * gq).astype(BF16), (k_hat * gk).astype(BF16)
            prob, score = attend(qn, kn, grad, value, mask[...])
            steps = [mul(part, group(kn, j)) for j, part in enumerate(split_rows(score, PAIR))]
            step = (ungroup(steps) * scaling).astype(BF16)
            result, part = norm_back(step, q_hat, q_inv, gq)
            settle(out, swap, rows, result)
            fold(acc, where, part)
            wide = mul(jnp.concatenate([prob, score], axis=1), spread)
            for j, part in enumerate(split_rows(wide, PAIR)):
                total = jnp.where(lanes == i * count + j, part, total)
            return total

        total = lax.fori_loop(0, BLOCK // TOGETHER, some, jnp.zeros((PAIR, HOPS * 128), F32))
        for h, pack in enumerate(packs):
            pack[...] = total[:, h * 128 : (h + 1) * 128].astype(BF16)

    start, rows = first_of(chunk), rows_of(chunk)
    pltpu.emit_pipeline(
        block,
        grid=(steps,),
        in_specs=[row_spec(4)] * 5 + [gain_spec(first, cycle)] * 2,
        out_specs=[row_spec(1)] * 2 + [PACKED] * 4,
    )(down, up, u1, u2, u3, gain_q, gain_k, window(out, core, start, rows), swap.at[pl.ds(0, 1)], t0, t1, t2, t3)
    total[...] = sum_heads(acc, heads)


def key_kernel(
    chunk, heads, up, down, d1, d2, d3, t0, t1, t2, t3, gain_q, gain_k, *refs
):
    out_k, out_v, swap, total, acc = refs[3:]
    _, core = place()
    first, steps = sum(CUTS[:chunk]), CUTS[chunk]
    count = TOGETHER // GROUP
    cycle = acc.shape[0] // BLOCK
    acc[...] = jnp.zeros_like(acc)

    def block(up, down, d1, d2, d3, t0, t1, t2, t3, gain_q, gain_k, out_k, out_v, swap_k, swap_v):
        base = ((first + pl.program_id(0)) % cycle) * BLOCK
        scaling = 1.0 / math.sqrt(128)
        same = iota((HOPS * PAIR, PAIR), 0) % GROUP == iota((HOPS * PAIR, PAIR), 1) % GROUP
        lanes = iota((HOPS * PAIR, 128), 1) // 4
        value, sink = iota((128, PAIR), 0) % 4, iota((128, PAIR), 1) // GROUP
        take_p = jnp.where(value == sink, 1.0, 0.0).astype(BF16)
        take_s = jnp.where(value == sink + 2, 1.0, 0.0).astype(BF16)
        packed = cat([t[...] for t in (t0, t1, t2, t3)]).astype(F32)

        def some(i, carry):
            rows = pl.ds(pl.multiple_of(i * TOGETHER, TOGETHER), TOGETHER)
            where = pl.ds(pl.multiple_of(base + i * TOGETHER, TOGETHER), TOGETHER)
            gq, gk = cat([gain_q[rows, :]] * 2 * HOPS), cat([gain_k[rows, :]] * 2)
            k_hat, k_inv = rms(read((up,), 0, rows))
            q_hat, _ = rms(read((down, d1, d2, d3), 0, rows))
            grad = read((down, d1, d2, d3), 1, rows)
            qn = (q_hat * gq).astype(BF16)
            k_steps, v_steps = [], []
            for j in range(count):
                mine = jnp.where(lanes == i * count + j, packed, 0.0).astype(BF16)
                prob = jnp.where(same, mul(mine, take_p), 0.0).astype(BF16)
                score = jnp.where(same, mul(mine, take_s), 0.0).astype(BF16)
                k_steps.append(t_mul(score, group(qn, j)))
                v_steps.append(t_mul(prob, group(grad, j)))
            step = (ungroup(k_steps) * scaling).astype(BF16)
            result, part = norm_back(step, k_hat, k_inv, gk)
            settle(out_k, swap_k, rows, result)
            settle(out_v, swap_v, rows, ungroup(v_steps).astype(BF16))
            fold(acc, where, part)
            return carry

        lax.fori_loop(0, BLOCK // TOGETHER, some, 0)

    start, rows = first_of(chunk), rows_of(chunk)
    pltpu.emit_pipeline(
        block,
        grid=(steps,),
        in_specs=[row_spec(4)] * 5 + [PACKED] * 4 + [gain_spec(first, cycle)] * 2,
        out_specs=[row_spec(1)] * 4,
    )(
        up, down, d1, d2, d3, t0, t1, t2, t3, gain_q, gain_k,
        window(out_k, core, start, rows), window(out_v, core, start, rows),
        swap.at[pl.ds(1, 1)], swap.at[pl.ds(2, 1)],
    )
    total[...] = sum_heads(acc, heads)


def side_cost(rows):
    return pl.CostEstimate(
        flops=rows * 40000, bytes_accessed=rows * 128 * 2 * 24, transcendentals=rows * 300
    )


def query_side(chunk, heads, data, gains, out, after):
    rows, cycle = rows_of(chunk), gains[0].shape[0]
    return call(
        functools.partial(query_kernel, chunk, heads),
        (*data, *gains, out),
        [ANY] * 8,
        after,
        out_shape=[jax.ShapeDtypeStruct(out.shape, BF16), jax.ShapeDtypeStruct((3, rows, 128), BF16)]
        + [jax.ShapeDtypeStruct((CUTS[chunk] * PAIR, 128), BF16)] * 4
        + [jax.ShapeDtypeStruct((heads, 128), F32)],
        out_specs=[ANY] * 6 + [VMEM],
        scratch_shapes=[pltpu.VMEM((cycle, 128), F32), pltpu.VMEM((PAIR, HOPS * PAIR), F32)],
        input_output_aliases={7: 0},
        cost_estimate=side_cost(rows),
        name="query_side",
    )


def key_side(chunk, heads, data, packed, gains, outs, swap, after):
    rows, cycle = rows_of(chunk), gains[0].shape[0]
    return call(
        functools.partial(key_kernel, chunk, heads),
        (*data, *packed, *gains, *outs, swap),
        [ANY] * 14,
        after,
        out_shape=[jax.ShapeDtypeStruct(x.shape, BF16) for x in (*outs, swap)]
        + [jax.ShapeDtypeStruct((heads, 128), F32)],
        out_specs=[ANY] * 3 + [VMEM],
        scratch_shapes=[pltpu.VMEM((cycle, 128), F32)],
        input_output_aliases={11: 0, 12: 1, 13: 2},
        cost_estimate=side_cost(rows),
        name="key_side",
    )


def blank(half):
    def kernel(*refs):
        pass

    return call(
        kernel,
        (),
        [],
        out_shape=[jax.ShapeDtypeStruct((2, half, 128), BF16)] * 3,
        out_specs=[ANY] * 3,
        name="blank_rows",
    )


def send(array, pairs):
    return lax.ppermute(array, "seq", pairs)


def sum_gains(part):
    count = lax.axis_size("dp")
    mine = part.shape[1] // count
    pieces = part.reshape(2, count, mine, part.shape[2])
    total = jnp.sum(lax.all_to_all(pieces, "dp", split_axis=1, concat_axis=1, tiled=True), axis=1)
    for pairs in (SWAP, NEAR, FAR):
        total = total + send(total, pairs)
    return total


def line_body(queries, key_proj, value_proj, out_grad, query_gain, key_gain):
    shape = queries.shape
    heads, width = shape[-2:]
    half = shape[2] // 2 * heads
    arrays = [x.reshape(2, half, width) for x in (queries, key_proj, value_proj, out_grad)]
    cycle = math.lcm(BLOCK, heads)
    chunks = len(CUTS)

    near = send(halves(0, rows_of(0), arrays, ()), SWAP)
    traded = [(near, 0)]
    ups, downs, packs, swaps, sums = {}, {}, {}, {}, []

    def bring(chunk):
        after = []
        if chunk >= 1:
            after += [ups[chunk - 1][2], downs[chunk - 1][2]]
        if chunk >= 2:
            after.append(packs[chunk - 2][0])
        swapped, offset = traded[min(chunk, 1)]
        up, down = pack(chunk, offset, arrays, swapped, after)
        ups[chunk], downs[chunk] = [up], [down]
        for _ in range(HOPS - 1):
            ups[chunk].append(send(ups[chunk][-1], UP))
            downs[chunk].append(send(downs[chunk][-1], DOWN))
        return up

    first = bring(0)
    rest = halves(rows_of(0), half - rows_of(0), arrays, (first,))
    traded.append((send(rest, SWAP), rows_of(0)))
    both = lax.all_gather(jnp.stack([query_gain, key_gain]), "dp", axis=1, tiled=True)
    gains = [jnp.tile(both[t], (cycle // heads, 1)) for t in range(2)]

    outs = list(blank(half))
    bring(1)
    for chunk in range(chunks):
        own_up, own_down = ups[chunk][0], downs[chunk][0]
        data = (own_down, *ups[chunk])
        outs[0], swap, *packed, sum_q = query_side(chunk, heads, data, gains, outs[0], ())
        packs[chunk] = packed
        if chunk + 2 < chunks:
            bring(chunk + 2)
        met = [packed[0]] + [
            send(packed[h], [(i, i - 2 * h) for i in range(2 * h, 2 * HOPS)]) for h in range(1, HOPS)
        ]
        data = (own_up, *downs[chunk])
        outs[1], outs[2], swap, sum_k = key_side(chunk, heads, data, met, gains, outs[1:], swap, ())
        outs = list(settle_rows(chunk, send(swap, SWAP), outs))
        sums.append((sum_q, sum_k))

    totals = jnp.stack([functools.reduce(jnp.add, [s[t] for s in sums]) for t in range(2)])
    totals = sum_gains(totals)
    return (*[x.reshape(shape) for x in outs], totals[0], totals[1])


def wide_attention(query_norm, key_norm, value_in, grad_in):
    frames = query_norm.shape[1]
    scaling = 1.0 / math.sqrt(query_norm.shape[-1])
    scores = (
        jnp.einsum("efphd,egphd->ephfg", query_norm, key_norm, preferred_element_type=F32) * scaling
    )
    allowed = iota((frames, frames), 1) <= iota((frames, frames), 0)
    scores = jnp.where(allowed, scores, -jnp.inf)
    expo = jnp.exp(scores - jnp.max(scores, axis=-1, keepdims=True))
    probability = expo / jnp.sum(expo, axis=-1, keepdims=True)
    prob_low = probability.astype(BF16)
    attn_out = jnp.einsum("ephfg,egphd->efphd", prob_low, value_in, preferred_element_type=F32)
    row_dots = jnp.transpose(jnp.sum(grad_in.astype(F32) * attn_out, axis=-1), (0, 2, 3, 1))
    prob_grad = jnp.einsum("efphd,egphd->ephfg", grad_in, value_in, preferred_element_type=F32)
    score_low = (probability * (prob_grad - row_dots[..., None])).astype(BF16)
    query_step = jnp.einsum("ephfg,egphd->efphd", score_low, key_norm, preferred_element_type=F32)
    key_step = jnp.einsum("ephfg,efphd->egphd", score_low, query_norm, preferred_element_type=F32)
    value_step = jnp.einsum("ephfg,efphd->egphd", prob_low, grad_in, preferred_element_type=F32)
    return (
        (query_step * scaling).astype(BF16),
        (key_step * scaling).astype(BF16),
        value_step.astype(BF16),
    )


def wide_body(queries, key_proj, value_proj, out_grad, query_gain, key_gain):
    gain_q = lax.all_gather(query_gain, "dp", axis=0, tiled=True)
    gain_k = lax.all_gather(key_gain, "dp", axis=0, tiled=True)
    q_hat, q_inv = rms(queries)
    k_hat, k_inv = rms(key_proj)
    pieces = [
        lax.all_to_all(x, "seq", split_axis=2, concat_axis=1, tiled=True)
        for x in ((q_hat * gain_q).astype(BF16), (k_hat * gain_k).astype(BF16), value_proj, out_grad)
    ]
    steps = [
        lax.all_to_all(x, "seq", split_axis=1, concat_axis=2, tiled=True)
        for x in wide_attention(*pieces)
    ]
    query_grad, part_q = norm_back(steps[0], q_hat, q_inv, gain_q)
    key_grad, part_k = norm_back(steps[1], k_hat, k_inv, gain_k)
    axes = tuple(range(part_q.ndim - 2))
    totals = lax.psum((jnp.sum(part_q, axis=axes), jnp.sum(part_k, axis=axes)), "seq")
    totals = [lax.psum_scatter(t, "dp", scatter_dimension=0, tiled=True) for t in totals]
    return (query_grad, key_grad, steps[2], *totals)


def body(*args):
    frames = lax.axis_size("seq")
    patches, heads, width = args[0].shape[2:]
    rows = patches // 2 * heads
    if frames == 8 and args[0].shape[:2] == (1, 1) and width == 128 and rows == sum(CUTS) * BLOCK:
        return line_body(*args)
    return wide_body(*args)


def solution(mesh):
    whole = P("dp", "seq", None, None, None)
    gain = P("dp", None)
    return jax.shard_map(
        body,
        mesh=mesh,
        in_specs=(whole,) * 4 + (gain,) * 2,
        out_specs=(whole,) * 3 + (gain,) * 2,
        check_vma=False,
    )
```

```python
import functools
import math

import jax
import jax.numpy as jnp
from jax import lax
from jax.experimental import pallas as pl
from jax.experimental.pallas import tpu as pltpu
from jax.sharding import PartitionSpec as P

EPSILON = 1e-06
BLOCK = 256
GROUP = 16
SLOTS = 4
WIDE = GROUP * SLOTS
TOGETHER = 64
CUTS = (3, 3, 3, 3, 3, 2, 2, 1)

EDGE = ((0, 2), (1, 3), (6, 4), (7, 5))
MIDDLE = ((2, 4), (3, 5), (4, 2), (5, 3))
DOWN = ((4, 2), (5, 3))
BACK_S = ((2, 0), (3, 1), (4, 6), (5, 7))
BACK_X = ((2, 1), (3, 0), (4, 7), (5, 6))
SWAP = tuple((i, i ^ 1) for i in range(8))

F32 = jnp.float32
BF16 = jnp.bfloat16
ANY = pl.BlockSpec(memory_space=pl.ANY)
VMEM = pl.BlockSpec(memory_space=pltpu.VMEM)


def place():
    index = lax.axis_index("seq")
    chip, core = index // 2, index % 2
    return chip, core


def call(kernel, inputs, in_specs, after=(), **kwargs):
    count, extra = len(inputs), len(after)

    def trimmed(*refs):
        kernel(*refs[:count], *refs[count + extra :])

    return pl.pallas_call(
        trimmed,
        in_specs=list(in_specs) + [ANY] * extra,
        compiler_params=pltpu.CompilerParams(vmem_limit_bytes=56 * 1024 * 1024),
        **kwargs,
    )(*inputs, *after)


def first_of(chunk):
    return sum(CUTS[:chunk]) * BLOCK


def rows_of(chunk):
    return CUTS[chunk] * BLOCK


def out_rows(slot):
    return max(CUTS[max(slot - 1, 0) : slot + 1]) * BLOCK


def copy_cost(rows, tensors):
    return pl.CostEstimate(flops=0, bytes_accessed=rows * 128 * 2 * 2 * tensors, transcendentals=0)


def tile_of(rows):
    return next(rows // k for k in range(2, rows) if rows % (16 * k) == 0 and rows // k <= 1024)


def stream(rows, sources, sinks, move):
    tile = tile_of(rows)

    def spec(ref):
        return pl.BlockSpec((ref.shape[0], tile, 128), lambda i: (0, i, 0))

    pltpu.emit_pipeline(
        move,
        grid=(rows // tile,),
        in_specs=[spec(ref) for ref in sources],
        out_specs=[spec(ref) for ref in sinks],
    )(*sources, *sinks)


def window(ref, index, start, rows, count=1):
    return ref.at[pl.ds(index, count), pl.ds(start, rows)]


def halves_kernel(start, rows, q, k, v, g, out):
    _, core = place()

    def move(*blocks):
        for t in range(4):
            blocks[4][t] = blocks[t][0]

    stream(rows, [window(ref, 1 - core, start, rows) for ref in (q, k, v, g)], [out], move)


def halves(start, rows, arrays, after):
    return call(
        functools.partial(halves_kernel, start, rows),
        arrays,
        [ANY] * 4,
        after,
        out_shape=jax.ShapeDtypeStruct((4, rows, 128), BF16),
        out_specs=ANY,
        cost_estimate=copy_cost(rows, 4),
        name="other_half",
    )


def pack_kernel(start, rows, offset, q, k, v, g, x, edge):
    chip, core = place()

    def run(order):
        def move(*blocks):
            sent = blocks[8]
            for pair in range(2):
                for t in range(2):
                    for frame in range(2):
                        sent[4 * pair + 2 * frame + t] = blocks[4 * frame + 2 * pair + t][0]

        own = [window((q, k, v, g)[t], core, start, rows) for t in order]
        other = [window(x, t, start - offset, rows) for t in order]
        stream(rows, own + other, [edge], move)

    @pl.when(chip < 2)
    def _():
        run((1, 2, 0, 3))

    @pl.when(chip >= 2)
    def _():
        run((0, 3, 1, 2))


def pack(chunk, offset, arrays, swapped, after):
    rows = rows_of(chunk)
    return call(
        functools.partial(pack_kernel, first_of(chunk), rows, offset),
        (*arrays, swapped),
        [ANY] * 5,
        after,
        out_shape=jax.ShapeDtypeStruct((8, rows, 128), BF16),
        out_specs=ANY,
        cost_estimate=copy_cost(rows, 8),
        name="pack_rows",
    )


def forward_kernel(sizes, *refs):
    sources, out = refs[:-1], refs[-1]
    chip, _ = place()

    def move(src, *dsts):
        for q, dst in enumerate(dsts):
            dst[...] = src[q]

    @pl.when((chip == 1) | (chip == 2))
    def _():
        start = 0
        for rows, src in zip(sizes, sources):
            tile = tile_of(rows)
            pltpu.emit_pipeline(
                move,
                grid=(rows // tile,),
                in_specs=[pl.BlockSpec((4, tile, 128), lambda i: (0, i, 0))],
                out_specs=[pl.BlockSpec((tile, 128), lambda i: (i, 0))] * 4,
            )(src, *[out.at[pl.ds(start + q * rows, rows)] for q in range(4)])
            start += 4 * rows


def forward(sources, after):
    sizes = [x.shape[1] for x in sources]
    return call(
        functools.partial(forward_kernel, sizes),
        sources,
        [ANY] * len(sources),
        after,
        out_shape=jax.ShapeDtypeStruct((4 * sum(sizes), 128), BF16),
        out_specs=ANY,
        cost_estimate=copy_cost(sum(sizes), 4),
        name="forward_rows",
    )


def copy_three(src, *dsts):
    for t, dst in enumerate(dsts):
        dst[0] = src[t]


def copy_all(src, dst):
    dst[...] = src[...]


def by_chip(slot, run):
    chip, _ = place()
    for which in range(4):
        chunk = slot if which >= 2 else slot - 1
        if 0 <= chunk < len(CUTS):
            pl.when(chip == which)(functools.partial(run, chunk, which in (1, 2)))


def place_kernel(slot, own, other, back, *refs):
    outs, late, token = refs[-5:-2], refs[-2], refs[-1]
    token[...] = jnp.zeros_like(token)
    _, core = place()

    def run(chunk, hub):
        start, rows = first_of(chunk), rows_of(chunk)
        near = own.at[:, pl.ds(0, rows)] if hub else window(back, 0, 0, rows, 3)
        far = other.at[:, pl.ds(0, rows)] if hub else window(back, 3, 0, rows, 3)
        stream(rows, [near], [window(out, core, start, rows) for out in outs], copy_three)
        stream(rows, [far], [window(late, 0, start, rows, 3)], copy_all)

    by_chip(slot, run)


def place_last_kernel(slot, own, other, back_s, back_x, *refs):
    outs, token = refs[-4:-1], refs[-1]
    token[...] = jnp.zeros_like(token)
    _, core = place()

    def run(chunk, hub):
        start, rows = first_of(chunk), rows_of(chunk)
        for half, src in ((core, own if hub else back_s), (1 - core, other if hub else back_x)):
            sinks = [window(out, half, start, rows) for out in outs]
            stream(rows, [src.at[:, pl.ds(0, rows)]], sinks, copy_three)

    by_chip(slot, run)


def place_late_kernel(slot, late, *refs):
    outs, token = refs[-4:-1], refs[-1]
    token[...] = jnp.zeros_like(token)
    chip, core = place()

    def run(rows):
        sinks = [window(out, 1 - core, 0, rows) for out in outs]
        stream(rows, [window(late, 0, 0, rows, 3)], sinks, copy_three)

    @pl.when(chip < 2)
    def _():
        run(first_of(slot))

    @pl.when(chip >= 2)
    def _():
        run(first_of(slot + 1))


def settle_rows(kernel, half, pieces, kept, count, rows, after=()):
    kept = kept or ()
    return call(
        kernel,
        (*pieces, *kept),
        [ANY] * (len(pieces) + len(kept)),
        after,
        out_shape=[jax.ShapeDtypeStruct((n, half, 128), BF16) for n in (2, 2, 2, 3)[:count]]
        + [jax.ShapeDtypeStruct((8, 128), F32)],
        out_specs=[ANY] * count + [VMEM],
        input_output_aliases={len(pieces) + i: i for i in range(len(kept))},
        cost_estimate=copy_cost(rows, 6),
        name="place_rows",
    )


def rms(values):
    wide = values.astype(F32)
    inverse = lax.rsqrt(jnp.mean(wide * wide, axis=-1, keepdims=True) + EPSILON)
    return wide * inverse, inverse


def norm_back(step, hat, inverse, gain):
    wide = step.astype(F32)
    gained = gain * wide
    result = inverse * (gained - hat * jnp.mean(gained * hat, axis=-1, keepdims=True))
    return result.astype(BF16), wide * hat


def mul_t(a, b):
    return lax.dot_general(a, b, (((1,), (1,)), ((), ())), preferred_element_type=F32)


def t_mul(a, b):
    return lax.dot_general(a, b, (((0,), (0,)), ((), ())), preferred_element_type=F32)


def mul(a, b):
    return jnp.dot(a, b, preferred_element_type=F32)


def iota(shape, axis):
    return lax.broadcasted_iota(jnp.int32, shape, axis)


def frame_of(slot, core, upper):
    cross = slot % 2
    side = slot // 2
    side = side if upper else 1 - side
    return 2 * side + cross + core - 2 * cross * core


def causal(core, upper):
    shape = (WIDE, 2 * WIDE if upper else WIDE)
    rows, cols = iota(shape, 0), iota(shape, 1)
    key = cols // GROUP
    frame = frame_of(key % SLOTS, core, upper)
    if upper:
        frame = jnp.where(key < SLOTS, -1, frame)
    late = frame <= frame_of(rows // GROUP, core, upper)
    return (rows % GROUP == cols % GROUP) & late


def cat(parts):
    return jnp.concatenate(parts, axis=0)


def tiled(gain):
    return cat([gain] * SLOTS)


def group(wide, j):
    slots = wide.shape[0] // TOGETHER
    return cat([wide[s * TOGETHER + j * GROUP :][:GROUP] for s in range(slots)])


def ungroup(parts):
    return cat([part[s * GROUP :][:GROUP] for s in range(SLOTS) for part in parts])


def fold(acc, rows, part):
    total = part[:TOGETHER]
    for s in range(1, SLOTS):
        total = total + part[s * TOGETHER :][:TOGETHER]
    acc[rows, :] += total


def settle(outs, rows, parts):
    for t, part in enumerate(parts):
        for s, out in enumerate(outs):
            out[t, rows, :] = part[s * TOGETHER :][:TOGETHER]


def sum_heads(acc, heads):
    total = acc[0:heads, :]
    for i in range(1, acc.shape[0] // heads):
        total = total + acc[i * heads : (i + 1) * heads, :]
    return total


def read(refs, t, rows):
    return cat([ref[2 * x + t, rows, :] for ref in refs for x in range(2)])


def read_met(near, far, t, rows):
    return cat([side[2 * x + t][rows, :] for side in (near, far) for x in range(2)])


def hub_specs(steps):
    four = lambda n: pl.BlockSpec((4, BLOCK, 128), lambda i: (n, i, 0))
    flat = lambda q: pl.BlockSpec((BLOCK, 128), lambda i: (q * steps + i, 0))
    return [four(0), four(1), four(0), four(1)] + [flat(q) for q in range(4)] * 2


def hub_refs(steps, skip, own, edge, other, far):
    rows = 4 * steps * BLOCK
    return [own, own, edge, edge] + [other.at[pl.ds(skip, rows)]] * 4 + [far.at[pl.ds(0, rows)]] * 4


def grad_specs():
    return [pl.BlockSpec((3, BLOCK, 128), lambda i: (0, i, 0))] * 4


def grad_refs(outs):
    if len(outs) == 4:
        return list(outs)
    return [outs[0], outs[1], outs[2].at[pl.ds(0, 3)], outs[2].at[pl.ds(3, 3)]]


def gain_spec(first, cycle):
    return pl.BlockSpec((BLOCK, 128), lambda i: ((first + i) % cycle, 0))


def attend(qn, kn, grad, value, allowed):
    scaling = 1.0 / math.sqrt(qn.shape[-1])
    count = TOGETHER // GROUP
    scores = cat([mul_t(group(qn, j), group(kn, j)) for j in range(count)])
    prob_grad = cat([mul_t(group(grad, j), group(value, j)) for j in range(count)])
    mask = cat([allowed] * count)
    scores = jnp.where(mask > 0, scores * scaling, -jnp.inf)
    expo = jnp.exp(scores - jnp.max(scores, axis=-1, keepdims=True))
    prob = expo * (1.0 / jnp.sum(expo, axis=-1, keepdims=True))
    prob_low = prob.astype(BF16)
    dots = jnp.sum(prob_low.astype(F32) * prob_grad, axis=-1, keepdims=True)
    score_low = (prob * (prob_grad - dots)).astype(BF16)
    split = lambda x: [x[j * WIDE :][:WIDE] for j in range(count)]
    return split(prob_low), split(score_low)


def upper_kernel(chunk, skip, heads, own, edge, other, far, gain_q, gain_k, *refs):
    outs, (packed, sum_q, sum_k, acc_q, acc_k, mask) = refs[:-6], refs[-6:]
    chip, core = place()
    first, steps = sum(CUTS[:chunk]), CUTS[chunk]
    count = TOGETHER // GROUP
    cycle = acc_q.shape[0] // BLOCK

    def block(own_a, own_b, edge_a, edge_b, *refs):
        other, far, (gain_q, gain_k), out, pack_ref = refs[:4], refs[4:8], refs[8:10], refs[10:14], refs[14]
        base = ((first + pl.program_id(0)) % cycle) * BLOCK
        scaling = 1.0 / math.sqrt(128)
        lanes = iota((WIDE, 128), 1) // 8
        spread_r, spread_c = iota((2 * WIDE, 128), 0), iota((2 * WIDE, 128), 1)
        spread = jnp.where(spread_r // GROUP == spread_c % 8, 1.0, 0.0).astype(BF16)

        def some(i, total):
            rows = pl.ds(pl.multiple_of(i * TOGETHER, TOGETHER), TOGETHER)
            place = pl.ds(pl.multiple_of(base + i * TOGETHER, TOGETHER), TOGETHER)
            gq, gk = tiled(gain_q[rows, :]), tiled(gain_k[rows, :])
            q_hat, q_inv = rms(read((own_a, edge_a), 0, rows))
            grad = read((own_a, edge_a), 1, rows)
            kl_hat, _ = rms(read_met(other, far, 0, rows))
            ku_hat, ku_inv = rms(read((own_b, edge_b), 0, rows))
            value = cat([read_met(other, far, 1, rows), read((own_b, edge_b), 1, rows)])
            qn = (q_hat * gq).astype(BF16)
            kn = cat([(kl_hat * gk).astype(BF16), (ku_hat * gk).astype(BF16)])
            prob, score = attend(qn, kn, grad, value, mask[...])
            q_step = ungroup([mul(score[j], group(kn, j)) for j in range(count)])
            k_step = ungroup([t_mul(score[j][:, WIDE:], group(qn, j)) for j in range(count)])
            v_step = ungroup([t_mul(prob[j][:, WIDE:], group(grad, j)) for j in range(count)])
            q_step, k_step = (q_step * scaling).astype(BF16), (k_step * scaling).astype(BF16)
            dq, part_q = norm_back(q_step, q_hat, q_inv, gq)
            dk, part_k = norm_back(k_step, ku_hat, ku_inv, gk)
            settle(out, rows, (dq, dk, v_step.astype(BF16)))
            fold(acc_q, place, part_q)
            fold(acc_k, place, part_k)
            for j in range(count):
                cross = jnp.concatenate([prob[j][:, :WIDE], score[j][:, :WIDE]], axis=1)
                total = jnp.where(lanes == i * count + j, mul(cross, spread), total)
            return total

        total = lax.fori_loop(0, BLOCK // TOGETHER, some, jnp.zeros((WIDE, 128), F32))
        pack_ref[...] = total.astype(BF16)

    @pl.when(chip == 2)
    def _():
        acc_q[...] = jnp.zeros_like(acc_q)
        acc_k[...] = jnp.zeros_like(acc_k)
        mask[...] = causal(core, True).astype(F32)
        pltpu.emit_pipeline(
            block,
            grid=(steps,),
            in_specs=hub_specs(steps) + [gain_spec(first, cycle)] * 2,
            out_specs=grad_specs() + [pl.BlockSpec((WIDE, 128), lambda i: (i, 0))],
        )(*hub_refs(steps, skip, own, edge, other, far), gain_q, gain_k, *grad_refs(outs), packed)
        sum_q[...] = sum_heads(acc_q, heads)
        sum_k[...] = sum_heads(acc_k, heads)

    @pl.when(chip != 2)
    def _():
        sum_q[...] = jnp.zeros_like(sum_q)
        sum_k[...] = jnp.zeros_like(sum_k)


def lower_kernel(chunk, skip, heads, own, edge, other, far, packed, gain_q, gain_k, *refs):
    outs, (sum_q, sum_k, acc_q, acc_k, mask) = refs[:-5], refs[-5:]
    outs = outs[len(outs) // 2 :]
    chip, core = place()
    first, steps = sum(CUTS[:chunk]), CUTS[chunk]
    count = TOGETHER // GROUP
    cycle = acc_q.shape[0] // BLOCK

    def block(own_a, own_b, edge_a, edge_b, *refs):
        other, far, (gain_q, gain_k, pack_ref), out = refs[:4], refs[4:8], refs[8:11], refs[11:]
        base = ((first + pl.program_id(0)) % cycle) * BLOCK
        both = iota((WIDE, 2 * WIDE), 0) % GROUP == iota((WIDE, 2 * WIDE), 1) % GROUP
        scaling = 1.0 / math.sqrt(128)
        lanes = iota((WIDE, 128), 1) // 8
        spread_r, spread_c = iota((128, 2 * WIDE), 0), iota((128, 2 * WIDE), 1)
        spread = jnp.where(spread_c // GROUP == spread_r % 8, 1.0, 0.0).astype(BF16)
        crossed = pack_ref[...].astype(F32)

        def some(i, carry):
            rows = pl.ds(pl.multiple_of(i * TOGETHER, TOGETHER), TOGETHER)
            place = pl.ds(pl.multiple_of(base + i * TOGETHER, TOGETHER), TOGETHER)
            gq, gk = tiled(gain_q[rows, :]), tiled(gain_k[rows, :])
            k_hat, k_inv = rms(read((own_a, edge_a), 0, rows))
            value = read((own_a, edge_a), 1, rows)
            q_hat, q_inv = rms(read((own_b, edge_b), 0, rows))
            grad = read((own_b, edge_b), 1, rows)
            qu_hat, _ = rms(read_met(other, far, 0, rows))
            grad_u = read_met(other, far, 1, rows)
            kn = (k_hat * gk).astype(BF16)
            qn = (q_hat * gq).astype(BF16)
            qn_u = (qu_hat * gq).astype(BF16)
            prob, score = attend(qn, kn, grad, value, mask[...])
            cross = []
            for j in range(count):
                mine = jnp.where(lanes == i * count + j, crossed, 0.0).astype(BF16)
                cross.append(jnp.where(both, mul(mine, spread), 0.0).astype(BF16))
            q_step = ungroup([mul(score[j], group(kn, j)) for j in range(count)])
            k_step = ungroup(
                [
                    t_mul(cat([score[j], cross[j][:, WIDE:]]), cat([group(qn, j), group(qn_u, j)]))
                    for j in range(count)
                ]
            )
            v_step = ungroup(
                [
                    t_mul(cat([prob[j], cross[j][:, :WIDE]]), cat([group(grad, j), group(grad_u, j)]))
                    for j in range(count)
                ]
            )
            q_step, k_step = (q_step * scaling).astype(BF16), (k_step * scaling).astype(BF16)
            dq, part_q = norm_back(q_step, q_hat, q_inv, gq)
            dk, part_k = norm_back(k_step, k_hat, k_inv, gk)
            settle(out, rows, (dq, dk, v_step.astype(BF16)))
            fold(acc_q, place, part_q)
            fold(acc_k, place, part_k)
            return carry

        lax.fori_loop(0, BLOCK // TOGETHER, some, 0)

    @pl.when(chip == 1)
    def _():
        acc_q[...] = jnp.zeros_like(acc_q)
        acc_k[...] = jnp.zeros_like(acc_k)
        mask[...] = causal(core, False).astype(F32)
        pltpu.emit_pipeline(
            block,
            grid=(steps,),
            in_specs=hub_specs(steps)
            + [gain_spec(first, cycle)] * 2
            + [pl.BlockSpec((WIDE, 128), lambda i: (i, 0))],
            out_specs=grad_specs(),
        )(
            *hub_refs(steps, skip, own, edge, other, far),
            gain_q,
            gain_k,
            packed,
            *grad_refs(outs),
        )
        sum_q[...] = sum_heads(acc_q, heads)
        sum_k[...] = sum_heads(acc_k, heads)

    @pl.when(chip != 1)
    def _():
        sum_q[...] = jnp.zeros_like(sum_q)
        sum_k[...] = jnp.zeros_like(sum_k)


def hub_cost(rows):
    return pl.CostEstimate(
        flops=rows * 60000, bytes_accessed=rows * 128 * 2 * 36, transcendentals=rows * 600
    )


def grad_shapes(slot):
    sizes = (3, 3, 6) if slot < len(CUTS) - 1 else (3, 3, 3, 3)
    return [jax.ShapeDtypeStruct((n, out_rows(slot), 128), BF16) for n in sizes]


def upper(slot, skip, heads, data, gains, after):
    steps = CUTS[slot]
    cycle = gains[0].shape[0]
    shapes = grad_shapes(slot)
    return call(
        functools.partial(upper_kernel, slot, skip, heads),
        (*data, *gains),
        [ANY] * 6,
        after,
        out_shape=shapes
        + [jax.ShapeDtypeStruct((steps * WIDE, 128), BF16)]
        + [jax.ShapeDtypeStruct((heads, 128), F32)] * 2,
        out_specs=[ANY] * (len(shapes) + 1) + [VMEM] * 2,
        scratch_shapes=[pltpu.VMEM((cycle, 128), F32)] * 2 + [pltpu.VMEM((WIDE, 2 * WIDE), F32)],
        cost_estimate=hub_cost(steps * BLOCK),
        name="upper_frames",
    )


def lower(slot, heads, data, packed, skip, gains, outs, after):
    chunk = slot - 1
    cycle = gains[0].shape[0]
    shapes = grad_shapes(slot)
    return call(
        functools.partial(lower_kernel, chunk, skip, heads),
        (*data, packed, *gains, *outs),
        [ANY] * (7 + len(outs)),
        after,
        out_shape=shapes + [jax.ShapeDtypeStruct((heads, 128), F32)] * 2,
        out_specs=[ANY] * len(shapes) + [VMEM] * 2,
        scratch_shapes=[pltpu.VMEM((cycle, 128), F32)] * 2 + [pltpu.VMEM((WIDE, WIDE), F32)],
        input_output_aliases={7 + i: i for i in range(len(outs))},
        cost_estimate=hub_cost(rows_of(chunk)),
        name="lower_frames",
    )


def blank(slot, after):
    def kernel(*refs):
        pass

    shapes = grad_shapes(slot)
    return call(
        kernel, (), [], after, out_shape=shapes, out_specs=[ANY] * len(shapes), name="blank_rows"
    )


def send(array, pairs):
    return lax.ppermute(array, "seq", pairs)


def sum_gains(part):
    count = lax.axis_size("dp")
    mine = part.shape[1] // count
    pieces = part.reshape(2, count, mine, part.shape[2])
    total = jnp.sum(lax.all_to_all(pieces, "dp", split_axis=1, concat_axis=1, tiled=True), axis=1)
    total = total + send(total, SWAP)
    total = total + send(total, MIDDLE)
    edge = send(total, BACK_S)
    chip, _ = place()
    return jnp.where((chip == 1) | (chip == 2), total, edge)


def hub_body(queries, key_proj, value_proj, out_grad, query_gain, key_gain):
    shape = queries.shape
    heads, width = shape[-2:]
    half = shape[2] // 2 * heads
    arrays = [x.reshape(2, half, width) for x in (queries, key_proj, value_proj, out_grad)]
    cycle = math.lcm(BLOCK, heads)
    chunks = len(CUTS)

    edges, grads, crossed, middle, traded = {}, {}, {}, {}, []
    sums, kept, chain = [], {-1: None}, []

    def then(token):
        chain[:] = [token]

    def trade(low, high):
        rows = halves(low, high - low, arrays, chain)
        then(rows)
        traded.append((send(rows, SWAP), low))

    def bring(chunk):
        swapped, offset = traded[min(chunk, 1)]
        rows = pack(chunk, offset, arrays, swapped, chain)
        then(rows)
        edges[chunk] = (rows, send(rows, EDGE))

    def cross(chunk):
        sources = [edges[chunk][1]] if chunk >= 0 else []
        if chunk + 1 < chunks:
            sources.append(edges[chunk + 1][0])
        if chunk == 0:
            chain.append(middle[-1])
        if chunk >= 2:
            chain.append(crossed[chunk - 2])
        rows = forward(sources, chain)
        then(rows)
        middle[chunk] = send(rows, MIDDLE)

    def data_of(chunk):
        return (*edges[chunk], middle[chunk - 1], middle[chunk])

    def skip_of(chunk):
        return 4 * rows_of(chunk - 1) if chunk else 0

    def work(slot):
        if slot < chunks:
            *parts, packed, sum_q, sum_k = upper(slot, skip_of(slot), heads, data_of(slot), gains, chain)
            crossed[slot] = send(packed, DOWN)
            sums.append((sum_q, sum_k))
        else:
            parts = blank(slot, chain)
        if slot > 0:
            chunk = slot - 1
            *parts, sum_q, sum_k = lower(
                slot, heads, data_of(chunk), crossed[chunk], skip_of(chunk), gains, parts, [sum_q] if slot < chunks else ()
            )
            sums.append((sum_q, sum_k))
        then(sum_q)
        own, other, *edge = parts
        if slot < chunks - 1:
            grads[slot] = (own, other, send(edge[0], BACK_S))
        else:
            grads[slot] = (own, send(other, SWAP), send(edge[0], BACK_S), send(edge[1], BACK_X))

    def settle_slot(slot):
        rows = out_rows(slot)
        if slot < chunks - 1:
            kernel = functools.partial(place_kernel, slot)
            *kept[slot], token = settle_rows(kernel, half, grads[slot], kept[slot - 1], 4, rows, chain)
            if slot == chunks - 2:
                grads["late"] = send(kept[slot][3], SWAP)
        else:
            outs = kept[slot - 1]
            if slot == chunks - 1:
                kernel = functools.partial(place_late_kernel, slot - 1)
                *outs, token = settle_rows(kernel, half, (grads["late"],), outs[:3], 3, half // 2, chain)
                then(token)
            kernel = functools.partial(place_last_kernel, slot)
            *kept[slot], token = settle_rows(kernel, half, grads[slot], outs, 3, rows, chain)
        then(token)

    trade(0, rows_of(0))
    bring(0)
    cross(-1)
    trade(rows_of(0), half)
    bring(1)
    both = lax.all_gather(jnp.stack([query_gain, key_gain]), "dp", axis=1, tiled=True)
    gains = [jnp.tile(both[t], (cycle // heads, 1)) for t in range(2)]
    cross(0)
    bring(2)
    for slot in range(chunks + 1):
        if slot + 1 < chunks:
            cross(slot + 1)
        if slot + 3 < chunks:
            bring(slot + 3)
        work(slot)
        if slot >= 1:
            settle_slot(slot - 1)
    for slot in range(chunks + 1 - 1, chunks + 1):
        settle_slot(slot)

    totals = jnp.stack([functools.reduce(jnp.add, [s[t] for s in sums]) for t in range(2)])
    totals = sum_gains(totals)
    return (*[x.reshape(shape) for x in kept[chunks]], totals[0], totals[1])


def wide_attention(query_norm, key_norm, value_in, grad_in):
    frames = query_norm.shape[1]
    scaling = 1.0 / math.sqrt(query_norm.shape[-1])
    scores = (
        jnp.einsum("efphd,egphd->ephfg", query_norm, key_norm, preferred_element_type=F32) * scaling
    )
    allowed = iota((frames, frames), 1) <= iota((frames, frames), 0)
    scores = jnp.where(allowed, scores, -jnp.inf)
    expo = jnp.exp(scores - jnp.max(scores, axis=-1, keepdims=True))
    probability = expo / jnp.sum(expo, axis=-1, keepdims=True)
    prob_low = probability.astype(BF16)
    attn_out = jnp.einsum("ephfg,egphd->efphd", prob_low, value_in, preferred_element_type=F32)
    row_dots = jnp.transpose(jnp.sum(grad_in.astype(F32) * attn_out, axis=-1), (0, 2, 3, 1))
    prob_grad = jnp.einsum("efphd,egphd->ephfg", grad_in, value_in, preferred_element_type=F32)
    score_low = (probability * (prob_grad - row_dots[..., None])).astype(BF16)
    query_step = jnp.einsum("ephfg,egphd->efphd", score_low, key_norm, preferred_element_type=F32)
    key_step = jnp.einsum("ephfg,efphd->egphd", score_low, query_norm, preferred_element_type=F32)
    value_step = jnp.einsum("ephfg,efphd->egphd", prob_low, grad_in, preferred_element_type=F32)
    return (
        (query_step * scaling).astype(BF16),
        (key_step * scaling).astype(BF16),
        value_step.astype(BF16),
    )


def wide_body(queries, key_proj, value_proj, out_grad, query_gain, key_gain):
    gain_q = lax.all_gather(query_gain, "dp", axis=0, tiled=True)
    gain_k = lax.all_gather(key_gain, "dp", axis=0, tiled=True)
    q_hat, q_inv = rms(queries)
    k_hat, k_inv = rms(key_proj)
    pieces = [
        lax.all_to_all(x, "seq", split_axis=2, concat_axis=1, tiled=True)
        for x in ((q_hat * gain_q).astype(BF16), (k_hat * gain_k).astype(BF16), value_proj, out_grad)
    ]
    steps = [
        lax.all_to_all(x, "seq", split_axis=1, concat_axis=2, tiled=True)
        for x in wide_attention(*pieces)
    ]
    query_grad, part_q = norm_back(steps[0], q_hat, q_inv, gain_q)
    key_grad, part_k = norm_back(steps[1], k_hat, k_inv, gain_k)
    axes = tuple(range(part_q.ndim - 2))
    totals = lax.psum((jnp.sum(part_q, axis=axes), jnp.sum(part_k, axis=axes)), "seq")
    totals = [lax.psum_scatter(t, "dp", scatter_dimension=0, tiled=True) for t in totals]
    return (query_grad, key_grad, steps[2], *totals)


def body(*args):
    frames = lax.axis_size("seq")
    patches, heads, width = args[0].shape[2:]
    rows = patches // 2 * heads
    if frames == 8 and args[0].shape[:2] == (1, 1) and width == 128 and rows == sum(CUTS) * BLOCK:
        return hub_body(*args)
    return wide_body(*args)


def solution(mesh):
    whole = P("dp", "seq", None, None, None)
    gain = P("dp", None)
    return jax.shard_map(
        body,
        mesh=mesh,
        in_specs=(whole,) * 4 + (gain,) * 2,
        out_specs=(whole,) * 3 + (gain,) * 2,
        check_vma=False,
    )
```

```python
import functools
import math

import jax
import jax.numpy as jnp
from jax import lax
from jax.experimental import pallas as pl
from jax.experimental.pallas import tpu as pltpu
from jax.sharding import PartitionSpec as P

EPSILON = 1e-06
BLOCK = 256
GROUP = 16
SLOTS = 4
WIDE = GROUP * SLOTS
TOGETHER = 128
CUTS = (3, 3, 3, 3, 3, 3, 2)
LAG = 2
DIRECT = 2

EDGE = ((0, 2), (1, 3), (6, 4), (7, 5))
MIDDLE = ((2, 4), (3, 5), (4, 2), (5, 3))
DOWN = ((4, 2), (5, 3))
BACK_S = ((2, 0), (3, 1), (4, 6), (5, 7))
BACK_X = ((2, 1), (3, 0), (4, 7), (5, 6))
SWAP = tuple((i, i ^ 1) for i in range(8))

F32 = jnp.float32
BF16 = jnp.bfloat16
ANY = pl.BlockSpec(memory_space=pl.ANY)
VMEM = pl.BlockSpec(memory_space=pltpu.VMEM)


def place():
    index = lax.axis_index("seq")
    chip, core = index // 2, index % 2
    return chip, core


def call(kernel, inputs, in_specs, after=(), **kwargs):
    count, extra = len(inputs), len(after)

    def trimmed(*refs):
        kernel(*refs[:count], *refs[count + extra :])

    return pl.pallas_call(
        trimmed,
        in_specs=list(in_specs) + [ANY] * extra,
        compiler_params=pltpu.CompilerParams(vmem_limit_bytes=56 * 1024 * 1024),
        **kwargs,
    )(*inputs, *after)


def first_of(chunk):
    return sum(CUTS[:chunk]) * BLOCK


def rows_of(chunk):
    return CUTS[chunk] * BLOCK


def chunk_of(slot, high):
    chunk = slot if high else slot - LAG
    return chunk if 0 <= chunk < len(CUTS) else None


def out_rows(slot):
    chunks = [chunk_of(slot, high) for high in (False, True)]
    return max(rows_of(chunk) for chunk in chunks if chunk is not None)


def copy_cost(rows, tensors):
    return pl.CostEstimate(flops=0, bytes_accessed=rows * 128 * 2 * 2 * tensors, transcendentals=0)


def tile_of(rows):
    return next(rows // k for k in range(2, rows) if rows % (16 * k) == 0 and rows // k <= 1024)


def stream(rows, sources, sinks, move):
    tile = tile_of(rows)

    def spec(ref):
        return pl.BlockSpec((ref.shape[0], tile, 128), lambda i: (0, i, 0))

    pltpu.emit_pipeline(
        move,
        grid=(rows // tile,),
        in_specs=[spec(ref) for ref in sources],
        out_specs=[spec(ref) for ref in sinks],
    )(*sources, *sinks)


def window(ref, index, start, rows, count=1):
    return ref.at[pl.ds(index, count), pl.ds(start, rows)]


def halves_kernel(start, rows, q, k, v, g, out):
    _, core = place()

    def move(*blocks):
        for t in range(4):
            blocks[4][t] = blocks[t][0]

    stream(rows, [window(ref, 1 - core, start, rows) for ref in (q, k, v, g)], [out], move)


def halves(start, rows, arrays, after):
    return call(
        functools.partial(halves_kernel, start, rows),
        arrays,
        [ANY] * 4,
        after,
        out_shape=jax.ShapeDtypeStruct((4, rows, 128), BF16),
        out_specs=ANY,
        cost_estimate=copy_cost(rows, 4),
        name="other_half",
    )


def pack_kernel(start, rows, offset, q, k, v, g, x, edge):
    chip, core = place()

    def run(order):
        def move(*blocks):
            sent = blocks[8]
            for pair in range(2):
                for t in range(2):
                    for frame in range(2):
                        sent[4 * pair + 2 * frame + t] = blocks[4 * frame + 2 * pair + t][0]

        own = [window((q, k, v, g)[t], core, start, rows) for t in order]
        other = [window(x, t, start - offset, rows) for t in order]
        stream(rows, own + other, [edge], move)

    @pl.when(chip < 2)
    def _():
        run((1, 2, 0, 3))

    @pl.when(chip >= 2)
    def _():
        run((0, 3, 1, 2))


def pack(chunk, offset, arrays, swapped, after):
    rows = rows_of(chunk)
    return call(
        functools.partial(pack_kernel, first_of(chunk), rows, offset),
        (*arrays, swapped),
        [ANY] * 5,
        after,
        out_shape=jax.ShapeDtypeStruct((8, rows, 128), BF16),
        out_specs=ANY,
        cost_estimate=copy_cost(rows, 8),
        name="pack_rows",
    )


def forward_kernel(sizes, *refs):
    sources, out = refs[:-1], refs[-1]
    chip, _ = place()

    def move(src, *dsts):
        for q, dst in enumerate(dsts):
            dst[...] = src[q]

    @pl.when((chip == 1) | (chip == 2))
    def _():
        start = 0
        for rows, src in zip(sizes, sources):
            if len(src.shape) == 2:
                pltpu.emit_pipeline(
                    copy_all,
                    grid=(1,),
                    in_specs=[pl.BlockSpec((rows, 128), lambda i: (0, 0))],
                    out_specs=[pl.BlockSpec((rows, 128), lambda i: (0, 0))],
                )(src, out.at[pl.ds(start, rows)])
                continue
            tile = tile_of(rows)
            pltpu.emit_pipeline(
                move,
                grid=(rows // tile,),
                in_specs=[pl.BlockSpec((4, tile, 128), lambda i: (0, i, 0))],
                out_specs=[pl.BlockSpec((tile, 128), lambda i: (i, 0))] * 4,
            )(src, *[out.at[pl.ds(start + q * rows, rows)] for q in range(4)])
            start += 4 * rows


def forward(sources, after):
    sizes = [x.shape[-2] for x in sources]
    total = sum(n if x.ndim == 2 else 4 * n for n, x in zip(sizes, sources))
    return call(
        functools.partial(forward_kernel, sizes),
        sources,
        [ANY] * len(sources),
        after,
        out_shape=jax.ShapeDtypeStruct((total, 128), BF16),
        out_specs=ANY,
        cost_estimate=copy_cost(sum(sizes), 4),
        name="forward_rows",
    )


def copy_three(src, *dsts):
    for t, dst in enumerate(dsts):
        dst[0] = src[t]


def copy_all(src, dst):
    dst[...] = src[...]


def by_chip(slot, run):
    chip, _ = place()
    for which in range(4):
        chunk = chunk_of(slot, which >= 2)
        if chunk is not None:
            pl.when(chip == which)(functools.partial(run, chunk, which in (1, 2)))


def place_kernel(slot, own, other, back, *refs):
    outs, late, token = refs[-5:-2], refs[-2], refs[-1]
    token[...] = jnp.zeros_like(token)
    _, core = place()

    def run(chunk, hub):
        start, rows = first_of(chunk), rows_of(chunk)
        near = own.at[:, pl.ds(0, rows)] if hub else window(back, 0, 0, rows, 3)
        far = other.at[:, pl.ds(0, rows)] if hub else window(back, 3, 0, rows, 3)
        stream(rows, [near], [window(out, core, start, rows) for out in outs], copy_three)
        stream(rows, [far], [window(late, 0, start, rows, 3)], copy_all)

    by_chip(slot, run)


def place_last_kernel(slot, own, other, back_s, back_x, *refs):
    outs, token = refs[-4:-1], refs[-1]
    token[...] = jnp.zeros_like(token)
    _, core = place()

    def run(chunk, hub):
        start, rows = first_of(chunk), rows_of(chunk)
        for half, src in ((core, own if hub else back_s), (1 - core, other if hub else back_x)):
            sinks = [window(out, half, start, rows) for out in outs]
            stream(rows, [src.at[:, pl.ds(0, rows)]], sinks, copy_three)

    by_chip(slot, run)


def place_late_kernel(slot, late, *refs):
    outs, token = refs[-4:-1], refs[-1]
    token[...] = jnp.zeros_like(token)
    chip, core = place()

    def run(rows):
        sinks = [window(out, 1 - core, 0, rows) for out in outs]
        stream(rows, [window(late, 0, 0, rows, 3)], sinks, copy_three)

    @pl.when(chip < 2)
    def _():
        run(first_of(slot - LAG + 1))

    @pl.when(chip >= 2)
    def _():
        run(first_of(min(slot + 1, len(CUTS))))


def settle_rows(kernel, half, pieces, kept, count, rows, after=()):
    kept = kept or ()
    return call(
        kernel,
        (*pieces, *kept),
        [ANY] * (len(pieces) + len(kept)),
        after,
        out_shape=[jax.ShapeDtypeStruct((n, half, 128), BF16) for n in (2, 2, 2, 3)[:count]]
        + [jax.ShapeDtypeStruct((8, 128), F32)],
        out_specs=[ANY] * count + [VMEM],
        input_output_aliases={len(pieces) + i: i for i in range(len(kept))},
        cost_estimate=copy_cost(rows, 6),
        name="place_rows",
    )


def rms(values):
    wide = values.astype(F32)
    inverse = lax.rsqrt(jnp.mean(wide * wide, axis=-1, keepdims=True) + EPSILON)
    return wide * inverse, inverse


def norm_back(step, hat, inverse, gain):
    wide = step.astype(F32)
    gained = gain * wide
    result = inverse * (gained - hat * jnp.mean(gained * hat, axis=-1, keepdims=True))
    return result.astype(BF16), wide * hat


def mul_t(a, b):
    return lax.dot_general(a, b, (((1,), (1,)), ((), ())), preferred_element_type=F32)


def t_mul(a, b):
    return lax.dot_general(a, b, (((0,), (0,)), ((), ())), preferred_element_type=F32)


def mul(a, b):
    return jnp.dot(a, b, preferred_element_type=F32)


def iota(shape, axis):
    return lax.broadcasted_iota(jnp.int32, shape, axis)


def frame_of(slot, core, upper):
    cross = slot % 2
    side = slot // 2
    side = side if upper else 1 - side
    return 2 * side + cross + core - 2 * cross * core


def causal(core, upper):
    shape = (WIDE, 2 * WIDE if upper else WIDE)
    rows, cols = iota(shape, 0), iota(shape, 1)
    key = cols // GROUP
    frame = frame_of(key % SLOTS, core, upper)
    if upper:
        frame = jnp.where(key < SLOTS, -1, frame)
    late = frame <= frame_of(rows // GROUP, core, upper)
    return (rows % GROUP == cols % GROUP) & late


def cat(parts):
    return jnp.concatenate(parts, axis=0)


def tiled(gain):
    return cat([gain] * SLOTS)


def group(wide, j):
    slots = wide.shape[0] // TOGETHER
    return cat([wide[s * TOGETHER + j * GROUP :][:GROUP] for s in range(slots)])


def ungroup(parts):
    return cat([part[s * GROUP :][:GROUP] for s in range(SLOTS) for part in parts])


def fold(acc, rows, part):
    total = part[:TOGETHER]
    for s in range(1, SLOTS):
        total = total + part[s * TOGETHER :][:TOGETHER]
    acc[rows, :] += total


def settle(outs, rows, parts):
    for t, part in enumerate(parts):
        for s, out in enumerate(outs):
            out[t, rows, :] = part[s * TOGETHER :][:TOGETHER]


def sum_heads(acc, heads):
    total = acc[0:heads, :]
    for i in range(1, acc.shape[0] // heads):
        total = total + acc[i * heads : (i + 1) * heads, :]
    return total


def read(refs, t, rows):
    return cat([ref[2 * x + t, rows, :] for ref in refs for x in range(2)])


def read_met(near, far, t, rows):
    return cat([side[2 * x + t][rows, :] for side in (near, far) for x in range(2)])


def hub_specs(steps):
    four = lambda n: pl.BlockSpec((4, BLOCK, 128), lambda i: (n, i, 0))
    flat = lambda q: pl.BlockSpec((BLOCK, 128), lambda i: (q * steps + i, 0))
    return [four(0), four(1), four(0), four(1)] + [flat(q) for q in range(4)] * 2


def hub_refs(steps, skip, own, edge, other, far):
    rows = 4 * steps * BLOCK
    return [own, own, edge, edge] + [other.at[pl.ds(skip, rows)]] * 4 + [far.at[pl.ds(0, rows)]] * 4


def grad_specs():
    return [pl.BlockSpec((3, BLOCK, 128), lambda i: (0, i, 0))] * 4


def grad_refs(outs):
    if len(outs) == 4:
        return list(outs)
    return [outs[0], outs[1], outs[2].at[pl.ds(0, 3)], outs[2].at[pl.ds(3, 3)]]


def gain_spec(first, cycle):
    return pl.BlockSpec((BLOCK, 128), lambda i: ((first + i) % cycle, 0))


def attend(qn, kn, grad, value, allowed):
    scaling = 1.0 / math.sqrt(qn.shape[-1])
    count = TOGETHER // GROUP
    scores = cat([mul_t(group(qn, j), group(kn, j)) for j in range(count)])
    prob_grad = cat([mul_t(group(grad, j), group(value, j)) for j in range(count)])
    mask = cat([allowed] * count)
    scores = jnp.where(mask > 0, scores * scaling, -jnp.inf)
    expo = jnp.exp(scores - jnp.max(scores, axis=-1, keepdims=True))
    prob = expo * (1.0 / jnp.sum(expo, axis=-1, keepdims=True))
    prob_low = prob.astype(BF16)
    dots = jnp.sum(prob_low.astype(F32) * prob_grad, axis=-1, keepdims=True)
    score_low = (prob * (prob_grad - dots)).astype(BF16)
    split = lambda x: [x[j * WIDE :][:WIDE] for j in range(count)]
    return split(prob_low), split(score_low)


def upper_kernel(chunk, skip, heads, own, edge, other, far, gain_q, gain_k, *refs):
    outs, (packed, sum_q, sum_k, acc_q, acc_k, mask) = refs[:-6], refs[-6:]
    chip, core = place()
    first, steps = sum(CUTS[:chunk]), CUTS[chunk]
    count = TOGETHER // GROUP
    cycle = acc_q.shape[0] // BLOCK

    def block(own_a, own_b, edge_a, edge_b, *refs):
        other, far, (gain_q, gain_k), out, pack_ref = refs[:4], refs[4:8], refs[8:10], refs[10:14], refs[14]
        base = ((first + pl.program_id(0)) % cycle) * BLOCK
        scaling = 1.0 / math.sqrt(128)
        lanes = iota((WIDE, 128), 1) // 8
        spread_r, spread_c = iota((2 * WIDE, 128), 0), iota((2 * WIDE, 128), 1)
        spread = jnp.where(spread_r // GROUP == spread_c % 8, 1.0, 0.0).astype(BF16)

        def some(i, total):
            rows = pl.ds(pl.multiple_of(i * TOGETHER, TOGETHER), TOGETHER)
            place = pl.ds(pl.multiple_of(base + i * TOGETHER, TOGETHER), TOGETHER)
            gq, gk = tiled(gain_q[rows, :]), tiled(gain_k[rows, :])
            q_hat, q_inv = rms(read((own_a, edge_a), 0, rows))
            grad = read((own_a, edge_a), 1, rows)
            kl_hat, _ = rms(read_met(other, far, 0, rows))
            ku_hat, ku_inv = rms(read((own_b, edge_b), 0, rows))
            value = cat([read_met(other, far, 1, rows), read((own_b, edge_b), 1, rows)])
            qn = (q_hat * gq).astype(BF16)
            kn = cat([(kl_hat * gk).astype(BF16), (ku_hat * gk).astype(BF16)])
            prob, score = attend(qn, kn, grad, value, mask[...])
            q_step = ungroup([mul(score[j], group(kn, j)) for j in range(count)])
            k_step = ungroup([t_mul(score[j][:, WIDE:], group(qn, j)) for j in range(count)])
            v_step = ungroup([t_mul(prob[j][:, WIDE:], group(grad, j)) for j in range(count)])
            q_step, k_step = (q_step * scaling).astype(BF16), (k_step * scaling).astype(BF16)
            dq, part_q = norm_back(q_step, q_hat, q_inv, gq)
            dk, part_k = norm_back(k_step, ku_hat, ku_inv, gk)
            settle(out, rows, (dq, dk, v_step.astype(BF16)))
            fold(acc_q, place, part_q)
            fold(acc_k, place, part_k)
            for j in range(count):
                cross = jnp.concatenate([prob[j][:, :WIDE], score[j][:, :WIDE]], axis=1)
                total = jnp.where(lanes == i * count + j, mul(cross, spread), total)
            return total

        total = lax.fori_loop(0, BLOCK // TOGETHER, some, jnp.zeros((WIDE, 128), F32))
        pack_ref[...] = total.astype(BF16)

    @pl.when(chip == 2)
    def _():
        acc_q[...] = jnp.zeros_like(acc_q)
        acc_k[...] = jnp.zeros_like(acc_k)
        mask[...] = causal(core, True).astype(F32)
        pltpu.emit_pipeline(
            block,
            grid=(steps,),
            in_specs=hub_specs(steps) + [gain_spec(first, cycle)] * 2,
            out_specs=grad_specs() + [pl.BlockSpec((WIDE, 128), lambda i: (i, 0))],
        )(*hub_refs(steps, skip, own, edge, other, far), gain_q, gain_k, *grad_refs(outs), packed)
        sum_q[...] = sum_heads(acc_q, heads)
        sum_k[...] = sum_heads(acc_k, heads)

    @pl.when(chip != 2)
    def _():
        sum_q[...] = jnp.zeros_like(sum_q)
        sum_k[...] = jnp.zeros_like(sum_k)


def lower_kernel(chunk, skip, at, heads, own, edge, other, far, packed, gain_q, gain_k, *refs):
    outs, (sum_q, sum_k, acc_q, acc_k, mask) = refs[:-5], refs[-5:]
    outs = outs[len(outs) // 2 :]
    chip, core = place()
    first, steps = sum(CUTS[:chunk]), CUTS[chunk]
    count = TOGETHER // GROUP
    cycle = acc_q.shape[0] // BLOCK

    def block(own_a, own_b, edge_a, edge_b, *refs):
        other, far, (gain_q, gain_k, pack_ref), out = refs[:4], refs[4:8], refs[8:11], refs[11:]
        base = ((first + pl.program_id(0)) % cycle) * BLOCK
        both = iota((WIDE, 2 * WIDE), 0) % GROUP == iota((WIDE, 2 * WIDE), 1) % GROUP
        scaling = 1.0 / math.sqrt(128)
        lanes = iota((WIDE, 128), 1) // 8
        spread_r, spread_c = iota((128, 2 * WIDE), 0), iota((128, 2 * WIDE), 1)
        spread = jnp.where(spread_c // GROUP == spread_r % 8, 1.0, 0.0).astype(BF16)
        crossed = pack_ref[...].astype(F32)

        def some(i, carry):
            rows = pl.ds(pl.multiple_of(i * TOGETHER, TOGETHER), TOGETHER)
            place = pl.ds(pl.multiple_of(base + i * TOGETHER, TOGETHER), TOGETHER)
            gq, gk = tiled(gain_q[rows, :]), tiled(gain_k[rows, :])
            k_hat, k_inv = rms(read((own_a, edge_a), 0, rows))
            value = read((own_a, edge_a), 1, rows)
            q_hat, q_inv = rms(read((own_b, edge_b), 0, rows))
            grad = read((own_b, edge_b), 1, rows)
            qu_hat, _ = rms(read_met(other, far, 0, rows))
            grad_u = read_met(other, far, 1, rows)
            kn = (k_hat * gk).astype(BF16)
            qn = (q_hat * gq).astype(BF16)
            qn_u = (qu_hat * gq).astype(BF16)
            prob, score = attend(qn, kn, grad, value, mask[...])
            cross = []
            for j in range(count):
                mine = jnp.where(lanes == i * count + j, crossed, 0.0).astype(BF16)
                cross.append(jnp.where(both, mul(mine, spread), 0.0).astype(BF16))
            q_step = ungroup([mul(score[j], group(kn, j)) for j in range(count)])
            k_step = ungroup(
                [
                    t_mul(cat([score[j], cross[j][:, WIDE:]]), cat([group(qn, j), group(qn_u, j)]))
                    for j in range(count)
                ]
            )
            v_step = ungroup(
                [
                    t_mul(cat([prob[j], cross[j][:, :WIDE]]), cat([group(grad, j), group(grad_u, j)]))
                    for j in range(count)
                ]
            )
            q_step, k_step = (q_step * scaling).astype(BF16), (k_step * scaling).astype(BF16)
            dq, part_q = norm_back(q_step, q_hat, q_inv, gq)
            dk, part_k = norm_back(k_step, k_hat, k_inv, gk)
            settle(out, rows, (dq, dk, v_step.astype(BF16)))
            fold(acc_q, place, part_q)
            fold(acc_k, place, part_k)
            return carry

        lax.fori_loop(0, BLOCK // TOGETHER, some, 0)

    @pl.when(chip == 1)
    def _():
        acc_q[...] = jnp.zeros_like(acc_q)
        acc_k[...] = jnp.zeros_like(acc_k)
        mask[...] = causal(core, False).astype(F32)
        pltpu.emit_pipeline(
            block,
            grid=(steps,),
            in_specs=hub_specs(steps)
            + [gain_spec(first, cycle)] * 2
            + [pl.BlockSpec((WIDE, 128), lambda i: (i, 0))],
            out_specs=grad_specs(),
        )(
            *hub_refs(steps, skip, own, edge, other, far),
            gain_q,
            gain_k,
            packed.at[pl.ds(at, steps * WIDE)],
            *grad_refs(outs),
        )
        sum_q[...] = sum_heads(acc_q, heads)
        sum_k[...] = sum_heads(acc_k, heads)

    @pl.when(chip != 1)
    def _():
        sum_q[...] = jnp.zeros_like(sum_q)
        sum_k[...] = jnp.zeros_like(sum_k)


def hub_cost(rows):
    return pl.CostEstimate(
        flops=rows * 60000, bytes_accessed=rows * 128 * 2 * 36, transcendentals=rows * 600
    )


def grad_shapes(slot):
    sizes = (3, 3, 6) if slot < len(CUTS) + LAG - DIRECT else (3, 3, 3, 3)
    return [jax.ShapeDtypeStruct((n, out_rows(slot), 128), BF16) for n in sizes]


def upper(slot, skip, heads, data, gains, after):
    steps = CUTS[slot]
    cycle = gains[0].shape[0]
    shapes = grad_shapes(slot)
    return call(
        functools.partial(upper_kernel, slot, skip, heads),
        (*data, *gains),
        [ANY] * 6,
        after,
        out_shape=shapes
        + [jax.ShapeDtypeStruct((steps * WIDE, 128), BF16)]
        + [jax.ShapeDtypeStruct((heads, 128), F32)] * 2,
        out_specs=[ANY] * (len(shapes) + 1) + [VMEM] * 2,
        scratch_shapes=[pltpu.VMEM((cycle, 128), F32)] * 2 + [pltpu.VMEM((WIDE, 2 * WIDE), F32)],
        cost_estimate=hub_cost(steps * BLOCK),
        name="upper_frames",
    )


def lower(slot, heads, data, packed, at, skip, gains, outs, after):
    chunk = slot - LAG
    cycle = gains[0].shape[0]
    shapes = grad_shapes(slot)
    return call(
        functools.partial(lower_kernel, chunk, skip, at, heads),
        (*data, packed, *gains, *outs),
        [ANY] * (7 + len(outs)),
        after,
        out_shape=shapes + [jax.ShapeDtypeStruct((heads, 128), F32)] * 2,
        out_specs=[ANY] * len(shapes) + [VMEM] * 2,
        scratch_shapes=[pltpu.VMEM((cycle, 128), F32)] * 2 + [pltpu.VMEM((WIDE, WIDE), F32)],
        input_output_aliases={7 + i: i for i in range(len(outs))},
        cost_estimate=hub_cost(rows_of(chunk)),
        name="lower_frames",
    )


def blank(slot, after):
    def kernel(*refs):
        pass

    shapes = grad_shapes(slot)
    return call(
        kernel, (), [], after, out_shape=shapes, out_specs=[ANY] * len(shapes), name="blank_rows"
    )


def send(array, pairs):
    return lax.ppermute(array, "seq", pairs)


def add_pieces(pieces, after):
    def kernel(src, out):
        total = src[:, 0]
        for i in range(1, src.shape[1]):
            total = total + src[:, i]
        out[...] = total

    shape = (pieces.shape[0], *pieces.shape[2:])
    return call(
        kernel, (pieces,), [VMEM], after, out_shape=jax.ShapeDtypeStruct(shape, F32), out_specs=VMEM, name="add_pieces"
    )


def sum_gains(part, after):
    count = lax.axis_size("dp")
    mine = part.shape[1] // count
    pieces = part.reshape(2, count, mine, part.shape[2])
    total = add_pieces(lax.all_to_all(pieces, "dp", split_axis=1, concat_axis=1, tiled=True), after)
    total = total + send(total, SWAP)
    total = total + send(total, MIDDLE)
    edge = send(total, BACK_S)
    chip, _ = place()
    return jnp.where((chip == 1) | (chip == 2), total, edge)


def hub_body(queries, key_proj, value_proj, out_grad, query_gain, key_gain):
    shape = queries.shape
    heads, width = shape[-2:]
    half = shape[2] // 2 * heads
    arrays = [x.reshape(2, half, width) for x in (queries, key_proj, value_proj, out_grad)]
    cycle = math.lcm(BLOCK, heads)
    chunks = len(CUTS)

    edges, grads, crossed, middle, packs, traded = {}, {}, {}, {}, {}, []
    slots = chunks + LAG
    sums, kept, chain = [], {-1: None}, []

    def then(token):
        chain[:] = [token]

    def trade(low, high):
        rows = halves(low, high - low, arrays, chain)
        then(rows)
        traded.append((send(rows, SWAP), low))

    def bring(chunk):
        swapped, offset = traded[min(chunk, 2)]
        rows = pack(chunk, offset, arrays, swapped, chain)
        then(rows)
        edges[chunk] = (rows, send(rows, EDGE))

    def cross(chunk):
        sources = [edges[chunk][1]] if chunk >= 0 else []
        if chunk + 1 < chunks:
            sources.append(edges[chunk + 1][0])
        if chunk >= LAG:
            sources.append(packs[chunk - LAG])
            crossed[chunk - LAG] = (chunk, sum(4 * x.shape[1] for x in sources[:-1]))
        if chunk == 0:
            chain.append(middle[-1])
        rows = forward(sources, chain)
        then(rows)
        middle[chunk] = send(rows, MIDDLE)

    def data_of(chunk):
        return (*edges[chunk], middle[chunk - 1], middle[chunk])

    def skip_of(chunk):
        return 4 * rows_of(chunk - 1) if chunk else 0

    def work(slot):
        if slot < chunks:
            *parts, packs[slot], sum_q, sum_k = upper(
                slot, skip_of(slot), heads, data_of(slot), gains, chain
            )
            if slot >= chunks - LAG:
                packs[slot] = send(packs[slot], DOWN)
            sums.append((sum_q, sum_k))
        else:
            parts = blank(slot, chain)
        if slot >= LAG:
            chunk = slot - LAG
            packed, at = packs[chunk], 0
            if chunk in crossed:
                packed, at = middle[crossed[chunk][0]], crossed[chunk][1]
            after = [sum_q] if slot < chunks else []
            *parts, sum_q, sum_k = lower(
                slot, heads, data_of(chunk), packed, at, skip_of(chunk), gains, parts, after
            )
            sums.append((sum_q, sum_k))
        then(sum_q)
        own, other, *edge = parts
        if slot < slots - DIRECT:
            grads[slot] = (own, other, send(edge[0], BACK_S))
        else:
            grads[slot] = (own, send(other, SWAP), send(edge[0], BACK_S), send(edge[1], BACK_X))

    def settle_slot(slot):
        rows = out_rows(slot)
        if slot < slots - DIRECT:
            kernel = functools.partial(place_kernel, slot)
            *kept[slot], token = settle_rows(kernel, half, grads[slot], kept[slot - 1], 4, rows, chain)
            if slot == slots - DIRECT - 1:
                grads["late"] = send(kept[slot][3], SWAP)
        else:
            outs = kept[slot - 1]
            if slot == slots - DIRECT:
                kernel = functools.partial(place_late_kernel, slot - 1)
                *outs, token = settle_rows(kernel, half, (grads["late"],), outs[:3], 3, half // 2, chain)
                then(token)
            kernel = functools.partial(place_last_kernel, slot)
            *kept[slot], token = settle_rows(kernel, half, grads[slot], outs, 3, rows, chain)
        then(token)

    trade(0, rows_of(0))
    bring(0)
    trade(rows_of(0), first_of(2))
    cross(-1)
    bring(1)
    both = lax.all_gather(jnp.stack([query_gain, key_gain]), "dp", axis=1, tiled=True)
    gains = [jnp.tile(both[t], (cycle // heads, 1)) for t in range(2)]
    cross(0)
    trade(first_of(2), half)
    bring(2)
    for slot in range(slots):
        if slot + 1 < chunks:
            cross(slot + 1)
        if slot + 3 < chunks:
            bring(slot + 3)
        work(slot)
        if slot >= 1:
            settle_slot(slot - 1)
    for slot in range(slots - 1, slots):
        settle_slot(slot)

    totals = jnp.stack([functools.reduce(jnp.add, [s[t] for s in sums]) for t in range(2)])
    totals = sum_gains(totals, chain)
    return (*[x.reshape(shape) for x in kept[slots - 1]], totals[0], totals[1])


def wide_attention(query_norm, key_norm, value_in, grad_in):
    frames = query_norm.shape[1]
    scaling = 1.0 / math.sqrt(query_norm.shape[-1])
    scores = (
        jnp.einsum("efphd,egphd->ephfg", query_norm, key_norm, preferred_element_type=F32) * scaling
    )
    allowed = iota((frames, frames), 1) <= iota((frames, frames), 0)
    scores = jnp.where(allowed, scores, -jnp.inf)
    expo = jnp.exp(scores - jnp.max(scores, axis=-1, keepdims=True))
    probability = expo / jnp.sum(expo, axis=-1, keepdims=True)
    prob_low = probability.astype(BF16)
    attn_out = jnp.einsum("ephfg,egphd->efphd", prob_low, value_in, preferred_element_type=F32)
    row_dots = jnp.transpose(jnp.sum(grad_in.astype(F32) * attn_out, axis=-1), (0, 2, 3, 1))
    prob_grad = jnp.einsum("efphd,egphd->ephfg", grad_in, value_in, preferred_element_type=F32)
    score_low = (probability * (prob_grad - row_dots[..., None])).astype(BF16)
    query_step = jnp.einsum("ephfg,egphd->efphd", score_low, key_norm, preferred_element_type=F32)
    key_step = jnp.einsum("ephfg,efphd->egphd", score_low, query_norm, preferred_element_type=F32)
    value_step = jnp.einsum("ephfg,efphd->egphd", prob_low, grad_in, preferred_element_type=F32)
    return (
        (query_step * scaling).astype(BF16),
        (key_step * scaling).astype(BF16),
        value_step.astype(BF16),
    )


def wide_body(queries, key_proj, value_proj, out_grad, query_gain, key_gain):
    gain_q = lax.all_gather(query_gain, "dp", axis=0, tiled=True)
    gain_k = lax.all_gather(key_gain, "dp", axis=0, tiled=True)
    q_hat, q_inv = rms(queries)
    k_hat, k_inv = rms(key_proj)
    pieces = [
        lax.all_to_all(x, "seq", split_axis=2, concat_axis=1, tiled=True)
        for x in ((q_hat * gain_q).astype(BF16), (k_hat * gain_k).astype(BF16), value_proj, out_grad)
    ]
    steps = [
        lax.all_to_all(x, "seq", split_axis=1, concat_axis=2, tiled=True)
        for x in wide_attention(*pieces)
    ]
    query_grad, part_q = norm_back(steps[0], q_hat, q_inv, gain_q)
    key_grad, part_k = norm_back(steps[1], k_hat, k_inv, gain_k)
    axes = tuple(range(part_q.ndim - 2))
    totals = lax.psum((jnp.sum(part_q, axis=axes), jnp.sum(part_k, axis=axes)), "seq")
    totals = [lax.psum_scatter(t, "dp", scatter_dimension=0, tiled=True) for t in totals]
    return (query_grad, key_grad, steps[2], *totals)


def body(*args):
    frames = lax.axis_size("seq")
    patches, heads, width = args[0].shape[2:]
    rows = patches // 2 * heads
    if frames == 8 and args[0].shape[:2] == (1, 1) and width == 128 and rows == sum(CUTS) * BLOCK:
        return hub_body(*args)
    return wide_body(*args)


def solution(mesh):
    whole = P("dp", "seq", None, None, None)
    gain = P("dp", None)
    return jax.shard_map(
        body,
        mesh=mesh,
        in_specs=(whole,) * 4 + (gain,) * 2,
        out_specs=(whole,) * 3 + (gain,) * 2,
        check_vma=False,
    )
```

```python
import functools
import math

import jax
import jax.numpy as jnp
from jax import lax
from jax.experimental import pallas as pl
from jax.experimental.pallas import tpu as pltpu
from jax.sharding import PartitionSpec as P

EPSILON = 1e-06
BLOCK = 256
GROUP = 16
SLOTS = 4
WIDE = GROUP * SLOTS
TOGETHER = 256
CUTS = (2, 2, 2, 2, 2, 2, 2, 2, 2, 2)
LAG = 2
DIRECT = 2

EDGE = ((0, 2), (1, 3), (6, 4), (7, 5))
MIDDLE = ((2, 4), (3, 5), (4, 2), (5, 3))
DOWN = ((4, 2), (5, 3))
BACK_S = ((2, 0), (3, 1), (4, 6), (5, 7))
BACK_X = ((2, 1), (3, 0), (4, 7), (5, 6))
SWAP = tuple((i, i ^ 1) for i in range(8))

F32 = jnp.float32
BF16 = jnp.bfloat16
ANY = pl.BlockSpec(memory_space=pl.ANY)
VMEM = pl.BlockSpec(memory_space=pltpu.VMEM)


def place():
    index = lax.axis_index("seq")
    chip, core = index // 2, index % 2
    return chip, core


def call(kernel, inputs, in_specs, after=(), **kwargs):
    count, extra = len(inputs), len(after)

    def trimmed(*refs):
        kernel(*refs[:count], *refs[count + extra :])

    return pl.pallas_call(
        trimmed,
        in_specs=list(in_specs) + [ANY] * extra,
        compiler_params=pltpu.CompilerParams(vmem_limit_bytes=56 * 1024 * 1024),
        **kwargs,
    )(*inputs, *after)


def first_of(chunk):
    return sum(CUTS[:chunk]) * BLOCK


def rows_of(chunk):
    return CUTS[chunk] * BLOCK


def chunk_of(slot, high):
    chunk = slot if high else slot - LAG
    return chunk if 0 <= chunk < len(CUTS) else None


def out_rows(slot):
    chunks = [chunk_of(slot, high) for high in (False, True)]
    return max(rows_of(chunk) for chunk in chunks if chunk is not None)


def copy_cost(rows, tensors):
    return pl.CostEstimate(flops=0, bytes_accessed=rows * 128 * 2 * 2 * tensors, transcendentals=0)


def tile_of(rows):
    return next(rows // k for k in range(2, rows) if rows % (16 * k) == 0 and rows // k <= 1024)


def stream(rows, sources, sinks, move):
    tile = tile_of(rows)

    def spec(ref):
        return pl.BlockSpec((ref.shape[0], tile, 128), lambda i: (0, i, 0))

    pltpu.emit_pipeline(
        move,
        grid=(rows // tile,),
        in_specs=[spec(ref) for ref in sources],
        out_specs=[spec(ref) for ref in sinks],
    )(*sources, *sinks)


def window(ref, index, start, rows, count=1):
    return ref.at[pl.ds(index, count), pl.ds(start, rows)]


def halves_kernel(start, rows, q, k, v, g, out):
    _, core = place()

    def move(*blocks):
        for t in range(4):
            blocks[4][t] = blocks[t][0]

    stream(rows, [window(ref, 1 - core, start, rows) for ref in (q, k, v, g)], [out], move)


def halves(start, rows, arrays, after):
    return call(
        functools.partial(halves_kernel, start, rows),
        arrays,
        [ANY] * 4,
        after,
        out_shape=jax.ShapeDtypeStruct((4, rows, 128), BF16),
        out_specs=ANY,
        cost_estimate=copy_cost(rows, 4),
        name="other_half",
    )


def pack_kernel(start, rows, offset, q, k, v, g, x, edge):
    chip, core = place()

    def run(order):
        def move(*blocks):
            sent = blocks[8]
            for pair in range(2):
                for t in range(2):
                    for frame in range(2):
                        sent[4 * pair + 2 * frame + t] = blocks[4 * frame + 2 * pair + t][0]

        own = [window((q, k, v, g)[t], core, start, rows) for t in order]
        other = [window(x, t, start - offset, rows) for t in order]
        stream(rows, own + other, [edge], move)

    @pl.when(chip < 2)
    def _():
        run((1, 2, 0, 3))

    @pl.when(chip >= 2)
    def _():
        run((0, 3, 1, 2))


def pack(chunk, offset, arrays, swapped, after):
    rows = rows_of(chunk)
    return call(
        functools.partial(pack_kernel, first_of(chunk), rows, offset),
        (*arrays, swapped),
        [ANY] * 5,
        after,
        out_shape=jax.ShapeDtypeStruct((8, rows, 128), BF16),
        out_specs=ANY,
        cost_estimate=copy_cost(rows, 8),
        name="pack_rows",
    )


def forward_kernel(sizes, *refs):
    sources, out = refs[:-1], refs[-1]
    chip, _ = place()

    def move(src, *dsts):
        for q, dst in enumerate(dsts):
            dst[...] = src[q]

    @pl.when((chip == 1) | (chip == 2))
    def _():
        start = 0
        for rows, src in zip(sizes, sources):
            if len(src.shape) == 2:
                pltpu.emit_pipeline(
                    copy_all,
                    grid=(1,),
                    in_specs=[pl.BlockSpec((rows, 128), lambda i: (0, 0))],
                    out_specs=[pl.BlockSpec((rows, 128), lambda i: (0, 0))],
                )(src, out.at[pl.ds(start, rows)])
                continue
            tile = tile_of(rows)
            pltpu.emit_pipeline(
                move,
                grid=(rows // tile,),
                in_specs=[pl.BlockSpec((4, tile, 128), lambda i: (0, i, 0))],
                out_specs=[pl.BlockSpec((tile, 128), lambda i: (i, 0))] * 4,
            )(src, *[out.at[pl.ds(start + q * rows, rows)] for q in range(4)])
            start += 4 * rows


def forward(sources, after):
    sizes = [x.shape[-2] for x in sources]
    total = sum(n if x.ndim == 2 else 4 * n for n, x in zip(sizes, sources))
    return call(
        functools.partial(forward_kernel, sizes),
        sources,
        [ANY] * len(sources),
        after,
        out_shape=jax.ShapeDtypeStruct((total, 128), BF16),
        out_specs=ANY,
        cost_estimate=copy_cost(sum(sizes), 4),
        name="forward_rows",
    )


def copy_three(src, *dsts):
    for t, dst in enumerate(dsts):
        dst[0] = src[t]


def copy_all(src, dst):
    dst[...] = src[...]


def by_chip(slot, run):
    chip, _ = place()
    for which in range(4):
        chunk = chunk_of(slot, which >= 2)
        if chunk is not None:
            pl.when(chip == which)(functools.partial(run, chunk, which in (1, 2)))


def place_kernel(slot, own, other, back, *refs):
    outs, late, token = refs[-5:-2], refs[-2], refs[-1]
    token[...] = jnp.zeros_like(token)
    _, core = place()

    def run(chunk, hub):
        start, rows = first_of(chunk), rows_of(chunk)
        near = own.at[:, pl.ds(0, rows)] if hub else window(back, 0, 0, rows, 3)
        far = other.at[:, pl.ds(0, rows)] if hub else window(back, 3, 0, rows, 3)
        stream(rows, [near], [window(out, core, start, rows) for out in outs], copy_three)
        stream(rows, [far], [window(late, 0, start, rows, 3)], copy_all)

    by_chip(slot, run)


def place_last_kernel(slot, own, other, back_s, back_x, *refs):
    outs, token = refs[-4:-1], refs[-1]
    token[...] = jnp.zeros_like(token)
    _, core = place()

    def run(chunk, hub):
        start, rows = first_of(chunk), rows_of(chunk)
        for half, src in ((core, own if hub else back_s), (1 - core, other if hub else back_x)):
            sinks = [window(out, half, start, rows) for out in outs]
            stream(rows, [src.at[:, pl.ds(0, rows)]], sinks, copy_three)

    by_chip(slot, run)


def place_late_kernel(slot, late, *refs):
    outs, token = refs[-4:-1], refs[-1]
    token[...] = jnp.zeros_like(token)
    chip, core = place()

    def run(rows):
        sinks = [window(out, 1 - core, 0, rows) for out in outs]
        stream(rows, [window(late, 0, 0, rows, 3)], sinks, copy_three)

    @pl.when(chip < 2)
    def _():
        run(first_of(slot - LAG + 1))

    @pl.when(chip >= 2)
    def _():
        run(first_of(min(slot + 1, len(CUTS))))


def settle_rows(kernel, half, pieces, kept, count, rows, after=()):
    kept = kept or ()
    return call(
        kernel,
        (*pieces, *kept),
        [ANY] * (len(pieces) + len(kept)),
        after,
        out_shape=[jax.ShapeDtypeStruct((n, half, 128), BF16) for n in (2, 2, 2, 3)[:count]]
        + [jax.ShapeDtypeStruct((8, 128), F32)],
        out_specs=[ANY] * count + [VMEM],
        input_output_aliases={len(pieces) + i: i for i in range(len(kept))},
        cost_estimate=copy_cost(rows, 6),
        name="place_rows",
    )


def rms(values):
    wide = values.astype(F32)
    inverse = lax.rsqrt(jnp.mean(wide * wide, axis=-1, keepdims=True) + EPSILON)
    return wide * inverse, inverse


def norm_back(step, hat, inverse, gain):
    wide = step.astype(F32)
    gained = gain * wide
    result = inverse * (gained - hat * jnp.mean(gained * hat, axis=-1, keepdims=True))
    return result.astype(BF16), wide * hat


def mul_t(a, b):
    return lax.dot_general(a, b, (((1,), (1,)), ((), ())), preferred_element_type=F32)


def t_mul(a, b):
    return lax.dot_general(a, b, (((0,), (0,)), ((), ())), preferred_element_type=F32)


def mul(a, b):
    return jnp.dot(a, b, preferred_element_type=F32)


def iota(shape, axis):
    return lax.broadcasted_iota(jnp.int32, shape, axis)


def frame_of(slot, core, upper):
    cross = slot % 2
    side = slot // 2
    side = side if upper else 1 - side
    return 2 * side + cross + core - 2 * cross * core


def causal(core, upper):
    shape = (WIDE, 2 * WIDE if upper else WIDE)
    rows, cols = iota(shape, 0), iota(shape, 1)
    key = cols // GROUP
    frame = frame_of(key % SLOTS, core, upper)
    if upper:
        frame = jnp.where(key < SLOTS, -1, frame)
    late = frame <= frame_of(rows // GROUP, core, upper)
    return (rows % GROUP == cols % GROUP) & late


def cat(parts):
    return jnp.concatenate(parts, axis=0)


def tiled(gain):
    return cat([gain] * SLOTS)


def group(wide, j):
    slots = wide.shape[0] // TOGETHER
    return cat([wide[s * TOGETHER + j * GROUP :][:GROUP] for s in range(slots)])


def ungroup(parts):
    return cat([part[s * GROUP :][:GROUP] for s in range(SLOTS) for part in parts])


def fold(acc, rows, part):
    total = part[:TOGETHER]
    for s in range(1, SLOTS):
        total = total + part[s * TOGETHER :][:TOGETHER]
    acc[rows, :] += total


def settle(outs, rows, parts):
    for t, part in enumerate(parts):
        for s, out in enumerate(outs):
            out[t, rows, :] = part[s * TOGETHER :][:TOGETHER]


def sum_heads(acc, heads):
    total = acc[0:heads, :]
    for i in range(1, acc.shape[0] // heads):
        total = total + acc[i * heads : (i + 1) * heads, :]
    return total


def read(refs, t, rows):
    return cat([ref[2 * x + t, rows, :] for ref in refs for x in range(2)])


def read_met(near, far, t, rows):
    return cat([side[2 * x + t][rows, :] for side in (near, far) for x in range(2)])


def hub_specs(steps):
    four = lambda n: pl.BlockSpec((4, BLOCK, 128), lambda i: (n, i, 0))
    flat = lambda q: pl.BlockSpec((BLOCK, 128), lambda i: (q * steps + i, 0))
    return [four(0), four(1), four(0), four(1)] + [flat(q) for q in range(4)] * 2


def hub_refs(steps, skip, own, edge, other, far):
    rows = 4 * steps * BLOCK
    return [own, own, edge, edge] + [other.at[pl.ds(skip, rows)]] * 4 + [far.at[pl.ds(0, rows)]] * 4


def grad_specs():
    return [pl.BlockSpec((3, BLOCK, 128), lambda i: (0, i, 0))] * 4


def grad_refs(outs):
    if len(outs) == 4:
        return list(outs)
    return [outs[0], outs[1], outs[2].at[pl.ds(0, 3)], outs[2].at[pl.ds(3, 3)]]


def gain_spec(first, cycle):
    return pl.BlockSpec((BLOCK, 128), lambda i: ((first + i) % cycle, 0))


def attend(qn, kn, grad, value, allowed):
    scaling = 1.0 / math.sqrt(qn.shape[-1])
    count = TOGETHER // GROUP
    scores = cat([mul_t(group(qn, j), group(kn, j)) for j in range(count)])
    prob_grad = cat([mul_t(group(grad, j), group(value, j)) for j in range(count)])
    mask = cat([allowed] * count)
    scores = jnp.where(mask > 0, scores * scaling, -jnp.inf)
    expo = jnp.exp(scores - jnp.max(scores, axis=-1, keepdims=True))
    prob = expo * (1.0 / jnp.sum(expo, axis=-1, keepdims=True))
    prob_low = prob.astype(BF16)
    dots = jnp.sum(prob_low.astype(F32) * prob_grad, axis=-1, keepdims=True)
    score_low = (prob * (prob_grad - dots)).astype(BF16)
    split = lambda x: [x[j * WIDE :][:WIDE] for j in range(count)]
    return split(prob_low), split(score_low)


def upper_kernel(chunk, skip, heads, own, edge, other, far, gain_q, gain_k, *refs):
    outs, (packed, sum_q, sum_k, acc_q, acc_k, mask) = refs[:-6], refs[-6:]
    chip, core = place()
    first, steps = sum(CUTS[:chunk]), CUTS[chunk]
    count = TOGETHER // GROUP
    cycle = acc_q.shape[0] // BLOCK

    def block(own_a, own_b, edge_a, edge_b, *refs):
        other, far, (gain_q, gain_k), out, pack_ref = refs[:4], refs[4:8], refs[8:10], refs[10:14], refs[14]
        base = ((first + pl.program_id(0)) % cycle) * BLOCK
        scaling = 1.0 / math.sqrt(128)
        lanes = iota((WIDE, 128), 1) // 8
        spread_r, spread_c = iota((2 * WIDE, 128), 0), iota((2 * WIDE, 128), 1)
        spread = jnp.where(spread_r // GROUP == spread_c % 8, 1.0, 0.0).astype(BF16)

        def some(i, total):
            rows = pl.ds(pl.multiple_of(i * TOGETHER, TOGETHER), TOGETHER)
            place = pl.ds(pl.multiple_of(base + i * TOGETHER, TOGETHER), TOGETHER)
            gq, gk = tiled(gain_q[rows, :]), tiled(gain_k[rows, :])
            q_hat, q_inv = rms(read((own_a, edge_a), 0, rows))
            grad = read((own_a, edge_a), 1, rows)
            kl_hat, _ = rms(read_met(other, far, 0, rows))
            ku_hat, ku_inv = rms(read((own_b, edge_b), 0, rows))
            value = cat([read_met(other, far, 1, rows), read((own_b, edge_b), 1, rows)])
            qn = (q_hat * gq).astype(BF16)
            kn = cat([(kl_hat * gk).astype(BF16), (ku_hat * gk).astype(BF16)])
            prob, score = attend(qn, kn, grad, value, mask[...])
            q_step = ungroup([mul(score[j], group(kn, j)) for j in range(count)])
            k_step = ungroup([t_mul(score[j][:, WIDE:], group(qn, j)) for j in range(count)])
            v_step = ungroup([t_mul(prob[j][:, WIDE:], group(grad, j)) for j in range(count)])
            q_step, k_step = (q_step * scaling).astype(BF16), (k_step * scaling).astype(BF16)
            dq, part_q = norm_back(q_step, q_hat, q_inv, gq)
            dk, part_k = norm_back(k_step, ku_hat, ku_inv, gk)
            settle(out, rows, (dq, dk, v_step.astype(BF16)))
            fold(acc_q, place, part_q)
            fold(acc_k, place, part_k)
            for j in range(count):
                cross = jnp.concatenate([prob[j][:, :WIDE], score[j][:, :WIDE]], axis=1)
                total = jnp.where(lanes == i * count + j, mul(cross, spread), total)
            return total

        total = lax.fori_loop(0, BLOCK // TOGETHER, some, jnp.zeros((WIDE, 128), F32))
        pack_ref[...] = total.astype(BF16)

    @pl.when(chip == 2)
    def _():
        acc_q[...] = jnp.zeros_like(acc_q)
        acc_k[...] = jnp.zeros_like(acc_k)
        mask[...] = causal(core, True).astype(F32)
        pltpu.emit_pipeline(
            block,
            grid=(steps,),
            in_specs=hub_specs(steps) + [gain_spec(first, cycle)] * 2,
            out_specs=grad_specs() + [pl.BlockSpec((WIDE, 128), lambda i: (i, 0))],
        )(*hub_refs(steps, skip, own, edge, other, far), gain_q, gain_k, *grad_refs(outs), packed)
        sum_q[...] = sum_heads(acc_q, heads)
        sum_k[...] = sum_heads(acc_k, heads)

    @pl.when(chip != 2)
    def _():
        sum_q[...] = jnp.zeros_like(sum_q)
        sum_k[...] = jnp.zeros_like(sum_k)


def lower_kernel(chunk, skip, at, heads, own, edge, other, far, packed, gain_q, gain_k, *refs):
    outs, (sum_q, sum_k, acc_q, acc_k, mask) = refs[:-5], refs[-5:]
    outs = outs[len(outs) // 2 :]
    chip, core = place()
    first, steps = sum(CUTS[:chunk]), CUTS[chunk]
    count = TOGETHER // GROUP
    cycle = acc_q.shape[0] // BLOCK

    def block(own_a, own_b, edge_a, edge_b, *refs):
        other, far, (gain_q, gain_k, pack_ref), out = refs[:4], refs[4:8], refs[8:11], refs[11:]
        base = ((first + pl.program_id(0)) % cycle) * BLOCK
        both = iota((WIDE, 2 * WIDE), 0) % GROUP == iota((WIDE, 2 * WIDE), 1) % GROUP
        scaling = 1.0 / math.sqrt(128)
        lanes = iota((WIDE, 128), 1) // 8
        spread_r, spread_c = iota((128, 2 * WIDE), 0), iota((128, 2 * WIDE), 1)
        spread = jnp.where(spread_c // GROUP == spread_r % 8, 1.0, 0.0).astype(BF16)
        crossed = pack_ref[...].astype(F32)

        def some(i, carry):
            rows = pl.ds(pl.multiple_of(i * TOGETHER, TOGETHER), TOGETHER)
            place = pl.ds(pl.multiple_of(base + i * TOGETHER, TOGETHER), TOGETHER)
            gq, gk = tiled(gain_q[rows, :]), tiled(gain_k[rows, :])
            k_hat, k_inv = rms(read((own_a, edge_a), 0, rows))
            value = read((own_a, edge_a), 1, rows)
            q_hat, q_inv = rms(read((own_b, edge_b), 0, rows))
            grad = read((own_b, edge_b), 1, rows)
            qu_hat, _ = rms(read_met(other, far, 0, rows))
            grad_u = read_met(other, far, 1, rows)
            kn = (k_hat * gk).astype(BF16)
            qn = (q_hat * gq).astype(BF16)
            qn_u = (qu_hat * gq).astype(BF16)
            prob, score = attend(qn, kn, grad, value, mask[...])
            cross = []
            for j in range(count):
                mine = jnp.where(lanes == i * count + j, crossed, 0.0).astype(BF16)
                cross.append(jnp.where(both, mul(mine, spread), 0.0).astype(BF16))
            q_step = ungroup([mul(score[j], group(kn, j)) for j in range(count)])
            k_step = ungroup(
                [
                    t_mul(cat([score[j], cross[j][:, WIDE:]]), cat([group(qn, j), group(qn_u, j)]))
                    for j in range(count)
                ]
            )
            v_step = ungroup(
                [
                    t_mul(cat([prob[j], cross[j][:, :WIDE]]), cat([group(grad, j), group(grad_u, j)]))
                    for j in range(count)
                ]
            )
            q_step, k_step = (q_step * scaling).astype(BF16), (k_step * scaling).astype(BF16)
            dq, part_q = norm_back(q_step, q_hat, q_inv, gq)
            dk, part_k = norm_back(k_step, k_hat, k_inv, gk)
            settle(out, rows, (dq, dk, v_step.astype(BF16)))
            fold(acc_q, place, part_q)
            fold(acc_k, place, part_k)
            return carry

        lax.fori_loop(0, BLOCK // TOGETHER, some, 0)

    @pl.when(chip == 1)
    def _():
        acc_q[...] = jnp.zeros_like(acc_q)
        acc_k[...] = jnp.zeros_like(acc_k)
        mask[...] = causal(core, False).astype(F32)
        pltpu.emit_pipeline(
            block,
            grid=(steps,),
            in_specs=hub_specs(steps)
            + [gain_spec(first, cycle)] * 2
            + [pl.BlockSpec((WIDE, 128), lambda i: (i, 0))],
            out_specs=grad_specs(),
        )(
            *hub_refs(steps, skip, own, edge, other, far),
            gain_q,
            gain_k,
            packed.at[pl.ds(at, steps * WIDE)],
            *grad_refs(outs),
        )
        sum_q[...] = sum_heads(acc_q, heads)
        sum_k[...] = sum_heads(acc_k, heads)

    @pl.when(chip != 1)
    def _():
        sum_q[...] = jnp.zeros_like(sum_q)
        sum_k[...] = jnp.zeros_like(sum_k)


def hub_cost(rows):
    return pl.CostEstimate(
        flops=rows * 60000, bytes_accessed=rows * 128 * 2 * 36, transcendentals=rows * 600
    )


def grad_shapes(slot):
    sizes = (3, 3, 6) if slot < len(CUTS) + LAG - DIRECT else (3, 3, 3, 3)
    return [jax.ShapeDtypeStruct((n, out_rows(slot), 128), BF16) for n in sizes]


def upper(slot, skip, heads, data, gains, after):
    steps = CUTS[slot]
    cycle = gains[0].shape[0]
    shapes = grad_shapes(slot)
    return call(
        functools.partial(upper_kernel, slot, skip, heads),
        (*data, *gains),
        [ANY] * 6,
        after,
        out_shape=shapes
        + [jax.ShapeDtypeStruct((steps * WIDE, 128), BF16)]
        + [jax.ShapeDtypeStruct((heads, 128), F32)] * 2,
        out_specs=[ANY] * (len(shapes) + 1) + [VMEM] * 2,
        scratch_shapes=[pltpu.VMEM((cycle, 128), F32)] * 2 + [pltpu.VMEM((WIDE, 2 * WIDE), F32)],
        cost_estimate=hub_cost(steps * BLOCK),
        name="upper_frames",
    )


def lower(slot, heads, data, packed, at, skip, gains, outs, after):
    chunk = slot - LAG
    cycle = gains[0].shape[0]
    shapes = grad_shapes(slot)
    return call(
        functools.partial(lower_kernel, chunk, skip, at, heads),
        (*data, packed, *gains, *outs),
        [ANY] * (7 + len(outs)),
        after,
        out_shape=shapes + [jax.ShapeDtypeStruct((heads, 128), F32)] * 2,
        out_specs=[ANY] * len(shapes) + [VMEM] * 2,
        scratch_shapes=[pltpu.VMEM((cycle, 128), F32)] * 2 + [pltpu.VMEM((WIDE, WIDE), F32)],
        input_output_aliases={7 + i: i for i in range(len(outs))},
        cost_estimate=hub_cost(rows_of(chunk)),
        name="lower_frames",
    )


def blank(slot, after):
    def kernel(*refs):
        pass

    shapes = grad_shapes(slot)
    return call(
        kernel, (), [], after, out_shape=shapes, out_specs=[ANY] * len(shapes), name="blank_rows"
    )


def send(array, pairs):
    return lax.ppermute(array, "seq", pairs)


def add_pieces(pieces, after):
    def kernel(src, out):
        total = src[:, 0]
        for i in range(1, src.shape[1]):
            total = total + src[:, i]
        out[...] = total

    shape = (pieces.shape[0], *pieces.shape[2:])
    return call(
        kernel, (pieces,), [VMEM], after, out_shape=jax.ShapeDtypeStruct(shape, F32), out_specs=VMEM, name="add_pieces"
    )


def sum_gains(part, after):
    count = lax.axis_size("dp")
    mine = part.shape[1] // count
    pieces = part.reshape(2, count, mine, part.shape[2])
    total = add_pieces(lax.all_to_all(pieces, "dp", split_axis=1, concat_axis=1, tiled=True), after)
    total = total + send(total, SWAP)
    total = total + send(total, MIDDLE)
    edge = send(total, BACK_S)
    chip, _ = place()
    return jnp.where((chip == 1) | (chip == 2), total, edge)


def hub_body(queries, key_proj, value_proj, out_grad, query_gain, key_gain):
    shape = queries.shape
    heads, width = shape[-2:]
    half = shape[2] // 2 * heads
    arrays = [x.reshape(2, half, width) for x in (queries, key_proj, value_proj, out_grad)]
    cycle = math.lcm(BLOCK, heads)
    chunks = len(CUTS)

    edges, grads, crossed, middle, packs, traded = {}, {}, {}, {}, {}, []
    slots = chunks + LAG
    sums, kept, chain, marks = [], {-1: None}, [], []

    def then(token):
        chain[:] = [token]

    def trade(low, high):
        rows = halves(low, high - low, arrays, chain)
        then(rows)
        traded.append((send(rows, SWAP), low))

    def bring(chunk):
        swapped, offset = traded[min(chunk, 1)]
        rows = pack(chunk, offset, arrays, swapped, chain)
        then(rows)
        edges[chunk] = (rows, send(rows, EDGE))

    def cross(chunk):
        sources = [edges[chunk][1]] if chunk >= 0 else []
        if chunk + 1 < chunks:
            sources.append(edges[chunk + 1][0])
        if chunk >= LAG:
            sources.append(packs[chunk - LAG])
            crossed[chunk - LAG] = (chunk, sum(4 * x.shape[1] for x in sources[:-1]))
        if chunk == 0:
            chain.extend([middle[-1], *gains])
        rows = forward(sources, chain)
        then(rows)
        middle[chunk] = send(rows, MIDDLE)

    def data_of(chunk):
        return (*edges[chunk], middle[chunk - 1], middle[chunk])

    def skip_of(chunk):
        return 4 * rows_of(chunk - 1) if chunk else 0

    def work(slot):
        if slot < chunks:
            *parts, packs[slot], sum_q, sum_k = upper(
                slot, skip_of(slot), heads, data_of(slot), gains, chain
            )
            if slot >= chunks - LAG:
                packs[slot] = send(packs[slot], DOWN)
            sums.append((sum_q, sum_k))
        else:
            parts = blank(slot, chain)
        if slot >= LAG:
            chunk = slot - LAG
            packed, at = packs[chunk], 0
            if chunk in crossed:
                packed, at = middle[crossed[chunk][0]], crossed[chunk][1]
            after = [sum_q] if slot < chunks else []
            *parts, sum_q, sum_k = lower(
                slot, heads, data_of(chunk), packed, at, skip_of(chunk), gains, parts, after
            )
            sums.append((sum_q, sum_k))
        then(sum_q)
        own, other, *edge = parts
        if slot < slots - DIRECT:
            grads[slot] = (own, other, send(edge[0], BACK_S))
        else:
            grads[slot] = (own, send(other, SWAP), send(edge[0], BACK_S), send(edge[1], BACK_X))

    def settle_slot(slot):
        rows = out_rows(slot)
        if slot < slots - DIRECT:
            kernel = functools.partial(place_kernel, slot)
            *kept[slot], token = settle_rows(kernel, half, grads[slot], kept[slot - 1], 4, rows, chain)
            if slot == slots - DIRECT - 1:
                grads["late"] = send(kept[slot][3], SWAP)
        else:
            outs = kept[slot - 1]
            if slot == slots - DIRECT:
                kernel = functools.partial(place_late_kernel, slot - 1)
                *outs, token = settle_rows(kernel, half, (grads["late"],), outs[:3], 3, half // 2, chain)
                then(token)
            if slot == slots - 1:
                marks.extend(chain)
            kernel = functools.partial(place_last_kernel, slot)
            *kept[slot], token = settle_rows(kernel, half, grads[slot], outs, 3, rows, chain)
        then(token)

    trade(0, rows_of(0))
    bring(0)
    cross(-1)
    trade(rows_of(0), half)
    bring(1)
    both = lax.all_gather(jnp.stack([query_gain, key_gain]), "dp", axis=1, tiled=True)
    gains = [jnp.tile(both[t], (cycle // heads, 1)) for t in range(2)]
    cross(0)
    bring(2)
    for slot in range(slots):
        if slot + 1 < chunks:
            cross(slot + 1)
        if slot + 3 < chunks:
            bring(slot + 3)
        work(slot)
        if slot >= 1:
            settle_slot(slot - 1)
    for slot in range(slots - 1, slots):
        settle_slot(slot)

    totals = jnp.stack([functools.reduce(jnp.add, [s[t] for s in sums]) for t in range(2)])
    totals = sum_gains(totals, marks)
    return (*[x.reshape(shape) for x in kept[slots - 1]], totals[0], totals[1])


def wide_attention(query_norm, key_norm, value_in, grad_in):
    frames = query_norm.shape[1]
    scaling = 1.0 / math.sqrt(query_norm.shape[-1])
    scores = (
        jnp.einsum("efphd,egphd->ephfg", query_norm, key_norm, preferred_element_type=F32) * scaling
    )
    allowed = iota((frames, frames), 1) <= iota((frames, frames), 0)
    scores = jnp.where(allowed, scores, -jnp.inf)
    expo = jnp.exp(scores - jnp.max(scores, axis=-1, keepdims=True))
    probability = expo / jnp.sum(expo, axis=-1, keepdims=True)
    prob_low = probability.astype(BF16)
    attn_out = jnp.einsum("ephfg,egphd->efphd", prob_low, value_in, preferred_element_type=F32)
    row_dots = jnp.transpose(jnp.sum(grad_in.astype(F32) * attn_out, axis=-1), (0, 2, 3, 1))
    prob_grad = jnp.einsum("efphd,egphd->ephfg", grad_in, value_in, preferred_element_type=F32)
    score_low = (probability * (prob_grad - row_dots[..., None])).astype(BF16)
    query_step = jnp.einsum("ephfg,egphd->efphd", score_low, key_norm, preferred_element_type=F32)
    key_step = jnp.einsum("ephfg,efphd->egphd", score_low, query_norm, preferred_element_type=F32)
    value_step = jnp.einsum("ephfg,efphd->egphd", prob_low, grad_in, preferred_element_type=F32)
    return (
        (query_step * scaling).astype(BF16),
        (key_step * scaling).astype(BF16),
        value_step.astype(BF16),
    )


def wide_body(queries, key_proj, value_proj, out_grad, query_gain, key_gain):
    gain_q = lax.all_gather(query_gain, "dp", axis=0, tiled=True)
    gain_k = lax.all_gather(key_gain, "dp", axis=0, tiled=True)
    q_hat, q_inv = rms(queries)
    k_hat, k_inv = rms(key_proj)
    pieces = [
        lax.all_to_all(x, "seq", split_axis=2, concat_axis=1, tiled=True)
        for x in ((q_hat * gain_q).astype(BF16), (k_hat * gain_k).astype(BF16), value_proj, out_grad)
    ]
    steps = [
        lax.all_to_all(x, "seq", split_axis=1, concat_axis=2, tiled=True)
        for x in wide_attention(*pieces)
    ]
    query_grad, part_q = norm_back(steps[0], q_hat, q_inv, gain_q)
    key_grad, part_k = norm_back(steps[1], k_hat, k_inv, gain_k)
    axes = tuple(range(part_q.ndim - 2))
    totals = lax.psum((jnp.sum(part_q, axis=axes), jnp.sum(part_k, axis=axes)), "seq")
    totals = [lax.psum_scatter(t, "dp", scatter_dimension=0, tiled=True) for t in totals]
    return (query_grad, key_grad, steps[2], *totals)


def body(*args):
    frames = lax.axis_size("seq")
    patches, heads, width = args[0].shape[2:]
    rows = patches // 2 * heads
    if frames == 8 and args[0].shape[:2] == (1, 1) and width == 128 and rows == sum(CUTS) * BLOCK:
        return hub_body(*args)
    return wide_body(*args)


def solution(mesh):
    whole = P("dp", "seq", None, None, None)
    gain = P("dp", None)
    return jax.shard_map(
        body,
        mesh=mesh,
        in_specs=(whole,) * 4 + (gain,) * 2,
        out_specs=(whole,) * 3 + (gain,) * 2,
        check_vma=False,
    )
```

```python
import functools
import math

import jax
import jax.numpy as jnp
from jax import lax
from jax.experimental import pallas as pl
from jax.experimental.pallas import tpu as pltpu
from jax.sharding import PartitionSpec as P

EPSILON = 1e-06
BLOCK = 256
GROUP = 16
SLOTS = 4
WIDE = GROUP * SLOTS
TOGETHER = 256
CUTS = (2, 2, 2, 2, 2, 2, 2, 2, 2, 2)
LAG = 2
DIRECT = 2

EDGE = ((0, 2), (1, 3), (6, 4), (7, 5))
MIDDLE = ((2, 4), (3, 5), (4, 2), (5, 3))
DOWN = ((4, 2), (5, 3))
BACK_S = ((2, 0), (3, 1), (4, 6), (5, 7))
BACK_X = ((2, 1), (3, 0), (4, 7), (5, 6))
SWAP = tuple((i, i ^ 1) for i in range(8))

F32 = jnp.float32
BF16 = jnp.bfloat16
ANY = pl.BlockSpec(memory_space=pl.ANY)
VMEM = pl.BlockSpec(memory_space=pltpu.VMEM)


def place():
    index = lax.axis_index("seq")
    chip, core = index // 2, index % 2
    return chip, core


def call(kernel, inputs, in_specs, after=(), **kwargs):
    count, extra = len(inputs), len(after)

    def trimmed(*refs):
        kernel(*refs[:count], *refs[count + extra :])

    return pl.pallas_call(
        trimmed,
        in_specs=list(in_specs) + [ANY] * extra,
        compiler_params=pltpu.CompilerParams(vmem_limit_bytes=16 * 1024 * 1024),
        **kwargs,
    )(*inputs, *after)


def first_of(chunk):
    return sum(CUTS[:chunk]) * BLOCK


def rows_of(chunk):
    return CUTS[chunk] * BLOCK


def chunk_of(slot, high):
    chunk = slot if high else slot - LAG
    return chunk if 0 <= chunk < len(CUTS) else None


def out_rows(slot):
    chunks = [chunk_of(slot, high) for high in (False, True)]
    return max(rows_of(chunk) for chunk in chunks if chunk is not None)


def copy_cost(rows, tensors):
    return pl.CostEstimate(flops=0, bytes_accessed=rows * 128 * 2 * 2 * tensors, transcendentals=0)


def tile_of(rows):
    return next(rows // k for k in range(2, rows) if rows % (16 * k) == 0 and rows // k <= 1024)


def stream(rows, sources, sinks, move):
    tile = tile_of(rows)

    def spec(ref):
        return pl.BlockSpec((ref.shape[0], tile, 128), lambda i: (0, i, 0))

    pltpu.emit_pipeline(
        move,
        grid=(rows // tile,),
        in_specs=[spec(ref) for ref in sources],
        out_specs=[spec(ref) for ref in sinks],
    )(*sources, *sinks)


def window(ref, index, start, rows, count=1):
    return ref.at[pl.ds(index, count), pl.ds(start, rows)]


def halves_kernel(start, rows, q, k, v, g, out):
    _, core = place()

    def move(*blocks):
        for t in range(4):
            blocks[4][t] = blocks[t][0]

    stream(rows, [window(ref, 1 - core, start, rows) for ref in (q, k, v, g)], [out], move)


def halves(start, rows, arrays, after):
    return call(
        functools.partial(halves_kernel, start, rows),
        arrays,
        [ANY] * 4,
        after,
        out_shape=jax.ShapeDtypeStruct((4, rows, 128), BF16),
        out_specs=ANY,
        cost_estimate=copy_cost(rows, 4),
        name="other_half",
    )


def pack_kernel(start, rows, offset, q, k, v, g, x, edge):
    chip, core = place()

    def run(order):
        def move(*blocks):
            sent = blocks[8]
            for pair in range(2):
                for t in range(2):
                    for frame in range(2):
                        sent[4 * pair + 2 * frame + t] = blocks[4 * frame + 2 * pair + t][0]

        own = [window((q, k, v, g)[t], core, start, rows) for t in order]
        other = [window(x, t, start - offset, rows) for t in order]
        stream(rows, own + other, [edge], move)

    @pl.when(chip < 2)
    def _():
        run((1, 2, 0, 3))

    @pl.when(chip >= 2)
    def _():
        run((0, 3, 1, 2))


def pack(chunk, offset, arrays, swapped, after):
    rows = rows_of(chunk)
    return call(
        functools.partial(pack_kernel, first_of(chunk), rows, offset),
        (*arrays, swapped),
        [ANY] * 5,
        after,
        out_shape=jax.ShapeDtypeStruct((8, rows, 128), BF16),
        out_specs=ANY,
        cost_estimate=copy_cost(rows, 8),
        name="pack_rows",
    )


def forward_kernel(sizes, *refs):
    sources, out = refs[:-1], refs[-1]
    chip, _ = place()
    starts = [0]
    for rows, src in zip(sizes, sources):
        starts.append(starts[-1] + (rows if len(src.shape) == 2 else 4 * rows))

    def copy(picked, steps):
        def move(*blocks):
            sinks = iter(blocks[len(picked) :])
            for src in blocks[: len(picked)]:
                for part in (src,) if len(src.shape) == 2 else [src.at[q] for q in range(4)]:
                    next(sinks)[...] = part[...]

        ins, in_specs, outs, out_specs = [], [], [], []
        for i in picked:
            rows, flat = sizes[i], len(sources[i].shape) == 2
            spec = pl.BlockSpec((rows // steps, 128), lambda i: (i, 0))
            ins.append(sources[i])
            in_specs.append(spec if flat else pl.BlockSpec((4, rows // steps, 128), lambda i: (0, i, 0)))
            for q in range(1 if flat else 4):
                outs.append(out.at[pl.ds(starts[i] + q * rows, rows)])
                out_specs.append(spec)
        pltpu.emit_pipeline(move, grid=(steps,), in_specs=in_specs, out_specs=out_specs)(*ins, *outs)

    @pl.when((chip == 1) | (chip == 2))
    def _():
        steps = sizes[0] // tile_of(sizes[0])
        if all(rows % (16 * steps) == 0 for rows in sizes):
            copy(range(len(sizes)), steps)
        else:
            for i, rows in enumerate(sizes):
                copy([i], rows // tile_of(rows))


def forward(sources, after):
    sizes = [x.shape[-2] for x in sources]
    total = sum(n if x.ndim == 2 else 4 * n for n, x in zip(sizes, sources))
    return call(
        functools.partial(forward_kernel, sizes),
        sources,
        [ANY] * len(sources),
        after,
        out_shape=jax.ShapeDtypeStruct((total, 128), BF16),
        out_specs=ANY,
        cost_estimate=copy_cost(sum(sizes), 4),
        name="forward_rows",
    )


def copy_three(src, *dsts):
    for t, dst in enumerate(dsts):
        dst[0] = src[t]


def copy_all(src, dst):
    dst[...] = src[...]


def by_chip(slot, run):
    chip, _ = place()
    for which in range(4):
        chunk = chunk_of(slot, which >= 2)
        if chunk is not None:
            pl.when(chip == which)(functools.partial(run, chunk, which in (1, 2)))


def place_kernel(slot, own, other, back, *refs):
    outs, late, token = refs[-5:-2], refs[-2], refs[-1]
    token[...] = jnp.zeros_like(token)
    _, core = place()

    def run(chunk, hub):
        start, rows = first_of(chunk), rows_of(chunk)
        near = own.at[:, pl.ds(0, rows)] if hub else window(back, 0, 0, rows, 3)
        far = other.at[:, pl.ds(0, rows)] if hub else window(back, 3, 0, rows, 3)
        sinks = [window(out, core, start, rows) for out in outs] + [window(late, 0, start, rows, 3)]

        def move(near, far, *dsts):
            copy_three(near, *dsts[:3])
            copy_all(far, dsts[3])

        stream(rows, [near, far], sinks, move)

    by_chip(slot, run)


def place_last_kernel(slot, own, other, back_s, back_x, *refs):
    outs, token = refs[-4:-1], refs[-1]
    token[...] = jnp.zeros_like(token)
    _, core = place()

    def run(chunk, hub):
        start, rows = first_of(chunk), rows_of(chunk)
        near, far = [ref.at[:, pl.ds(0, rows)] for ref in ((own, other) if hub else (back_s, back_x))]
        sinks = [window(out, half, start, rows) for half in (core, 1 - core) for out in outs]

        def move(near, far, *dsts):
            copy_three(near, *dsts[:3])
            copy_three(far, *dsts[3:])

        stream(rows, [near, far], sinks, move)

    by_chip(slot, run)


def place_late_kernel(slot, late, *refs):
    outs, token = refs[-4:-1], refs[-1]
    token[...] = jnp.zeros_like(token)
    chip, core = place()

    def run(rows):
        sinks = [window(out, 1 - core, 0, rows) for out in outs]
        stream(rows, [window(late, 0, 0, rows, 3)], sinks, copy_three)

    @pl.when(chip < 2)
    def _():
        run(first_of(slot - LAG + 1))

    @pl.when(chip >= 2)
    def _():
        run(first_of(min(slot + 1, len(CUTS))))


def settle_rows(kernel, half, pieces, kept, count, rows, after=()):
    kept = kept or ()
    return call(
        kernel,
        (*pieces, *kept),
        [ANY] * (len(pieces) + len(kept)),
        after,
        out_shape=[jax.ShapeDtypeStruct((n, half, 128), BF16) for n in (2, 2, 2, 3)[:count]]
        + [jax.ShapeDtypeStruct((8, 128), F32)],
        out_specs=[ANY] * count + [VMEM],
        input_output_aliases={len(pieces) + i: i for i in range(len(kept))},
        cost_estimate=copy_cost(rows, 6),
        name="place_rows",
    )


def rms(values):
    wide = values.astype(F32)
    inverse = lax.rsqrt(jnp.mean(wide * wide, axis=-1, keepdims=True) + EPSILON)
    return wide * inverse, inverse


def norm_back(step, hat, inverse, gain):
    wide = step.astype(F32)
    gained = gain * wide
    result = inverse * (gained - hat * jnp.mean(gained * hat, axis=-1, keepdims=True))
    return result.astype(BF16), wide * hat


def mul_t(a, b):
    return lax.dot_general(a, b, (((1,), (1,)), ((), ())), preferred_element_type=F32)


def t_mul(a, b):
    return lax.dot_general(a, b, (((0,), (0,)), ((), ())), preferred_element_type=F32)


def mul(a, b):
    return jnp.dot(a, b, preferred_element_type=F32)


def iota(shape, axis):
    return lax.broadcasted_iota(jnp.int32, shape, axis)


def frame_of(slot, core, upper):
    cross = slot % 2
    side = slot // 2
    side = side if upper else 1 - side
    return 2 * side + cross + core - 2 * cross * core


def causal(core, upper):
    shape = (WIDE, 2 * WIDE if upper else WIDE)
    rows, cols = iota(shape, 0), iota(shape, 1)
    key = cols // GROUP
    frame = frame_of(key % SLOTS, core, upper)
    if upper:
        frame = jnp.where(key < SLOTS, -1, frame)
    late = frame <= frame_of(rows // GROUP, core, upper)
    return (rows % GROUP == cols % GROUP) & late


def cat(parts):
    return jnp.concatenate(parts, axis=0)


def tiled(gain):
    return cat([gain] * SLOTS)


def group(wide, j):
    slots = wide.shape[0] // TOGETHER
    return cat([wide[s * TOGETHER + j * GROUP :][:GROUP] for s in range(slots)])


def ungroup(parts):
    return cat([part[s * GROUP :][:GROUP] for s in range(SLOTS) for part in parts])


def fold(acc, rows, part):
    total = part[:TOGETHER]
    for s in range(1, SLOTS):
        total = total + part[s * TOGETHER :][:TOGETHER]
    acc[rows, :] += total


def settle(outs, rows, parts):
    for t, part in enumerate(parts):
        for s, out in enumerate(outs):
            out[t, rows, :] = part[s * TOGETHER :][:TOGETHER]


def sum_heads(acc, heads):
    total = acc[0:heads, :]
    for i in range(1, acc.shape[0] // heads):
        total = total + acc[i * heads : (i + 1) * heads, :]
    return total


def read(refs, t, rows):
    return cat([ref[2 * x + t, rows, :] for ref in refs for x in range(2)])


def read_met(near, far, t, rows):
    return cat([side[2 * x + t][rows, :] for side in (near, far) for x in range(2)])


def hub_specs(steps):
    four = lambda n: pl.BlockSpec((4, BLOCK, 128), lambda i: (n, i, 0))
    flat = lambda q: pl.BlockSpec((BLOCK, 128), lambda i: (q * steps + i, 0))
    return [four(0), four(1), four(0), four(1)] + [flat(q) for q in range(4)] * 2


def hub_refs(steps, skip, own, edge, other, far):
    rows = 4 * steps * BLOCK
    return [own, own, edge, edge] + [other.at[pl.ds(skip, rows)]] * 4 + [far.at[pl.ds(0, rows)]] * 4


def grad_specs():
    return [pl.BlockSpec((3, BLOCK, 128), lambda i: (0, i, 0))] * 4


def grad_refs(outs):
    if len(outs) == 4:
        return list(outs)
    return [outs[0], outs[1], outs[2].at[pl.ds(0, 3)], outs[2].at[pl.ds(3, 3)]]


def gain_spec(first, cycle):
    return pl.BlockSpec((BLOCK, 128), lambda i: ((first + i) % cycle, 0))


def attend(qn, kn, grad, value, allowed):
    scaling = 1.0 / math.sqrt(qn.shape[-1])
    count = TOGETHER // GROUP
    scores = cat([mul_t(group(qn, j), group(kn, j)) for j in range(count)])
    prob_grad = cat([mul_t(group(grad, j), group(value, j)) for j in range(count)])
    mask = cat([allowed] * count)
    scores = jnp.where(mask > 0, scores * scaling, -jnp.inf)
    expo = jnp.exp(scores - jnp.max(scores, axis=-1, keepdims=True))
    prob = expo * (1.0 / jnp.sum(expo, axis=-1, keepdims=True))
    prob_low = prob.astype(BF16)
    dots = jnp.sum(prob_low.astype(F32) * prob_grad, axis=-1, keepdims=True)
    score_low = (prob * (prob_grad - dots)).astype(BF16)
    split = lambda x: [x[j * WIDE :][:WIDE] for j in range(count)]
    return split(prob_low), split(score_low)


def upper_kernel(chunk, skip, heads, own, edge, other, far, gain_q, gain_k, *refs):
    outs, (packed, sum_q, sum_k, acc_q, acc_k, mask) = refs[:-6], refs[-6:]
    chip, core = place()
    first, steps = sum(CUTS[:chunk]), CUTS[chunk]
    count = TOGETHER // GROUP
    cycle = acc_q.shape[0] // BLOCK

    def block(own_a, own_b, edge_a, edge_b, *refs):
        other, far, (gain_q, gain_k), out, pack_ref = refs[:4], refs[4:8], refs[8:10], refs[10:14], refs[14]
        base = ((first + pl.program_id(0)) % cycle) * BLOCK
        scaling = 1.0 / math.sqrt(128)
        lanes = iota((WIDE, 128), 1) // 8
        spread_r, spread_c = iota((2 * WIDE, 128), 0), iota((2 * WIDE, 128), 1)
        spread = jnp.where(spread_r // GROUP == spread_c % 8, 1.0, 0.0).astype(BF16)

        def some(i, total):
            rows = pl.ds(pl.multiple_of(i * TOGETHER, TOGETHER), TOGETHER)
            place = pl.ds(pl.multiple_of(base + i * TOGETHER, TOGETHER), TOGETHER)
            gq, gk = tiled(gain_q[rows, :]), tiled(gain_k[rows, :])
            q_hat, q_inv = rms(read((own_a, edge_a), 0, rows))
            grad = read((own_a, edge_a), 1, rows)
            kl_hat, _ = rms(read_met(other, far, 0, rows))
            ku_hat, ku_inv = rms(read((own_b, edge_b), 0, rows))
            value = cat([read_met(other, far, 1, rows), read((own_b, edge_b), 1, rows)])
            qn = (q_hat * gq).astype(BF16)
            kn = cat([(kl_hat * gk).astype(BF16), (ku_hat * gk).astype(BF16)])
            prob, score = attend(qn, kn, grad, value, mask[...])
            q_step = ungroup([mul(score[j], group(kn, j)) for j in range(count)])
            k_step = ungroup([t_mul(score[j][:, WIDE:], group(qn, j)) for j in range(count)])
            v_step = ungroup([t_mul(prob[j][:, WIDE:], group(grad, j)) for j in range(count)])
            q_step, k_step = (q_step * scaling).astype(BF16), (k_step * scaling).astype(BF16)
            dq, part_q = norm_back(q_step, q_hat, q_inv, gq)
            dk, part_k = norm_back(k_step, ku_hat, ku_inv, gk)
            settle(out, rows, (dq, dk, v_step.astype(BF16)))
            fold(acc_q, place, part_q)
            fold(acc_k, place, part_k)
            for j in range(count):
                cross = jnp.concatenate([prob[j][:, :WIDE], score[j][:, :WIDE]], axis=1)
                total = jnp.where(lanes == i * count + j, mul(cross, spread), total)
            return total

        total = lax.fori_loop(0, BLOCK // TOGETHER, some, jnp.zeros((WIDE, 128), F32))
        pack_ref[...] = total.astype(BF16)

    @pl.when(chip == 2)
    def _():
        acc_q[...] = jnp.zeros_like(acc_q)
        acc_k[...] = jnp.zeros_like(acc_k)
        mask[...] = causal(core, True).astype(F32)
        pltpu.emit_pipeline(
            block,
            grid=(steps,),
            in_specs=hub_specs(steps) + [gain_spec(first, cycle)] * 2,
            out_specs=grad_specs() + [pl.BlockSpec((WIDE, 128), lambda i: (i, 0))],
        )(*hub_refs(steps, skip, own, edge, other, far), gain_q, gain_k, *grad_refs(outs), packed)
        sum_q[...] = sum_heads(acc_q, heads)
        sum_k[...] = sum_heads(acc_k, heads)

    @pl.when(chip != 2)
    def _():
        sum_q[...] = jnp.zeros_like(sum_q)
        sum_k[...] = jnp.zeros_like(sum_k)


def lower_kernel(chunk, skip, at, heads, own, edge, other, far, packed, gain_q, gain_k, *refs):
    outs, (sum_q, sum_k, acc_q, acc_k, mask) = refs[:-5], refs[-5:]
    outs = outs[len(outs) // 2 :]
    chip, core = place()
    first, steps = sum(CUTS[:chunk]), CUTS[chunk]
    count = TOGETHER // GROUP
    cycle = acc_q.shape[0] // BLOCK

    def block(own_a, own_b, edge_a, edge_b, *refs):
        other, far, (gain_q, gain_k, pack_ref), out = refs[:4], refs[4:8], refs[8:11], refs[11:]
        base = ((first + pl.program_id(0)) % cycle) * BLOCK
        both = iota((WIDE, 2 * WIDE), 0) % GROUP == iota((WIDE, 2 * WIDE), 1) % GROUP
        scaling = 1.0 / math.sqrt(128)
        lanes = iota((WIDE, 128), 1) // 8
        spread_r, spread_c = iota((128, 2 * WIDE), 0), iota((128, 2 * WIDE), 1)
        spread = jnp.where(spread_c // GROUP == spread_r % 8, 1.0, 0.0).astype(BF16)
        crossed = pack_ref[...].astype(F32)

        def some(i, carry):
            rows = pl.ds(pl.multiple_of(i * TOGETHER, TOGETHER), TOGETHER)
            place = pl.ds(pl.multiple_of(base + i * TOGETHER, TOGETHER), TOGETHER)
            gq, gk = tiled(gain_q[rows, :]), tiled(gain_k[rows, :])
            k_hat, k_inv = rms(read((own_a, edge_a), 0, rows))
            value = read((own_a, edge_a), 1, rows)
            q_hat, q_inv = rms(read((own_b, edge_b), 0, rows))
            grad = read((own_b, edge_b), 1, rows)
            qu_hat, _ = rms(read_met(other, far, 0, rows))
            grad_u = read_met(other, far, 1, rows)
            kn = (k_hat * gk).astype(BF16)
            qn = (q_hat * gq).astype(BF16)
            qn_u = (qu_hat * gq).astype(BF16)
            prob, score = attend(qn, kn, grad, value, mask[...])
            cross = []
            for j in range(count):
                mine = jnp.where(lanes == i * count + j, crossed, 0.0).astype(BF16)
                cross.append(jnp.where(both, mul(mine, spread), 0.0).astype(BF16))
            q_step = ungroup([mul(score[j], group(kn, j)) for j in range(count)])
            k_step = ungroup(
                [
                    t_mul(cat([score[j], cross[j][:, WIDE:]]), cat([group(qn, j), group(qn_u, j)]))
                    for j in range(count)
                ]
            )
            v_step = ungroup(
                [
                    t_mul(cat([prob[j], cross[j][:, :WIDE]]), cat([group(grad, j), group(grad_u, j)]))
                    for j in range(count)
                ]
            )
            q_step, k_step = (q_step * scaling).astype(BF16), (k_step * scaling).astype(BF16)
            dq, part_q = norm_back(q_step, q_hat, q_inv, gq)
            dk, part_k = norm_back(k_step, k_hat, k_inv, gk)
            settle(out, rows, (dq, dk, v_step.astype(BF16)))
            fold(acc_q, place, part_q)
            fold(acc_k, place, part_k)
            return carry

        lax.fori_loop(0, BLOCK // TOGETHER, some, 0)

    @pl.when(chip == 1)
    def _():
        acc_q[...] = jnp.zeros_like(acc_q)
        acc_k[...] = jnp.zeros_like(acc_k)
        mask[...] = causal(core, False).astype(F32)
        pltpu.emit_pipeline(
            block,
            grid=(steps,),
            in_specs=hub_specs(steps)
            + [gain_spec(first, cycle)] * 2
            + [pl.BlockSpec((WIDE, 128), lambda i: (i, 0))],
            out_specs=grad_specs(),
        )(
            *hub_refs(steps, skip, own, edge, other, far),
            gain_q,
            gain_k,
            packed.at[pl.ds(at, steps * WIDE)],
            *grad_refs(outs),
        )
        sum_q[...] = sum_heads(acc_q, heads)
        sum_k[...] = sum_heads(acc_k, heads)

    @pl.when(chip != 1)
    def _():
        sum_q[...] = jnp.zeros_like(sum_q)
        sum_k[...] = jnp.zeros_like(sum_k)


def hub_cost(rows):
    return pl.CostEstimate(
        flops=rows * 60000, bytes_accessed=rows * 128 * 2 * 36, transcendentals=rows * 600
    )


def grad_shapes(slot):
    sizes = (3, 3, 6) if slot < len(CUTS) + LAG - DIRECT else (3, 3, 3, 3)
    return [jax.ShapeDtypeStruct((n, out_rows(slot), 128), BF16) for n in sizes]


def upper(slot, skip, heads, data, gains, after):
    steps = CUTS[slot]
    cycle = gains[0].shape[0]
    shapes = grad_shapes(slot)
    return call(
        functools.partial(upper_kernel, slot, skip, heads),
        (*data, *gains),
        [ANY] * 6,
        after,
        out_shape=shapes
        + [jax.ShapeDtypeStruct((steps * WIDE, 128), BF16)]
        + [jax.ShapeDtypeStruct((heads, 128), F32)] * 2,
        out_specs=[ANY] * (len(shapes) + 1) + [VMEM] * 2,
        scratch_shapes=[pltpu.VMEM((cycle, 128), F32)] * 2 + [pltpu.VMEM((WIDE, 2 * WIDE), F32)],
        cost_estimate=hub_cost(steps * BLOCK),
        name="upper_frames",
    )


def lower(slot, heads, data, packed, at, skip, gains, outs, after):
    chunk = slot - LAG
    cycle = gains[0].shape[0]
    shapes = grad_shapes(slot)
    return call(
        functools.partial(lower_kernel, chunk, skip, at, heads),
        (*data, packed, *gains, *outs),
        [ANY] * (7 + len(outs)),
        after,
        out_shape=shapes + [jax.ShapeDtypeStruct((heads, 128), F32)] * 2,
        out_specs=[ANY] * len(shapes) + [VMEM] * 2,
        scratch_shapes=[pltpu.VMEM((cycle, 128), F32)] * 2 + [pltpu.VMEM((WIDE, WIDE), F32)],
        input_output_aliases={7 + i: i for i in range(len(outs))},
        cost_estimate=hub_cost(rows_of(chunk)),
        name="lower_frames",
    )


def blank(slot, after):
    def kernel(*refs):
        pass

    shapes = grad_shapes(slot)
    return call(
        kernel, (), [], after, out_shape=shapes, out_specs=[ANY] * len(shapes), name="blank_rows"
    )


def send(array, pairs):
    return lax.ppermute(array, "seq", pairs)


def add_pieces(pieces, after):
    def kernel(src, out):
        total = src[:, 0]
        for i in range(1, src.shape[1]):
            total = total + src[:, i]
        out[...] = total

    shape = (pieces.shape[0], *pieces.shape[2:])
    return call(
        kernel, (pieces,), [VMEM], after, out_shape=jax.ShapeDtypeStruct(shape, F32), out_specs=VMEM, name="add_pieces"
    )


def sum_gains(part, after):
    count = lax.axis_size("dp")
    mine = part.shape[1] // count
    pieces = part.reshape(2, count, mine, part.shape[2])
    total = add_pieces(lax.all_to_all(pieces, "dp", split_axis=1, concat_axis=1, tiled=True), after)
    total = total + send(total, SWAP)
    total = total + send(total, MIDDLE)
    edge = send(total, BACK_S)
    chip, _ = place()
    return jnp.where((chip == 1) | (chip == 2), total, edge)


def hub_body(queries, key_proj, value_proj, out_grad, query_gain, key_gain):
    shape = queries.shape
    heads, width = shape[-2:]
    half = shape[2] // 2 * heads
    arrays = [x.reshape(2, half, width) for x in (queries, key_proj, value_proj, out_grad)]
    cycle = math.lcm(BLOCK, heads)
    chunks = len(CUTS)

    edges, grads, crossed, middle, packs, traded = {}, {}, {}, {}, {}, []
    slots = chunks + LAG
    sums, kept, chain, marks = [], {-1: None}, [], []

    def then(token):
        chain[:] = [token]

    def trade(low, high):
        rows = halves(low, high - low, arrays, chain)
        then(rows)
        traded.append((send(rows, SWAP), low))

    def bring(chunk):
        swapped, offset = traded[min(chunk, 1)]
        rows = pack(chunk, offset, arrays, swapped, chain)
        then(rows)
        edges[chunk] = (rows, send(rows, EDGE))

    def cross(chunk):
        sources = [edges[chunk][1]] if chunk >= 0 else []
        if chunk + 1 < chunks:
            sources.append(edges[chunk + 1][0])
        if chunk >= LAG:
            sources.append(packs[chunk - LAG])
            crossed[chunk - LAG] = (chunk, sum(4 * x.shape[1] for x in sources[:-1]))
        if chunk == 0:
            chain.extend([middle[-1], *gains])
        rows = forward(sources, chain)
        then(rows)
        middle[chunk] = send(rows, MIDDLE)

    def data_of(chunk):
        return (*edges[chunk], middle[chunk - 1], middle[chunk])

    def skip_of(chunk):
        return 4 * rows_of(chunk - 1) if chunk else 0

    def work(slot):
        if slot < chunks:
            *parts, packs[slot], sum_q, sum_k = upper(
                slot, skip_of(slot), heads, data_of(slot), gains, chain
            )
            if slot >= chunks - LAG:
                packs[slot] = send(packs[slot], DOWN)
            sums.append((sum_q, sum_k))
        else:
            parts = blank(slot, chain)
        if slot >= LAG:
            chunk = slot - LAG
            packed, at = packs[chunk], 0
            if chunk in crossed:
                packed, at = middle[crossed[chunk][0]], crossed[chunk][1]
            after = [sum_q] if slot < chunks else []
            *parts, sum_q, sum_k = lower(
                slot, heads, data_of(chunk), packed, at, skip_of(chunk), gains, parts, after
            )
            sums.append((sum_q, sum_k))
        then(sum_q)
        own, other, *edge = parts
        if slot < slots - DIRECT:
            grads[slot] = (own, other, send(edge[0], BACK_S))
        else:
            grads[slot] = (own, send(other, SWAP), send(edge[0], BACK_S), send(edge[1], BACK_X))

    def settle_slot(slot):
        rows = out_rows(slot)
        if slot < slots - DIRECT:
            kernel = functools.partial(place_kernel, slot)
            *kept[slot], token = settle_rows(kernel, half, grads[slot], kept[slot - 1], 4, rows, chain)
            if slot == slots - DIRECT - 1:
                grads["late"] = send(kept[slot][3], SWAP)
        else:
            outs = kept[slot - 1]
            if slot == slots - DIRECT:
                kernel = functools.partial(place_late_kernel, slot - 1)
                *outs, token = settle_rows(kernel, half, (grads["late"],), outs[:3], 3, half // 2, chain)
                then(token)
            if slot == slots - 1:
                marks.extend(chain)
            kernel = functools.partial(place_last_kernel, slot)
            *kept[slot], token = settle_rows(kernel, half, grads[slot], outs, 3, rows, chain)
        then(token)

    trade(0, rows_of(0))
    bring(0)
    cross(-1)
    trade(rows_of(0), half)
    bring(1)
    both = lax.all_gather(jnp.stack([query_gain, key_gain]), "dp", axis=1, tiled=True)
    gains = [jnp.tile(both[t], (cycle // heads, 1)) for t in range(2)]
    cross(0)
    bring(2)
    for slot in range(slots):
        if slot + 1 < chunks:
            cross(slot + 1)
        if slot + 3 < chunks:
            bring(slot + 3)
        work(slot)
        if slot >= 1:
            settle_slot(slot - 1)
    for slot in range(slots - 1, slots):
        settle_slot(slot)

    totals = jnp.stack([functools.reduce(jnp.add, [s[t] for s in sums]) for t in range(2)])
    totals = sum_gains(totals, marks)
    return (*[x.reshape(shape) for x in kept[slots - 1]], totals[0], totals[1])


def wide_attention(query_norm, key_norm, value_in, grad_in):
    frames = query_norm.shape[1]
    scaling = 1.0 / math.sqrt(query_norm.shape[-1])
    scores = (
        jnp.einsum("efphd,egphd->ephfg", query_norm, key_norm, preferred_element_type=F32) * scaling
    )
    allowed = iota((frames, frames), 1) <= iota((frames, frames), 0)
    scores = jnp.where(allowed, scores, -jnp.inf)
    expo = jnp.exp(scores - jnp.max(scores, axis=-1, keepdims=True))
    probability = expo / jnp.sum(expo, axis=-1, keepdims=True)
    prob_low = probability.astype(BF16)
    attn_out = jnp.einsum("ephfg,egphd->efphd", prob_low, value_in, preferred_element_type=F32)
    row_dots = jnp.transpose(jnp.sum(grad_in.astype(F32) * attn_out, axis=-1), (0, 2, 3, 1))
    prob_grad = jnp.einsum("efphd,egphd->ephfg", grad_in, value_in, preferred_element_type=F32)
    score_low = (probability * (prob_grad - row_dots[..., None])).astype(BF16)
    query_step = jnp.einsum("ephfg,egphd->efphd", score_low, key_norm, preferred_element_type=F32)
    key_step = jnp.einsum("ephfg,efphd->egphd", score_low, query_norm, preferred_element_type=F32)
    value_step = jnp.einsum("ephfg,efphd->egphd", prob_low, grad_in, preferred_element_type=F32)
    return (
        (query_step * scaling).astype(BF16),
        (key_step * scaling).astype(BF16),
        value_step.astype(BF16),
    )


def wide_body(queries, key_proj, value_proj, out_grad, query_gain, key_gain):
    gain_q = lax.all_gather(query_gain, "dp", axis=0, tiled=True)
    gain_k = lax.all_gather(key_gain, "dp", axis=0, tiled=True)
    q_hat, q_inv = rms(queries)
    k_hat, k_inv = rms(key_proj)
    pieces = [
        lax.all_to_all(x, "seq", split_axis=2, concat_axis=1, tiled=True)
        for x in ((q_hat * gain_q).astype(BF16), (k_hat * gain_k).astype(BF16), value_proj, out_grad)
    ]
    steps = [
        lax.all_to_all(x, "seq", split_axis=1, concat_axis=2, tiled=True)
        for x in wide_attention(*pieces)
    ]
    query_grad, part_q = norm_back(steps[0], q_hat, q_inv, gain_q)
    key_grad, part_k = norm_back(steps[1], k_hat, k_inv, gain_k)
    axes = tuple(range(part_q.ndim - 2))
    totals = lax.psum((jnp.sum(part_q, axis=axes), jnp.sum(part_k, axis=axes)), "seq")
    totals = [lax.psum_scatter(t, "dp", scatter_dimension=0, tiled=True) for t in totals]
    return (query_grad, key_grad, steps[2], *totals)


def body(*args):
    frames = lax.axis_size("seq")
    patches, heads, width = args[0].shape[2:]
    rows = patches // 2 * heads
    if frames == 8 and args[0].shape[:2] == (1, 1) and width == 128 and rows == sum(CUTS) * BLOCK:
        return hub_body(*args)
    return wide_body(*args)


def solution(mesh):
    whole = P("dp", "seq", None, None, None)
    gain = P("dp", None)
    return jax.shard_map(
        body,
        mesh=mesh,
        in_specs=(whole,) * 4 + (gain,) * 2,
        out_specs=(whole,) * 3 + (gain,) * 2,
        check_vma=False,
    )
```
